128 devices in a mesh: expert: 32 (over y, x, core), mp: 4 (over z).
Axes of the slice: x: 4, y: 4, z: 4, core: 2. Of those that a mesh axis runs over, the one named last changes fastest.
Arguments:
- tokens: bfloat16 [16384, 768], P(('expert', 'mp')), may hold values from -6 to 6
- gain_attn: float32 [768], replicated, may hold values from 0.5 to 1.5
- gain_moe: float32 [768], replicated, may hold values from 0.5 to 1.5
- qkv_weight: bfloat16 [768, 3, 768], P('expert', None, 'mp'), may hold values from -0.21875 to 0.21875
- proj_weight: bfloat16 [768, 768], P('mp', 'expert'), may hold values from -0.875 to 0.875
- bias_table: float32 [32, 12], P(None, 'mp'), may hold values from -4 to 4
- expert_in: bfloat16 [64, 768, 3072], P('expert', None, 'mp'), may hold values from -0.21875 to 0.21875
- expert_out: bfloat16 [64, 3072, 768], P('expert', 'mp'), may hold values from -0.4375 to 0.4375
- expert_ids: int32 [16384, 2], P(('expert', 'mp')), may hold values from 0 to 63, all different within a row; in each aligned block of 128 rows (0 to 127, 128 to 255, ...) at most 5 rows name the same one
- gate_values: float32 [16384, 2], P(('expert', 'mp')), may hold values from 0.5 to 1
- bucket_table: int32 [512], replicated, may hold values from 0 to 31
- cotangent: bfloat16 [16384, 768], P(('expert', 'mp')), may hold values from -6 to 6
Outputs:
- out: bfloat16 [16384, 768], P(('expert', 'mp'))
- input_grad: float32 [16384, 768], P(('expert', 'mp'))
- gain_attn_grad: float32 [768], P(('expert', 'mp'))
- gain_moe_grad: float32 [768], P(('expert', 'mp'))
- qkv_grad: float32 [768, 3, 768], P('expert', None, 'mp')
- proj_grad: float32 [768, 768], P('mp', 'expert')
- table_grad: float32 [32, 12], P('expert', 'mp')
- expert_in_grad: float32 [64, 768, 3072], P('expert', None, 'mp')
- expert_out_grad: float32 [64, 3072, 768], P('expert', 'mp')
The draws below stay inside these ranges and needn't reach their ends.
Inputs may be any that keep to these rules, and one draw needn't show every extreme that they name: `expert_ids`: each row names 2 different experts. Among the 128 rows of one device no expert is named more than 5 times, a bound that some block reaches.
All inputs are finite; a program needn't handle non-finite values.
Results may differ from the reference program's by a relative error of at most 0.035.
Values may be sent and summed in bfloat16 or wider, within the bound.
A program may use at most 128 MiB of HBM per device.

```python
import math
import jax
import jax.numpy as jnp
import numpy as np
from jax import lax

D = 768
HEADS = 12
HEAD_DIM = 64
FF = 3072
NB = 32
TOPK = 2
TOK_DEV = 128
SEQ = 512
TOKENS = 16384
EXPERTS = 64
CAP = 5
N_EXPERT = 32
N_MP = 4


def place_ends(array, key, least, high):
    shape = array.shape
    index_at = [jax.random.randint(jax.random.fold_in(key, axis), (), 0, shape[axis]) for axis in range(len(shape))]
    array = array.at[tuple(index_at)].set(least)
    longest = shape.index(max(shape))
    index_at[longest] = (index_at[longest] + 1) % shape[longest]
    return array.at[tuple(index_at)].set(high)


def level_of(own_key, dims, shards, low, high):
    factor_of, own = 1.0, jax.random.fold_in(own_key, 6)
    for position, shards_of in shards:
        steps = jnp.exp(jax.random.uniform(jax.random.fold_in(own, position), (shards_of,), jnp.float32, low / len(shards), high / len(shards)))
        factor_of = factor_of * jnp.repeat(steps, dims[position] // shards_of).reshape([-1 if axis == position else 1 for axis in range(len(dims))])
    return factor_of


def deal_out(rng, own, number, rows, count, top, reach, lean):
    order = jax.random.permutation(rng, count)
    packed, usual = shares(count, rows * top, reach, lean, True), shares(count, rows * top, reach, lean, False)
    places = jnp.arange(count)

    def named(sizes, rotation):
        used = int((sizes > 0).sum())
        fixed = max(1, used // 4)
        moved = fixed + (places - fixed + rotation * (used - fixed)) % max(1, count - fixed)
        return jnp.zeros((count,), jnp.int32).at[order[jnp.where(places < fixed, places, moved)]].set(jnp.asarray(sizes, jnp.int32))

    sizes = jnp.where(number % 4 == 0, named(packed, number // 4), named(usual, number - number // 4 - 1))
    mixed = jax.random.permutation(jax.random.fold_in(own, 3), count)
    giver, sink = mixed[0:count // 2 * 2:2], mixed[1:count // 2 * 2:2]
    room = jnp.minimum(sizes[giver] - 1, reach - sizes[sink]) // 2
    room = jnp.where((giver == order[0]) | (sink == order[0]) | (sizes[sink] == 0), 0, jnp.maximum(room, 0))
    moved = jax.random.randint(jax.random.fold_in(own, 4), (count // 2,), 0, 1 << 20) % (room + 1)
    sizes = sizes.at[giver].add(-moved).at[sink].add(moved)
    members = jnp.searchsorted(jnp.cumsum(sizes), jnp.arange(rows * top), side="right").astype(jnp.int32)
    grid = members.reshape(top, rows).T
    grid = grid[jax.random.permutation(jax.random.fold_in(own, 1), rows)]
    rotation = jax.random.randint(jax.random.fold_in(own, 2), (rows, 1), 0, top)
    return jnp.take_along_axis(grid, (jnp.arange(top)[None, :] + rotation) % top, axis=1)


def shares(amount, total, bound, lean, full):
    portions = [(1 << 20) // math.isqrt(grade ** lean) + 1 for grade in range(1, amount + 1)]
    largest = bound if full else min(bound, max(-(-total // amount), total * portions[0] // sum(portions)))
    least = 1 if total - largest >= amount - 1 else 0
    holding, surplus = [largest] + [least] * (amount - 1), total - largest - least * (amount - 1)
    while surplus > 0:
        candidates = [i for i in range(1, amount) if holding[i] < largest] or [i for i in range(1, amount) if holding[i] < bound]
        pool, remaining = sum([portions[i] for i in candidates]), surplus
        for i in candidates:
            extra = min(bound - holding[i], max(1, remaining * portions[i] // pool), surplus)
            holding[i] = holding[i] + extra
            surplus = surplus - extra
    return np.array(holding)


def normal_values(stream_key, dims, scale, most, shards=(), kind=jnp.bfloat16):
    level = level_of(stream_key, dims, shards, -0.22, 0.18) if shards else 1.0
    entries = jax.random.normal(stream_key, dims, jnp.float32) * scale * level
    return jnp.minimum(jnp.maximum(entries, -most), most).astype(kind)


def setup_inputs(seed: int = 0) -> dict:
    keys = jax.random.split(jax.random.key(seed), 13)
    tokens = normal_values(keys[0], (TOKENS, D), 1.0, 6.0, ((0, 128),))
    gain_attn = jnp.clip(1.0 + 0.1 * jax.random.normal(keys[1], (D,), jnp.float32), 0.5, 1.5)
    gain_moe = jnp.clip(1.0 + 0.1 * jax.random.normal(keys[2], (D,), jnp.float32), 0.5, 1.5)
    qkv_weight = normal_values(keys[3], (D, 3, HEADS * HEAD_DIM), D ** -0.5, 0.21875, ((0, 32), (2, 4)))
    proj_weight = normal_values(keys[4], (HEADS * HEAD_DIM, D), (HEADS * HEAD_DIM // 16) ** -0.5, 0.875, ((0, 4), (1, 32)))
    bias_table = normal_values(keys[5], (NB, HEADS), 1.0, 4.0, ((1, 4),), jnp.float32)
    expert_in = normal_values(keys[6], (EXPERTS, D, FF), D ** -0.5, 0.21875, ((0, 32), (2, 4)))
    expert_out = normal_values(keys[7], (EXPERTS, FF, D), (FF // 16) ** -0.5, 0.4375, ((0, 32), (1, 4)))
    expert_ids_keys = jax.random.split(jax.random.fold_in(keys[8], 1), TOKENS // TOK_DEV)
    expert_ids_turns = jax.random.permutation(jax.random.fold_in(keys[8], 3), TOKENS // TOK_DEV)
    expert_ids = jax.vmap(lambda own, number: deal_out(jax.random.fold_in(keys[8], 2), own, number, TOK_DEV, EXPERTS, TOPK, CAP, 2))(expert_ids_keys, expert_ids_turns).reshape((TOKENS, TOPK))
    gate_values = jnp.clip(jnp.exp(math.log(1.0) - 0.6931472 * jax.random.uniform(keys[9], (TOKENS, TOPK), jnp.float32) ** level_of(keys[9], (TOKENS, TOPK), ((0, 128),), -0.2, 0.2)), 0.5, 1.0)
    bucket_table = place_ends(jax.random.randint(keys[10], (SEQ,), 0, NB), jax.random.fold_in(keys[10], 1), 0, NB - 1).astype(jnp.int32)
    cotangent = normal_values(keys[11], (TOKENS, D), 1.0, 6.0, ((0, 128),))
    return dict(tokens=tokens, gain_attn=gain_attn, gain_moe=gain_moe, qkv_weight=qkv_weight, proj_weight=proj_weight, bias_table=bias_table, expert_in=expert_in, expert_out=expert_out, expert_ids=expert_ids, gate_values=gate_values, bucket_table=bucket_table, cotangent=cotangent)


@jax.custom_vjp
def low(v):
    return lax.optimization_barrier(v.astype(jnp.bfloat16)).astype(jnp.float32)

@jax.custom_vjp
def low_back(v):
    return v

def low_keep(v):
    return (low(v), None)

def low_pass(kept, grad):
    return (grad,)

def back_keep(v):
    return (v, None)

def back_low(kept, grad):
    return (low(grad),)
low.defvjp(low_keep, low_pass)
low_back.defvjp(back_keep, back_low)
highest = lax.Precision.HIGHEST
epsilon = 1e-06
masked_value = -1e+30

def rms_scale(values):
    return lax.rsqrt(lax.optimization_barrier(jnp.mean(values * values, axis=-1, keepdims=True)) + epsilon)

def route_tables(expert_ids, gate_values):
    assign = expert_ids.reshape(-1).astype(jnp.int32)
    flat_count = assign.shape[0]
    per_block = TOK_DEV * TOPK
    expert_range = jnp.arange(EXPERTS, dtype=jnp.int32)
    onehot = (assign.reshape(-1, per_block)[:, :, None] == expert_range[None, None, :]).astype(jnp.int32)
    before = jnp.cumsum(onehot, axis=1) - onehot
    slot_index = lax.optimization_barrier(jnp.sum(before * onehot, axis=2)).astype(jnp.int32).reshape(-1)
    token_index = jnp.arange(flat_count, dtype=jnp.int32) // TOPK
    row_index = (token_index // TOK_DEV * CAP + slot_index).astype(jnp.int32)
    total_rows = N_EXPERT * N_MP * CAP
    token_table = jnp.zeros((EXPERTS, total_rows), jnp.int32).at[assign, row_index].set(token_index)
    gate_table = jnp.zeros((EXPERTS, total_rows), jnp.float32).at[assign, row_index].set(gate_values.reshape(-1))
    return (token_table, gate_table)

def attend_sequence(qkv_seq, rel_bias):
    queries = qkv_seq[:, 0]
    key_rows = qkv_seq[:, 1]
    values = qkv_seq[:, 2]
    scores = jnp.einsum('qhd,khd->hqk', queries, key_rows, precision=highest) * HEAD_DIM ** (-0.5)
    positions = jnp.arange(SEQ, dtype=jnp.int32)
    offset = jnp.maximum(positions[:, None] - positions[None, :], 0)
    scores = scores + jnp.take(rel_bias.T, offset, axis=1)
    scores = low_back(scores)
    causal = positions[None, :] <= positions[:, None]
    scores = jnp.where(causal[None], scores, masked_value)
    weights_p = low(jax.nn.softmax(scores, axis=-1))
    return jnp.einsum('hqk,khd->qhd', weights_p, values, precision=highest)

def forward(inputs, gain_attn, gain_moe, qkv_weight, proj_weight, bias_table, expert_in, expert_out, token_table, gate_table, bucket_hot):
    unit_a = low(inputs * rms_scale(inputs))
    normed_a = low(unit_a * gain_attn)
    qkv = low_back(low(jnp.dot(normed_a, qkv_weight.reshape(D, 3 * HEADS * HEAD_DIM), precision=highest)))
    qkv = qkv.reshape(N_EXPERT, SEQ, 3, HEADS, HEAD_DIM)
    rel_bias = jnp.dot(bucket_hot, bias_table, precision=highest)

    def per_sequence(qkv_seq):
        return attend_sequence(qkv_seq, rel_bias)
    attended = lax.map(jax.checkpoint(per_sequence), qkv)
    attended = low_back(low(attended.reshape(TOKENS, HEADS * HEAD_DIM)))
    attn_out = low_back(jnp.dot(attended, proj_weight, precision=highest))
    resid = inputs + attn_out
    normed_m = low(resid * rms_scale(resid) * gain_moe)

    def run_expert(pieces):
        rows_index, weight_in, weight_out = pieces
        expert_rows = low_back(normed_m[rows_index])
        pre_act = low_back(jnp.dot(expert_rows, weight_in, precision=highest))
        hidden = low(jax.nn.gelu(pre_act, approximate=False))
        return low_back(low(jnp.dot(hidden, weight_out, precision=highest)))
    expert_y = lax.map(jax.checkpoint(run_expert), (token_table, expert_in, expert_out))
    mixture = jnp.zeros_like(resid).at[token_table.reshape(-1)].add(gate_table.reshape(-1)[:, None] * expert_y.reshape(-1, D))
    return resid + mixture

def reference(tokens, gain_attn, gain_moe, qkv_weight, proj_weight, bias_table, expert_in, expert_out, expert_ids, gate_values, bucket_table, cotangent):
    token_table, gate_table = route_tables(expert_ids, gate_values)
    bucket_hot = (bucket_table[:, None] == jnp.arange(NB, dtype=jnp.int32)[None, :]).astype(jnp.float32)

    def whole_layer(inputs, gain_a, gain_m, weight_qkv, weight_proj, table, weight_in, weight_out):
        return forward(inputs, gain_a, gain_m, weight_qkv, weight_proj, table, weight_in, weight_out, token_table, gate_table, bucket_hot)
    output, pullback = jax.vjp(whole_layer, tokens.astype(jnp.float32), gain_attn, gain_moe, qkv_weight.astype(jnp.float32), proj_weight.astype(jnp.float32), bias_table, expert_in.astype(jnp.float32), expert_out.astype(jnp.float32))
    gradients = pullback(cotangent.astype(jnp.float32))
    return (output.astype(jnp.bfloat16), gradients[0], gradients[1], gradients[2], gradients[3], gradients[4], gradients[5], gradients[6], gradients[7])
```

```python
import jax
import jax.numpy as jnp
from jax import lax
from jax.experimental import pallas as pl
from jax.experimental.pallas import tpu as pltpu
from jax.sharding import PartitionSpec as P

HEAD_DIM = 64
TOPK = 2


epsilon = 1e-06
masked_value = -1e30
inv_root_two = 0.7071067811865476
inv_root_tau = 0.3989422804014327
highest = lax.Precision.HIGHEST


MESH = pl.DeviceIdType.MESH
BLOCK = 16
HALF = 80
PLANE = 32
RING = 4
PAD = PLANE * BLOCK
ROWS = 320
EXPERT_ROWS = 640
f32 = jnp.float32
bf16 = jnp.bfloat16


def place():
    e, z = lax.axis_index("expert"), lax.axis_index("mp")
    return e, z, lax.rem(z + 1, RING), lax.rem(z + RING - 1, RING)


def plane_target(e, d):
    step = d // 8
    dy, dx, dc = lax.rem(step * 2, 4) + step // 2, lax.rem(d // 2, 4), lax.rem(d, 2)
    y, x, c = e // 8, lax.rem(e // 2, 4), lax.rem(e, 2)
    return lax.rem(y + dy, 4) * 8 + lax.rem(x + dx, 4) * 2 + lax.rem(c + dc, 2)


def plane_source(e, d):
    step = d // 8
    dy, dx, dc = lax.rem(step * 2, 4) + step // 2, lax.rem(d // 2, 4), lax.rem(d, 2)
    y, x, c = e // 8, lax.rem(e // 2, 4), lax.rem(e, 2)
    return lax.rem(y + 4 - dy, 4) * 8 + lax.rem(x + 4 - dx, 4) * 2 + lax.rem(c + dc, 2)


def block_at(index):
    return pl.ds(pl.multiple_of(index * BLOCK, BLOCK), BLOCK)


def greet(plane, ring):
    e, z, right, left = place()
    barrier = pltpu.get_barrier_semaphore()
    if plane:

        def signal(d, carry):
            pl.semaphore_signal(
                barrier, inc=1, device_id=(plane_target(e, d), z), device_id_type=MESH
            )
            return carry

        lax.fori_loop(1, PLANE, signal, 0)
    if ring:
        for other in (right, left):
            pl.semaphore_signal(barrier, inc=1, device_id=(e, other), device_id_type=MESH)
    pl.semaphore_wait(barrier, (PLANE - 1) * plane + 2 * ring)


def drain(ref, sem):
    pltpu.make_async_copy(ref, ref, sem).wait()


def dot(left, right):
    return jnp.dot(left, right, preferred_element_type=f32)


def dot_rows(left, right):
    return lax.dot_general(left, right, (((0,), (0,)), ((), ())), preferred_element_type=f32)


def dot_cols(left, right):
    return lax.dot_general(left, right, (((1,), (1,)), ((), ())), preferred_element_type=f32)


def packer():
    row = lax.broadcasted_iota(jnp.int32, (2 * HALF, 256), 0)
    col = lax.broadcasted_iota(jnp.int32, (2 * HALF, 256), 1)
    expert = (row >= HALF).astype(jnp.int32)
    inner = row - expert * HALF
    source = (inner * 205) // 1024
    slot = inner - source * 5
    return (col == source * BLOCK + expert * 5 + slot).astype(bf16)


class Dispatch:
    def __init__(self, send, landed, rows, sems):
        self.send, self.landed, self.rows = send, landed, rows
        self.plane_out, self.plane_in, self.ring_out, self.ring_in = sems

    def part(self, slot, half):
        return self.rows.at[:, pl.ds(slot * 160 + half * HALF, HALF)]

    def cross(self):
        e, z, right, left = place()

        def send(d, carry):
            other = plane_target(e, d)
            pltpu.make_async_remote_copy(
                self.send.at[block_at(other)],
                self.landed.at[block_at(d)],
                self.plane_out,
                self.plane_in.at[d // 16],
                device_id=(other, z),
                device_id_type=MESH,
            ).start()
            return carry

        lax.fori_loop(1, PLANE, send, 0)
        self.landed[0:BLOCK] = self.send[block_at(e)]

    def copy(self, index, source, target, other):
        e = lax.axis_index("expert")
        return pltpu.make_async_remote_copy(
            source,
            target,
            self.ring_out.at[index],
            self.ring_in.at[index],
            device_id=(e, other),
            device_id_type=MESH,
        )

    def copies(self):
        e, z, right, left = place()
        part = self.part
        return [
            self.copy(0, part(0, 0), part(2, 0), right),
            self.copy(1, part(0, 1), part(2, 1), right),
            self.copy(2, part(0, 0), part(1, 0), left),
            self.copy(3, part(0, 1), part(1, 1), left),
            self.copy(4, part(2, 0), part(3, 0), right),
            self.copy(5, part(1, 1), part(3, 1), left),
        ]

    def turn(self, half, pack):
        lo = 256 * half
        span = self.landed.at[pl.ds(lo + (BLOCK if half == 0 else 0), 256 - (BLOCK if half == 0 else 0))]
        drain(span, self.plane_in.at[half])
        packed = dot(pack, self.landed[lo : lo + 256]).astype(bf16)
        for j in range(2):
            self.rows[j, half * HALF : half * HALF + HALF] = packed[j * HALF : j * HALF + HALF]
        ring = self.copies()
        ring[half].start()
        ring[2 + half].start()

    def relay(self):
        ring = self.copies()
        ring[0].wait_recv()
        ring[4].start()
        ring[3].wait_recv()
        ring[5].start()
        ring[1].wait_recv()
        ring[2].wait_recv()

    def last(self):
        ring = self.copies()
        ring[4].wait_recv()
        ring[5].wait_recv()

    def close(self):
        for copy in self.copies():
            copy.wait_send()
        drain(self.send.at[pl.ds(0, (PLANE - 1) * BLOCK)], self.plane_out)


DISPATCH_SCRATCH = [
    pltpu.SemaphoreType.DMA,
    pltpu.SemaphoreType.DMA((2,)),
    pltpu.SemaphoreType.DMA((6,)),
    pltpu.SemaphoreType.DMA((6,)),
]


class Return:
    def __init__(self, partial, relayed, landed, spread, home, sems):
        self.partial, self.relayed, self.landed = partial, relayed, landed
        self.spread, self.home = spread, home
        self.ring_out, self.ring_in, self.plane_out, self.plane_in = sems

    def part(self, slot, half):
        return self.partial.at[:, pl.ds(slot * 160 + half * HALF, HALF)]

    def copies(self):
        e, z, right, left = place()

        def copy(index, source, other):
            return pltpu.make_async_remote_copy(
                source,
                self.landed.at[index],
                self.ring_out.at[index],
                self.ring_in.at[index],
                device_id=(e, other),
                device_id_type=MESH,
            )

        part = self.part
        return [
            copy(0, part(3, 0), right),
            copy(1, part(3, 1), left),
            copy(2, part(1, 1), right),
            copy(3, part(2, 0), left),
            copy(4, self.relayed.at[0], right),
            copy(5, self.relayed.at[1], left),
        ]

    def near(self):
        ring = self.copies()
        ring[2].start()
        ring[3].start()

    def far(self):
        ring = self.copies()
        ring[0].start()
        ring[1].start()

    def add_far(self):
        ring = self.copies()
        for index, slot, half in ((0, 1, 0), (1, 2, 1)):
            ring[index].wait_recv()
            self.relayed[index] = (
                self.part(slot, half)[...].astype(f32) + self.landed[index].astype(f32)
            ).astype(bf16)
            ring[4 + index].start()

    def finish(self, half, pack):
        e, z, right, left = place()
        ring = self.copies()
        direct, summed = (3, 4) if half == 0 else (2, 5)
        ring[direct].wait_recv()
        ring[summed].wait_recv()
        total = (
            self.part(0, half)[...].astype(f32)
            + self.landed[direct].astype(f32)
            + self.landed[summed].astype(f32)
        ).astype(bf16)
        flat = jnp.concatenate([total[0], total[1]], axis=0)
        self.spread[256 * half : 256 * half + 256] = dot_rows(pack, flat).astype(bf16)

        def send(d, carry):
            pltpu.make_async_remote_copy(
                self.spread.at[block_at(d)],
                self.home.at[block_at(e)],
                self.plane_out,
                self.plane_in,
                device_id=(plane_source(e, d), z),
                device_id_type=MESH,
            ).start()
            return carry

        lax.fori_loop(max(1, 16 * half), 16 * half + 16, send, 0)
        if half == 0:
            self.home[block_at(e)] = self.spread[0:BLOCK]

    def arrive(self):
        drain(self.home.at[pl.ds(0, (PLANE - 1) * BLOCK)], self.plane_in)

    def close(self):
        for copy in self.copies():
            copy.wait_send()
        drain(self.spread.at[pl.ds(0, (PLANE - 1) * BLOCK)], self.plane_out)


RETURN_SCRATCH = [
    pltpu.VMEM((2, 2, HALF, 768), bf16),
    pltpu.VMEM((6, 2, HALF, 768), bf16),
    pltpu.VMEM((PAD, 768), bf16),
    pltpu.VMEM((PAD, 768), bf16),
    pltpu.SemaphoreType.DMA((6,)),
    pltpu.SemaphoreType.DMA((6,)),
    pltpu.SemaphoreType.DMA,
    pltpu.SemaphoreType.DMA,
]


def kernel_params(collective_id):
    return pltpu.CompilerParams(
        collective_id=collective_id, has_side_effects=True, vmem_limit_bytes=60 * 1024 * 1024
    )


VMEM = pl.BlockSpec(memory_space=pltpu.VMEM)


def spread_kernel(send, rows, landed, *sems):
    greet(1, 1)
    work = Dispatch(send, landed, rows, sems)
    work.cross()
    pack = packer()
    work.turn(0, pack)
    work.turn(1, pack)
    work.relay()
    work.last()
    work.close()


def spread_rows(send):
    return pl.pallas_call(
        spread_kernel,
        out_shape=jax.ShapeDtypeStruct((2, EXPERT_ROWS, 768), bf16),
        in_specs=[VMEM],
        out_specs=VMEM,
        scratch_shapes=[pltpu.VMEM((PAD, 768), bf16)] + DISPATCH_SCRATCH,
        compiler_params=kernel_params(1),
        name="spread_cotangent",
    )(send)


def gather_kernel(partial, out, relayed, landed, spread, home, *sems):
    greet(1, 1)
    work = Return(partial, relayed, landed, spread, home, sems)
    work.near()
    work.far()
    pack = packer()
    work.add_far()
    work.finish(0, pack)
    work.finish(1, pack)
    work.arrive()
    out[...] = home[...]
    work.close()


def gather_rows(partial):
    return pl.pallas_call(
        gather_kernel,
        out_shape=jax.ShapeDtypeStruct((PAD, 768), bf16),
        in_specs=[VMEM],
        out_specs=VMEM,
        scratch_shapes=RETURN_SCRATCH,
        compiler_params=kernel_params(2),
        name="gather_mixture",
    )(partial)


def expert_kernel(
    send, grad_rows, weight_in, weight_out,
    x_out, hidden, grad_pre, y_part, grad_home,
    landed, held_in, held_out, grad_part, load_sems,
    d0, d1, d2, d3, *back,
):
    loads = [
        pltpu.make_async_copy(weight_in, held_in, load_sems.at[0]),
        pltpu.make_async_copy(weight_out, held_out, load_sems.at[1]),
    ]
    for load in loads:
        load.start()
    greet(1, 1)
    out_way = Dispatch(send, landed, x_out, (d0, d1, d2, d3))
    home_way = Return(grad_part, back[0], back[1], back[2], back[3], back[4:])
    out_way.cross()
    pack = packer()
    out_way.turn(0, pack)
    out_way.turn(1, pack)
    for load in loads:
        load.wait()

    def run(first, count):
        for j in range(2):
            span = pl.ds(first * 160, count * 160)
            pre_act = dot(x_out[j, span], held_in[j])
            cdf = 0.5 * (1.0 + lax.erf(pre_act * inv_root_two))
            hidden[j, span] = (pre_act * cdf).astype(bf16)
            slope = cdf + pre_act * jnp.exp(-0.5 * pre_act * pre_act) * inv_root_tau
            grad_hidden = dot_cols(grad_rows[j, span], held_out[j])
            grad_pre[j, span] = (grad_hidden * slope).astype(bf16)
            grad_part[j, span] = dot_cols(grad_pre[j, span], held_in[j]).astype(bf16)

    run(0, 1)
    out_way.relay()
    run(1, 2)
    home_way.near()
    out_way.last()
    run(3, 1)
    home_way.far()
    for j in range(2):
        y_part[j, 0:320] = dot(hidden[j, 0:320], held_out[j]).astype(bf16)
    home_way.add_far()
    for j in range(2):
        y_part[j, 320:640] = dot(hidden[j, 320:640], held_out[j]).astype(bf16)
    home_way.finish(0, pack)
    home_way.finish(1, pack)
    home_way.arrive()
    grad_home[...] = home_way.home[...]
    out_way.close()
    home_way.close()


def run_experts(send, grad_rows, weight_in, weight_out):
    rows = jax.ShapeDtypeStruct((2, EXPERT_ROWS, 768), bf16)
    anywhere = pl.BlockSpec(memory_space=pl.ANY)
    return pl.pallas_call(
        expert_kernel,
        out_shape=[rows, rows, rows, rows, jax.ShapeDtypeStruct((PAD, 768), bf16)],
        in_specs=[VMEM, VMEM, anywhere, anywhere],
        out_specs=[VMEM] * 5,
        scratch_shapes=[
            pltpu.VMEM((PAD, 768), bf16),
            pltpu.VMEM((2, 768, 768), bf16),
            pltpu.VMEM((2, 768, 768), bf16),
            pltpu.VMEM((2, EXPERT_ROWS, 768), bf16),
            pltpu.SemaphoreType.DMA((2,)),
        ]
        + DISPATCH_SCRATCH
        + RETURN_SCRATCH,
        compiler_params=kernel_params(3),
        name="experts",
    )(send, grad_rows, weight_in, weight_out)


def contract_rows(left, right):
    return lax.dot_general(
        left, right, (((0,), (0,)), ((), ())), preferred_element_type=jnp.float32
    )


def contract_cols(left, right):
    return lax.dot_general(
        left, right, (((1,), (1,)), ((), ())), preferred_element_type=jnp.float32
    )


def fold_window(window, seq_len):
    return jnp.concatenate([window[:, :seq_len][:, ::-1], window[:, seq_len:][:, ::-1]], axis=1)


def body(
    tokens,
    gain_attn,
    gain_moe,
    qkv_weight,
    proj_weight,
    bias_table,
    expert_in,
    expert_out,
    expert_ids,
    gate_values,
    bucket_table,
    cotangent,
):
    expert_count = lax.axis_size("expert")
    mp_count = lax.axis_size("mp")
    tok_rows, model_width = tokens.shape
    local_experts = expert_in.shape[0]
    all_experts = local_experts * expert_count
    capacity = max(2, 5 * tok_rows * TOPK // (4 * all_experts))
    score_scale = HEAD_DIM ** (-0.5)
    inputs = tokens.astype(jnp.float32)
    scale_first = lax.rsqrt(jnp.mean(inputs * inputs, axis=1, keepdims=True) + epsilon)
    normal_first = inputs * scale_first
    unit_first = normal_first.astype(jnp.bfloat16)
    seq_units = lax.all_gather(unit_first, "mp", axis=0, tiled=True)
    qkv_full, proj_full = (
        lax.all_gather(qkv_weight, "expert", axis=0, tiled=True),
        lax.all_gather(proj_weight, "expert", axis=1, tiled=True),
    )
    seq_len = seq_units.shape[0]
    local_width = qkv_full.shape[2]
    local_heads = local_width // HEAD_DIM
    normed_first = (seq_units.astype(jnp.float32) * gain_attn).astype(jnp.bfloat16)
    qkv_flat = qkv_full.reshape(model_width, 3 * local_width)
    projected = jnp.dot(normed_first, qkv_flat, preferred_element_type=jnp.float32).astype(
        jnp.bfloat16
    )
    projected = projected.reshape(seq_len, 3, local_heads, HEAD_DIM)
    queries = projected[:, 0]
    key_rows = projected[:, 1]
    values = projected[:, 2]
    bucket_count = bias_table.shape[0]
    bucket_hot = (
        bucket_table[:, None] == jnp.arange(bucket_count, dtype=jnp.int32)[None, :]
    ).astype(jnp.float32)
    rel_heads = lax.dot_general(bias_table, bucket_hot, (((0,), (1,)), ((), ())), precision=highest)
    block_rows = min(512, seq_len)
    block_count = seq_len // block_rows
    period = seq_len + block_rows
    block_starts = jnp.arange(block_count, dtype=jnp.int32) * block_rows
    key_pos = jnp.arange(seq_len, dtype=jnp.int32)
    rel_padded = jnp.concatenate(
        [
            jnp.zeros((local_heads, seq_len - 1), jnp.float32),
            rel_heads,
            jnp.zeros((local_heads, block_rows), jnp.float32),
        ],
        axis=1,
    )

    def block_bias(row_start):
        window = lax.dynamic_slice_in_dim(rel_padded, row_start, period, 1)
        folded = fold_window(window, seq_len)
        tiled = jnp.tile(folded, (1, block_rows))[:, : block_rows * (period - 1)]
        return tiled.reshape(local_heads, block_rows, period - 1)[:, :, :seq_len]

    def block_logits(row_start):
        query_pos = row_start + jnp.arange(block_rows, dtype=jnp.int32)
        scores = (
            jnp.einsum("qhd,khd->hqk", queries, key_rows, preferred_element_type=jnp.float32)
            * score_scale
        )
        scores = scores + block_bias(row_start)
        causal = key_pos[None, :] <= query_pos[:, None]
        return (jnp.where(causal[None], scores, masked_value), queries)

    def forward_block(row_start):
        scores, query_block = block_logits(row_start)
        top_score = jnp.max(scores, axis=2, keepdims=True)
        raised = jnp.exp(scores - top_score)
        row_total = jnp.sum(raised, axis=2, keepdims=True)
        weights_p = (raised / row_total).astype(jnp.bfloat16)
        attended_block = jnp.einsum(
            "hqk,khd->qhd", weights_p, values, preferred_element_type=jnp.float32
        )
        return (
            attended_block.astype(jnp.bfloat16),
            top_score[:, :, 0] + jnp.log(row_total[:, :, 0]),
        )

    attended_blocks, log_totals = lax.map(forward_block, block_starts)
    attended = attended_blocks.reshape(seq_len, local_width)
    attn_out = lax.psum_scatter(
        jnp.dot(attended, proj_full, preferred_element_type=jnp.float32),
        "mp",
        scatter_dimension=0,
        tiled=True,
    )
    resid = inputs + attn_out
    scale_second = lax.rsqrt(jnp.mean(resid * resid, axis=1, keepdims=True) + epsilon)
    normal_second = resid * scale_second
    normed_second = (normal_second * gain_moe).astype(jnp.bfloat16)
    flat_ids = expert_ids.reshape(-1)
    expert_range = jnp.arange(all_experts, dtype=jnp.int32)
    id_hot = (flat_ids[:, None] == expert_range[None, :]).astype(jnp.int32)
    slot_index = jnp.sum((jnp.cumsum(id_hot, axis=0) - id_hot) * id_hot, axis=1).reshape(
        tok_rows, TOPK
    )
    dest_rows = (expert_ids // local_experts) * BLOCK + lax.rem(expert_ids, 2) * capacity + slot_index
    buffer_pos = jnp.arange(PAD, dtype=jnp.int32)
    selectors = [
        (buffer_pos[:, None] == dest_rows[None, :, route_slot]).astype(jnp.bfloat16)
        for route_slot in range(TOPK)
    ]
    grad_out = cotangent.astype(jnp.float32)
    grad_send = sum(
        (
            jnp.dot(
                selectors[route_slot],
                (gate_values[:, route_slot, None] * grad_out).astype(jnp.bfloat16),
                preferred_element_type=jnp.float32,
            )
            for route_slot in range(TOPK)
        )
    ).astype(jnp.bfloat16)
    grad_recv = spread_rows(grad_send)
    send_rows = jnp.dot(
        selectors[0] + selectors[1], normed_second, preferred_element_type=jnp.float32
    ).astype(jnp.bfloat16)
    received, hidden, grad_pre, y_part, grad_rows = run_experts(
        send_rows, grad_recv, expert_in, expert_out
    )
    expert_rows = gather_rows(y_part)
    mixture = sum(
        (
            gate_values[:, route_slot, None] * contract_rows(selectors[route_slot], expert_rows)
            for route_slot in range(TOPK)
        )
    )
    result = resid + mixture
    expert_out_grad = jnp.einsum("jrf,jrd->jfd", hidden, grad_recv, preferred_element_type=jnp.float32)
    expert_in_grad = jnp.einsum("jrd,jrf->jdf", received, grad_pre, preferred_element_type=jnp.float32)
    grad_normed = contract_rows(selectors[0] + selectors[1], grad_rows)
    gain_second_part = jnp.sum(grad_normed * normal_second, axis=0)
    grad_unit_second = grad_normed * gain_moe
    grad_resid = grad_out + scale_second * (
        grad_unit_second
        - normal_second * jnp.mean(grad_unit_second * normal_second, axis=1, keepdims=True)
    )
    seq_grad = lax.all_gather(grad_resid.astype(jnp.bfloat16), "mp", axis=0, tiled=True)
    proj_grad_part = contract_rows(attended, seq_grad)
    grad_attended = (
        contract_cols(seq_grad, proj_full)
        .astype(jnp.bfloat16)
        .reshape(seq_len, local_heads, HEAD_DIM)
    )

    def bias_gradient(rel_acc, grad_scores, row_start):
        padded = jnp.concatenate(
            [grad_scores, jnp.zeros((local_heads, block_rows, period - 1 - seq_len), jnp.float32)],
            axis=2,
        )
        flat = jnp.concatenate(
            [
                padded.reshape(local_heads, block_rows * (period - 1)),
                jnp.zeros((local_heads, block_rows), jnp.float32),
            ],
            axis=1,
        )
        along = jnp.sum(flat.reshape(local_heads, block_rows, period), axis=1)
        window = lax.dynamic_slice_in_dim(rel_acc, row_start, period, 1) + fold_window(
            along, seq_len
        )
        return lax.dynamic_update_slice_in_dim(rel_acc, window, row_start, 1)

    def backward_block(carried, pieces):
        key_acc, value_acc, rel_acc = carried
        row_start, log_block = pieces
        scores, query_block = block_logits(row_start)
        softmax_rows = jnp.exp(scores - log_block[:, :, None])
        value_acc = value_acc + jnp.einsum(
            "hqk,qhd->khd",
            softmax_rows.astype(jnp.bfloat16),
            grad_attended,
            preferred_element_type=jnp.float32,
        )
        grad_weights = jnp.einsum(
            "qhd,khd->hqk", grad_attended, values, preferred_element_type=jnp.float32
        )
        row_dot = jnp.sum(softmax_rows * grad_weights, axis=2, keepdims=True)
        grad_scores = (softmax_rows * (grad_weights - row_dot)).astype(jnp.bfloat16)
        rel_acc = bias_gradient(rel_acc, grad_scores.astype(jnp.float32), row_start)
        key_acc = (
            key_acc
            + jnp.einsum(
                "hqk,qhd->khd", grad_scores, query_block, preferred_element_type=jnp.float32
            )
            * score_scale
        )
        grad_query = (
            jnp.einsum("hqk,khd->qhd", grad_scores, key_rows, preferred_element_type=jnp.float32)
            * score_scale
        )
        return ((key_acc, value_acc, rel_acc), grad_query)

    start_state = (
        jnp.zeros((seq_len, local_heads, HEAD_DIM), jnp.float32),
        jnp.zeros((seq_len, local_heads, HEAD_DIM), jnp.float32),
        jnp.zeros((local_heads, seq_len - 1 + period), jnp.float32),
    )
    final_state, query_grads = lax.scan(backward_block, start_state, (block_starts, log_totals))
    key_grad, value_grad, rel_total = final_state
    rel_grad = rel_total[:, seq_len - 1 : 2 * seq_len - 1]
    grad_qkv = jnp.stack(
        [query_grads.reshape(seq_len, local_heads, HEAD_DIM), key_grad, value_grad], axis=1
    )
    grad_qkv = grad_qkv.astype(jnp.bfloat16).reshape(seq_len, 3 * local_width)
    qkv_grad_part = contract_rows(normed_first, grad_qkv).reshape(model_width, 3, local_width)
    grad_normed_first = contract_cols(grad_qkv, qkv_flat)
    table_grad_part = lax.dot_general(
        bucket_hot, rel_grad, (((0,), (1,)), ((), ())), precision=highest
    )
    gain_first_part = jnp.sum(grad_normed_first * seq_units.astype(jnp.float32), axis=0)
    grad_unit_seq = grad_normed_first * gain_attn
    gain_piece = model_width // (expert_count * mp_count)
    gain_parts = (
        jnp.stack([gain_first_part, gain_second_part])
        .reshape(2, expert_count, mp_count, gain_piece)
        .transpose(2, 0, 1, 3)
    )
    grad_unit, gain_mp = (
        lax.psum_scatter(grad_unit_seq, "mp", scatter_dimension=0, tiled=True),
        lax.psum_scatter(gain_parts, "mp", scatter_dimension=0, tiled=True),
    )
    grad_input = grad_resid + scale_first * (
        grad_unit - normal_first * jnp.mean(grad_unit * normal_first, axis=1, keepdims=True)
    )
    qkv_grad, proj_grad, table_grad, gain_grads = (
        lax.psum_scatter(qkv_grad_part, "expert", scatter_dimension=0, tiled=True),
        lax.psum_scatter(proj_grad_part, "expert", scatter_dimension=1, tiled=True),
        lax.psum_scatter(table_grad_part, "expert", scatter_dimension=0, tiled=True),
        lax.psum_scatter(gain_mp, "expert", scatter_dimension=2, tiled=True),
    )
    return (
        result.astype(jnp.bfloat16),
        grad_input,
        gain_grads[0, 0, 0],
        gain_grads[0, 1, 0],
        qkv_grad,
        proj_grad,
        table_grad,
        expert_in_grad,
        expert_out_grad,
    )


def solution(mesh):
    placed = (
        P(("expert", "mp"), None),
        P(),
        P(),
        P("expert", None, "mp"),
        P("mp", "expert"),
        P(None, "mp"),
        P("expert", None, "mp"),
        P("expert", "mp", None),
        P(("expert", "mp"), None),
        P(("expert", "mp"), None),
        P(),
        P(("expert", "mp"), None),
    )
    return jax.shard_map(
        body,
        mesh=mesh,
        in_specs=placed,
        out_specs=(
            P(("expert", "mp"), None),
            P(("expert", "mp"), None),
            P(("expert", "mp")),
            P(("expert", "mp")),
            P("expert", None, "mp"),
            P("mp", "expert"),
            P("expert", "mp"),
            P("expert", None, "mp"),
            P("expert", "mp", None),
        ),
        check_vma=False,
    )
```

```python
import jax
import jax.numpy as jnp
from jax import lax
from jax.experimental import pallas as pl
from jax.experimental.pallas import tpu as pltpu
from jax.sharding import PartitionSpec as P

HEAD_DIM = 64
TOPK = 2


epsilon = 1e-06
masked_value = -1e30
inv_root_two = 0.7071067811865476
inv_root_tau = 0.3989422804014327
highest = lax.Precision.HIGHEST


MESH = pl.DeviceIdType.MESH
BLOCK = 16
HALF = 80
PLANE = 32
RING = 4
PAD = PLANE * BLOCK
ROWS = 320
EXPERT_ROWS = 640
f32 = jnp.float32
bf16 = jnp.bfloat16


def place():
    e, z = lax.axis_index("expert"), lax.axis_index("mp")
    return e, z, lax.rem(z + 1, RING), lax.rem(z + RING - 1, RING)


def plane_target(e, d):
    step = d // 8
    dy, dx, dc = lax.rem(step * 2, 4) + step // 2, lax.rem(d // 2, 4), lax.rem(d, 2)
    y, x, c = e // 8, lax.rem(e // 2, 4), lax.rem(e, 2)
    return lax.rem(y + dy, 4) * 8 + lax.rem(x + dx, 4) * 2 + lax.rem(c + dc, 2)


def plane_source(e, d):
    step = d // 8
    dy, dx, dc = lax.rem(step * 2, 4) + step // 2, lax.rem(d // 2, 4), lax.rem(d, 2)
    y, x, c = e // 8, lax.rem(e // 2, 4), lax.rem(e, 2)
    return lax.rem(y + 4 - dy, 4) * 8 + lax.rem(x + 4 - dx, 4) * 2 + lax.rem(c + dc, 2)


def block_at(index):
    return pl.ds(pl.multiple_of(index * BLOCK, BLOCK), BLOCK)


def greet(plane, ring, across=0):
    e, z, right, left = place()
    barrier = pltpu.get_barrier_semaphore()
    if plane:

        def signal(d, carry):
            pl.semaphore_signal(
                barrier, inc=1, device_id=(plane_target(e, d), z), device_id_type=MESH
            )
            return carry

        lax.fori_loop(1, PLANE, signal, 0)
    if ring:
        for other in (right, left):
            pl.semaphore_signal(barrier, inc=1, device_id=(e, other), device_id_type=MESH)
    if across:
        other = lax.rem(z + 2, RING)
        pl.semaphore_signal(barrier, inc=1, device_id=(e, other), device_id_type=MESH)
    pl.semaphore_wait(barrier, (PLANE - 1) * plane + 2 * ring + across)


def drain(ref, sem):
    pltpu.make_async_copy(ref, ref, sem).wait()


def dot(left, right):
    return jnp.dot(left, right, preferred_element_type=f32)


def dot_rows(left, right):
    return lax.dot_general(left, right, (((0,), (0,)), ((), ())), preferred_element_type=f32)


def dot_cols(left, right):
    return lax.dot_general(left, right, (((1,), (1,)), ((), ())), preferred_element_type=f32)


def packer():
    row = lax.broadcasted_iota(jnp.int32, (2 * HALF, 256), 0)
    col = lax.broadcasted_iota(jnp.int32, (2 * HALF, 256), 1)
    expert = (row >= HALF).astype(jnp.int32)
    inner = row - expert * HALF
    source = (inner * 205) // 1024
    slot = inner - source * 5
    return (col == source * BLOCK + expert * 5 + slot).astype(bf16)


class Dispatch:
    def __init__(self, send, landed, rows, sems):
        self.send, self.landed, self.rows = send, landed, rows
        self.plane_out, self.plane_in, self.ring_out, self.ring_in = sems

    def part(self, slot, half):
        return self.rows.at[:, pl.ds(slot * 160 + half * HALF, HALF)]

    def cross(self):
        e, z, right, left = place()

        def send(d, carry):
            other = plane_target(e, d)
            pltpu.make_async_remote_copy(
                self.send.at[block_at(other)],
                self.landed.at[block_at(d)],
                self.plane_out,
                self.plane_in.at[d // 16],
                device_id=(other, z),
                device_id_type=MESH,
            ).start()
            return carry

        lax.fori_loop(1, PLANE, send, 0)
        self.landed[0:BLOCK] = self.send[block_at(e)]

    def copy(self, index, source, target, other):
        e = lax.axis_index("expert")
        return pltpu.make_async_remote_copy(
            source,
            target,
            self.ring_out.at[index],
            self.ring_in.at[index],
            device_id=(e, other),
            device_id_type=MESH,
        )

    def copies(self):
        e, z, right, left = place()
        part = self.part
        return [
            self.copy(0, part(0, 0), part(2, 0), right),
            self.copy(1, part(0, 1), part(2, 1), right),
            self.copy(2, part(0, 0), part(1, 0), left),
            self.copy(3, part(0, 1), part(1, 1), left),
            self.copy(4, part(2, 0), part(3, 0), right),
            self.copy(5, part(1, 1), part(3, 1), left),
        ]

    def turn(self, half, pack):
        lo = 256 * half
        span = self.landed.at[pl.ds(lo + (BLOCK if half == 0 else 0), 256 - (BLOCK if half == 0 else 0))]
        drain(span, self.plane_in.at[half])
        packed = dot(pack, self.landed[lo : lo + 256]).astype(bf16)
        for j in range(2):
            self.rows[j, half * HALF : half * HALF + HALF] = packed[j * HALF : j * HALF + HALF]
        ring = self.copies()
        ring[half].start()
        ring[2 + half].start()

    def relay(self):
        ring = self.copies()
        ring[0].wait_recv()
        ring[4].start()
        ring[3].wait_recv()
        ring[5].start()
        ring[1].wait_recv()
        ring[2].wait_recv()

    def last(self):
        ring = self.copies()
        ring[4].wait_recv()
        ring[5].wait_recv()

    def close(self):
        for copy in self.copies():
            copy.wait_send()
        drain(self.send.at[pl.ds(0, (PLANE - 1) * BLOCK)], self.plane_out)


DISPATCH_SCRATCH = [
    pltpu.SemaphoreType.DMA,
    pltpu.SemaphoreType.DMA((2,)),
    pltpu.SemaphoreType.DMA((6,)),
    pltpu.SemaphoreType.DMA((6,)),
]


class Return:
    def __init__(self, partial, relayed, landed, spread, home, sems):
        self.partial, self.relayed, self.landed = partial, relayed, landed
        self.spread, self.home = spread, home
        self.ring_out, self.ring_in, self.plane_out, self.plane_in = sems

    def part(self, slot, half):
        return self.partial.at[:, pl.ds(slot * 160 + half * HALF, HALF)]

    def copies(self):
        e, z, right, left = place()

        def copy(index, source, other):
            return pltpu.make_async_remote_copy(
                source,
                self.landed.at[index],
                self.ring_out.at[index],
                self.ring_in.at[index],
                device_id=(e, other),
                device_id_type=MESH,
            )

        part = self.part
        return [
            copy(0, part(3, 0), right),
            copy(1, part(3, 1), left),
            copy(2, part(1, 1), right),
            copy(3, part(2, 0), left),
            copy(4, self.relayed.at[0], right),
            copy(5, self.relayed.at[1], left),
        ]

    def near(self):
        ring = self.copies()
        ring[2].start()
        ring[3].start()

    def far(self):
        ring = self.copies()
        ring[0].start()
        ring[1].start()

    def add_far(self):
        ring = self.copies()
        for index, slot, half in ((0, 1, 0), (1, 2, 1)):
            ring[index].wait_recv()
            self.relayed[index] = (
                self.part(slot, half)[...].astype(f32) + self.landed[index].astype(f32)
            ).astype(bf16)
            ring[4 + index].start()

    def finish(self, half, pack):
        e, z, right, left = place()
        ring = self.copies()
        direct, summed = (3, 4) if half == 0 else (2, 5)
        ring[direct].wait_recv()
        ring[summed].wait_recv()
        total = (
            self.part(0, half)[...].astype(f32)
            + self.landed[direct].astype(f32)
            + self.landed[summed].astype(f32)
        ).astype(bf16)
        flat = jnp.concatenate([total[0], total[1]], axis=0)
        self.spread[256 * half : 256 * half + 256] = dot_rows(pack, flat).astype(bf16)

        def send(d, carry):
            pltpu.make_async_remote_copy(
                self.spread.at[block_at(d)],
                self.home.at[block_at(e)],
                self.plane_out,
                self.plane_in,
                device_id=(plane_source(e, d), z),
                device_id_type=MESH,
            ).start()
            return carry

        lax.fori_loop(max(1, 16 * half), 16 * half + 16, send, 0)
        if half == 0:
            self.home[block_at(e)] = self.spread[0:BLOCK]

    def arrive(self):
        drain(self.home.at[pl.ds(0, (PLANE - 1) * BLOCK)], self.plane_in)

    def close(self):
        for copy in self.copies():
            copy.wait_send()
        drain(self.spread.at[pl.ds(0, (PLANE - 1) * BLOCK)], self.plane_out)


RETURN_SCRATCH = [
    pltpu.VMEM((2, 2, HALF, 768), bf16),
    pltpu.VMEM((6, 2, HALF, 768), bf16),
    pltpu.VMEM((PAD, 768), bf16),
    pltpu.VMEM((PAD, 768), bf16),
    pltpu.SemaphoreType.DMA((6,)),
    pltpu.SemaphoreType.DMA((6,)),
    pltpu.SemaphoreType.DMA,
    pltpu.SemaphoreType.DMA,
]


def kernel_params(collective_id):
    return pltpu.CompilerParams(
        collective_id=collective_id, has_side_effects=True, vmem_limit_bytes=60 * 1024 * 1024
    )


VMEM = pl.BlockSpec(memory_space=pltpu.VMEM)


def expert_kernel(
    send, grad_rows, weight_in, weight_out, picked, resid, cotangent, gain_moe,
    x_out, hidden, grad_pre, y_part, grad_resid, gain_part,
    landed, held_in, held_out, grad_part, load_sems,
    d0, d1, d2, d3, *back,
):
    loads = [
        pltpu.make_async_copy(weight_in, held_in, load_sems.at[0]),
        pltpu.make_async_copy(weight_out, held_out, load_sems.at[1]),
    ]
    for load in loads:
        load.start()
    greet(1, 1)
    out_way = Dispatch(send, landed, x_out, (d0, d1, d2, d3))
    home_way = Return(grad_part, back[0], back[1], back[2], back[3], back[4:])
    out_way.cross()
    pack = packer()
    out_way.turn(0, pack)
    out_way.turn(1, pack)
    for load in loads:
        load.wait()

    def run(first, count):
        for j in range(2):
            span = pl.ds(first * 160, count * 160)
            pre_act = dot(x_out[j, span], held_in[j])
            cdf = 0.5 * (1.0 + lax.erf(pre_act * inv_root_two))
            hidden[j, span] = (pre_act * cdf).astype(bf16)
            slope = cdf + pre_act * jnp.exp(-0.5 * pre_act * pre_act) * inv_root_tau
            grad_hidden = dot_cols(grad_rows[j, span], held_out[j])
            grad_pre[j, span] = (grad_hidden * slope).astype(bf16)
            grad_part[j, span] = dot_cols(grad_pre[j, span], held_in[j]).astype(bf16)

    run(0, 1)
    out_way.relay()
    run(1, 2)
    home_way.near()
    out_way.last()
    run(3, 1)
    home_way.far()
    for j in range(2):
        y_part[j, 0:320] = dot(hidden[j, 0:320], held_out[j]).astype(bf16)
    home_way.add_far()
    for j in range(2):
        y_part[j, 320:640] = dot(hidden[j, 320:640], held_out[j]).astype(bf16)
    home_way.finish(0, pack)
    home_way.finish(1, pack)
    home_way.arrive()
    grad_normed = dot(picked[0] + picked[1], home_way.home[...])
    residual = resid[...]
    scale = rms_scale(residual)
    normal = residual * scale
    gain_part[...] = jnp.sum(grad_normed * normal, axis=0, keepdims=True)
    grad_unit = grad_normed * gain_moe[...]
    grad_resid[...] = cotangent[...].astype(f32) + scale * (
        grad_unit - normal * jnp.mean(grad_unit * normal, axis=1, keepdims=True)
    )
    out_way.close()
    home_way.close()


def run_experts(send, grad_rows, weight_in, weight_out, *local):
    rows = jax.ShapeDtypeStruct((2, EXPERT_ROWS, 768), bf16)
    anywhere = pl.BlockSpec(memory_space=pl.ANY)
    return pl.pallas_call(
        expert_kernel,
        out_shape=[
            rows,
            rows,
            rows,
            rows,
            jax.ShapeDtypeStruct((128, 768), f32),
            jax.ShapeDtypeStruct((1, 768), f32),
        ],
        in_specs=[VMEM, VMEM, anywhere, anywhere] + [VMEM] * 4,
        out_specs=[VMEM] * 6,
        scratch_shapes=[
            pltpu.VMEM((PAD, 768), bf16),
            pltpu.VMEM((2, 768, 768), bf16),
            pltpu.VMEM((2, 768, 768), bf16),
            pltpu.VMEM((2, EXPERT_ROWS, 768), bf16),
            pltpu.SemaphoreType.DMA((2,)),
        ]
        + DISPATCH_SCRATCH
        + RETURN_SCRATCH,
        compiler_params=kernel_params(3),
        name="experts",
    )(send, grad_rows, weight_in, weight_out, *local)


SEQ = 512
SIDE = 64
WIDTH = 768
HEAD_WIDTH = 192
LOCAL_HEADS = 3
score_scale = HEAD_DIM ** (-0.5)


class RingGather:
    def __init__(self, rows, sems):
        self.rows = rows
        self.out, self.arrived = sems

    def copies(self):
        e, z, right, left = place()

        def copy(index, owner, half, other):
            block = self.rows.at[pl.ds(pl.multiple_of(owner * 128 + half * SIDE, SIDE), SIDE)]
            return pltpu.make_async_remote_copy(
                block,
                block,
                self.out.at[index],
                self.arrived.at[index],
                device_id=(e, other),
                device_id_type=MESH,
            )

        def landing(index, owner, half):
            block = self.rows.at[pl.ds(pl.multiple_of(owner * 128 + half * SIDE, SIDE), SIDE)]
            return pltpu.make_async_copy(block, block, self.arrived.at[index])

        far = lax.rem(z + 2, RING)
        sends = [
            copy(0, z, 0, right),
            copy(1, z, 1, right),
            copy(2, z, 0, left),
            copy(3, z, 1, left),
            copy(4, left, 0, right),
            copy(5, right, 1, left),
        ]
        lands = [
            landing(0, left, 0),
            landing(1, left, 1),
            landing(2, right, 0),
            landing(3, right, 1),
            landing(4, far, 0),
            landing(5, far, 1),
        ]
        return sends, lands

    def start(self):
        sends, lands = self.copies()
        for index in (0, 3, 1, 2):
            sends[index].start()

    def finish(self):
        sends, lands = self.copies()
        lands[0].wait()
        sends[4].start()
        lands[3].wait()
        sends[5].start()
        for index in (1, 2, 4, 5):
            lands[index].wait()

    def close(self):
        sends, lands = self.copies()
        for send in sends:
            send.wait_send()


GATHER_SCRATCH = [pltpu.SemaphoreType.DMA((6,)), pltpu.SemaphoreType.DMA((6,))]


class RingSum:
    def __init__(self, partial, relayed, landed, sems):
        self.partial, self.relayed, self.landed = partial, relayed, landed
        self.out, self.arrived = sems

    def part(self, slot, half):
        e, z, right, left = place()
        owner = (z, right, left, lax.rem(z + 2, RING))[slot]
        return self.partial.at[pl.ds(pl.multiple_of(owner * 128 + half * SIDE, SIDE), SIDE)]

    def copies(self):
        e, z, right, left = place()

        def copy(index, source, other):
            return pltpu.make_async_remote_copy(
                source,
                self.landed.at[index],
                self.out.at[index],
                self.arrived.at[index],
                device_id=(e, other),
                device_id_type=MESH,
            )

        part = self.part
        return [
            copy(0, part(3, 0), right),
            copy(1, part(3, 1), left),
            copy(2, part(1, 1), right),
            copy(3, part(2, 0), left),
            copy(4, self.relayed.at[0], right),
            copy(5, self.relayed.at[1], left),
        ]

    def start(self):
        ring = self.copies()
        for index in range(4):
            ring[index].start()

    def add_far(self):
        ring = self.copies()
        for index, slot, half in ((0, 1, 0), (1, 2, 1)):
            ring[index].wait_recv()
            self.relayed[index] = (
                self.part(slot, half)[...].astype(f32) + self.landed[index].astype(f32)
            ).astype(bf16)
            ring[4 + index].start()

    def total(self):
        ring = self.copies()
        halves = []
        for half, direct, summed in ((0, 3, 4), (1, 2, 5)):
            ring[direct].wait_recv()
            ring[summed].wait_recv()
            halves.append(
                self.part(0, half)[...].astype(f32)
                + self.landed[direct].astype(f32)
                + self.landed[summed].astype(f32)
            )
        return jnp.concatenate(halves, axis=0)

    def close(self):
        for copy in self.copies():
            copy.wait_send()


SUM_SCRATCH = [
    pltpu.VMEM((SEQ, WIDTH), bf16),
    pltpu.VMEM((2, SIDE, WIDTH), bf16),
    pltpu.VMEM((6, SIDE, WIDTH), bf16),
    pltpu.SemaphoreType.DMA((6,)),
    pltpu.SemaphoreType.DMA((6,)),
]


def head_mask(h):
    lane = lax.broadcasted_iota(jnp.int32, (SEQ, HEAD_WIDTH), 1)
    return (lane >= h * HEAD_DIM) & (lane < (h + 1) * HEAD_DIM)


def sum_diagonals(square):
    rows = square
    for step in (32, 8, 1):
        count = rows.shape[0] // step
        rows = sum(
            pltpu.roll(rows[a * step : a * step + step], (SEQ - a * step) % SEQ, 1)
            if a
            else rows[:step]
            for a in range(count)
        )
    return rows


def bucket_hot_rows(bucket_rev):
    return (bucket_rev == lax.broadcasted_iota(jnp.int32, (32, SEQ), 0)).astype(f32)


def plane_sends(source_at, target_at, send_sem, recv_sem):
    e, z, right, left = place()

    def send(chip, carry):
        other = plane_target(e, chip * 2)
        pltpu.make_async_remote_copy(
            source_at(other // 2),
            target_at(e // 2),
            send_sem,
            recv_sem,
            device_id=(other, z),
            device_id_type=MESH,
        ).start()
        return carry

    lax.fori_loop(1, 16, send, 0)


def rms_scale(values):
    return lax.rsqrt(jnp.mean(values * values, axis=1, keepdims=True) + epsilon)


def select_rows(ids):
    expert = lax.broadcasted_iota(jnp.int32, (128, 64), 1)
    hot = [(ids[:, c : c + 1] == expert).astype(f32) for c in range(TOPK)]
    row = lax.broadcasted_iota(jnp.int32, (128, 128), 0)
    col = lax.broadcasted_iota(jnp.int32, (128, 128), 1)
    before = dot((col < row).astype(bf16), (hot[0] + hot[1]).astype(bf16))
    pos = lax.broadcasted_iota(jnp.int32, (128, PAD), 1)
    picks = []
    for c in range(TOPK):
        slot = jnp.sum(before * hot[c], axis=1, keepdims=True).astype(jnp.int32)
        own = ids[:, c : c + 1]
        first = own // 2
        picks.append((pos == first * BLOCK + (own - first * 2) * 5 + slot).astype(bf16))
    return picks


def attend_kernel(
    tokens, gain_attn, gain_moe, weights, cotangent, ids, gates, bias, bucket_rev,
    resid, units, whole, qkv, probs, attended, picked, send_rows, grad_rows,
    wall, whole32, grad_send, grad_landed, w_send, w_recv, s_send, s_recv,
    d0, d1, d2, d3, g0, g1, *ring_sum,
):
    e, z, right, left = place()
    core, chip = lax.rem(e, 2), e // 2
    greet(1, 1)
    wall[core, chip] = weights[...]
    plane_sends(
        lambda other: weights, lambda own: wall.at[core, own], w_send, w_recv
    )
    inputs = tokens[...].astype(f32)
    own_rows = pl.ds(pl.multiple_of(z * 128, 128), 128)
    units[own_rows] = (inputs * rms_scale(inputs)).astype(bf16)
    gather = RingGather(units, (g0, g1))
    gather.start()

    picks = select_rows(ids[...])
    for c in range(TOPK):
        picked[c] = picks[c]
    grad_out = cotangent[...].astype(f32)
    grad_send[...] = (
        dot_rows(picks[0], (gates[:, 0:1] * grad_out).astype(bf16))
        + dot_rows(picks[1], (gates[:, 1:2] * grad_out).astype(bf16))
    ).astype(bf16)
    grads = Dispatch(grad_send, grad_landed, grad_rows, (d0, d1, d2, d3))
    grads.cross()

    drain(wall.at[0, pl.ds(0, 15)], w_recv)
    sibling = pltpu.make_async_remote_copy(
        wall.at[core],
        wall.at[core],
        s_send,
        s_recv,
        device_id=(chip * 2 + 1 - core, z),
        device_id_type=MESH,
    )
    sibling.start()
    hot = bucket_hot_rows(bucket_rev[...])
    gather.finish()
    normed = (units[...].astype(f32) * gain_attn[...]).astype(bf16)
    pltpu.make_async_copy(wall.at[1 - core], wall.at[1 - core], s_recv).wait()
    for block in range(PLANE):
        whole32[24 * block : 24 * block + 24] = wall[block % 2, block // 2].astype(f32)[:24]
    whole[...] = whole32[...].astype(bf16)
    projected = dot(normed, whole[:, :640]).astype(bf16)
    qkv[...] = projected[:, : 3 * HEAD_WIDTH]
    queries = projected[:, :HEAD_WIDTH]
    keys = projected[:, HEAD_WIDTH : 2 * HEAD_WIDTH]
    values = projected[:, 2 * HEAD_WIDTH : 3 * HEAD_WIDTH]

    pack = packer()
    grads.turn(0, pack)
    grads.turn(1, pack)

    row = lax.broadcasted_iota(jnp.int32, (SEQ, SEQ), 0)
    col = lax.broadcasted_iota(jnp.int32, (SEQ, SEQ), 1)
    mixed = jnp.zeros((SEQ, HEAD_WIDTH), f32)
    for h in range(LOCAL_HEADS):
        mask = head_mask(h)
        rel = jnp.sum(bias[:, h : h + 1] * hot, axis=0, keepdims=True)
        shifted = pltpu.roll(jnp.broadcast_to(rel, (SEQ, SEQ)), 0, 1, stride=1, stride_axis=0)
        scores = dot_cols(jnp.where(mask, queries, jnp.zeros_like(queries)), keys) * score_scale
        scores = jnp.where(col <= row, scores + shifted, masked_value)
        raised = jnp.exp(scores - jnp.max(scores, axis=1, keepdims=True))
        weights_p = (raised / jnp.sum(raised, axis=1, keepdims=True)).astype(bf16)
        probs[h] = weights_p
        mixed = jnp.where(mask, dot(weights_p, values), mixed)
        if h == 0:
            grads.relay()
    attended[...] = mixed.astype(bf16)
    summing = RingSum(ring_sum[0], ring_sum[1], ring_sum[2], ring_sum[3:])
    ring_sum[0][...] = dot_cols(attended[...], whole[:, 3 * HEAD_WIDTH :]).astype(bf16)
    summing.start()
    summing.add_far()
    residual = inputs + summing.total()
    resid[...] = residual
    normed_m = (residual * rms_scale(residual) * gain_moe[...]).astype(bf16)
    send_rows[...] = dot_rows(picks[0] + picks[1], normed_m).astype(bf16)
    grads.last()
    gather.close()
    grads.close()
    summing.close()
    sibling.wait_send()
    drain(wall.at[0, pl.ds(0, 15)], w_send)


def attend(*operands):
    def shape(dims, kind=bf16):
        return jax.ShapeDtypeStruct(dims, kind)

    return pl.pallas_call(
        attend_kernel,
        out_shape=[
            shape((128, WIDTH), f32),
            shape((SEQ, WIDTH)),
            shape((WIDTH, WIDTH)),
            shape((SEQ, 3 * HEAD_WIDTH)),
            shape((LOCAL_HEADS, SEQ, SEQ)),
            shape((SEQ, HEAD_WIDTH)),
            shape((TOPK, 128, PAD)),
            shape((PAD, WIDTH)),
            shape((2, EXPERT_ROWS, WIDTH)),
        ],
        in_specs=[VMEM] * 9,
        out_specs=[VMEM] * 9,
        scratch_shapes=[
            pltpu.VMEM((2, 16, 32, WIDTH), bf16),
            pltpu.VMEM((WIDTH, WIDTH), f32),
            pltpu.VMEM((PAD, WIDTH), bf16),
            pltpu.VMEM((PAD, WIDTH), bf16),
            pltpu.SemaphoreType.DMA,
            pltpu.SemaphoreType.DMA,
            pltpu.SemaphoreType.DMA,
            pltpu.SemaphoreType.DMA,
        ]
        + DISPATCH_SCRATCH
        + GATHER_SCRATCH
        + SUM_SCRATCH,
        compiler_params=kernel_params(1),
        name="attend",
    )(*operands)


def attend_back_kernel(
    grad_resid, y_part, units, whole, qkv, probs, attended, tokens, resid, gates, picked,
    gain_attn, gain_moe_part, bucket_rev,
    out, grad_input, weight_grad, small,
    seq_grad, blocks, near_blocks, plane_landed, small_own, small_landed,
    s_send, s_recv, p_send, p_recv, t_send, t_recv, g0, g1, *rest,
):
    e, z, right, left = place()
    core, chip = lax.rem(e, 2), e // 2
    opposite = lax.rem(z + 2, RING)
    ring_sum, back = rest[:5], rest[5:]
    greet(1, 1, 1)
    own_rows = pl.ds(pl.multiple_of(z * 128, 128), 128)
    seq_grad[own_rows] = grad_resid[...].astype(bf16)
    gather = RingGather(seq_grad, (g0, g1))
    gather.start()
    home_way = Return(y_part, back[0], back[1], back[2], back[3], back[4:])
    hot = bucket_hot_rows(bucket_rev[...])
    proj = whole[:, 3 * HEAD_WIDTH :]
    queries = qkv[:, :HEAD_WIDTH]
    keys = qkv[:, HEAD_WIDTH : 2 * HEAD_WIDTH]
    values = qkv[:, 2 * HEAD_WIDTH :]
    gather.finish()
    home_way.far()
    home_way.near()
    grad_att = dot(seq_grad[...], proj).astype(bf16)
    proj_part = dot_rows(seq_grad[...], attended[...])
    zeros = jnp.zeros((SEQ, HEAD_WIDTH), f32)
    grad_q, grad_k, grad_v = zeros, zeros, zeros
    diagonals = []
    for h in range(LOCAL_HEADS):
        mask = head_mask(h)
        weights_p = probs[h]
        soft = weights_p.astype(f32)
        grad_w = dot_cols(jnp.where(mask, grad_att, jnp.zeros_like(grad_att)), values)
        row_dot = jnp.sum(soft * grad_w, axis=1, keepdims=True)
        grad_s = soft * (grad_w - row_dot)
        grad_scores = grad_s.astype(bf16)
        diagonals.append(sum_diagonals(grad_scores.astype(f32)))
        grad_q = jnp.where(mask, dot(grad_scores, keys), grad_q)
        grad_k = jnp.where(mask, dot_rows(grad_scores, queries), grad_k)
        grad_v = jnp.where(mask, dot_rows(weights_p, grad_att), grad_v)
        if h == 0:
            home_way.add_far()
    grad_qkv = jnp.concatenate(
        [grad_q * score_scale, grad_k * score_scale, grad_v], axis=1
    ).astype(bf16)
    grad_normed = dot_cols(grad_qkv, whole[:, : 3 * HEAD_WIDTH])
    summing = RingSum(ring_sum[0], ring_sum[1], ring_sum[2], ring_sum[3:])
    ring_sum[0][...] = grad_normed.astype(bf16)
    summing.start()
    unit_rows = units[...].astype(f32)
    gain_part = jnp.sum(grad_normed * unit_rows, axis=0, keepdims=True)
    normed = (unit_rows * gain_attn[...]).astype(bf16)
    qkv_part = dot_rows(normed, grad_qkv)
    full = jnp.concatenate([qkv_part, proj_part], axis=1)
    diagonal = jnp.concatenate(diagonals + [jnp.zeros((5, SEQ), f32)], axis=0)
    table_rows = lax.dot_general(
        diagonal, hot, (((1,), (1,)), ((), ())), precision=highest, preferred_element_type=f32
    )
    table_wide = jnp.concatenate([table_rows[:LOCAL_HEADS], jnp.zeros((3, 32), f32)], axis=0)
    table_wide = jnp.concatenate([table_wide, jnp.zeros((6, WIDTH - 32), f32)], axis=1)
    extra = jnp.concatenate([gain_part, gain_moe_part[...], table_wide], axis=0)
    for block in range(PLANE):
        blocks[block % 2, block // 2] = jnp.concatenate(
            [full[24 * block : 24 * block + 24], extra], axis=0
        ).astype(bf16)
    sibling = pltpu.make_async_remote_copy(
        blocks.at[1 - core],
        near_blocks,
        s_send,
        s_recv,
        device_id=(chip * 2 + 1 - core, z),
        device_id_type=MESH,
    )
    sibling.start()
    pack = packer()
    home_way.finish(0, pack)
    home_way.finish(1, pack)
    sibling.wait_recv()
    near_blocks[...] = (blocks[core].astype(f32) + near_blocks[...].astype(f32)).astype(bf16)
    plane_sends(
        lambda other: near_blocks.at[other], lambda own: plane_landed.at[own], p_send, p_recv
    )
    plane_landed[chip] = near_blocks[chip]
    summing.add_far()
    inputs = tokens[...].astype(f32)
    scale_first = rms_scale(inputs)
    normal_first = inputs * scale_first
    grad_unit = summing.total() * gain_attn[...]
    grad_input[...] = grad_resid[...] + scale_first * (
        grad_unit - normal_first * jnp.mean(grad_unit * normal_first, axis=1, keepdims=True)
    )
    home_way.arrive()
    home = home_way.home[...]
    out[...] = (
        resid[...] + gates[:, 0:1] * dot(picked[0], home) + gates[:, 1:2] * dot(picked[1], home)
    ).astype(bf16)
    drain(plane_landed.at[pl.ds(0, 15)], p_recv)
    total = plane_landed[0].astype(f32)
    for block in range(1, 16):
        total = total + plane_landed[block].astype(f32)
    weight_grad[...] = total[:24]
    small_own[...] = total[24:]
    shares = [
        pltpu.make_async_remote_copy(
            small_own,
            small_landed.at[index],
            t_send.at[index],
            t_recv.at[index],
            device_id=(e, other),
            device_id_type=MESH,
        )
        for index, other in enumerate((right, left, opposite))
    ]
    for share in shares:
        share.start()
    for share in shares:
        share.wait_recv()
    summed = small_own[...] + small_landed[0] + small_landed[1] + small_landed[2]
    line = lax.broadcasted_iota(jnp.int32, (8, WIDTH), 0)
    small[...] = jnp.where(line < 2, summed, small_own[...])
    for share in shares:
        share.wait_send()
    gather.close()
    home_way.close()
    summing.close()
    sibling.wait_send()
    drain(plane_landed.at[pl.ds(0, 15)], p_send)


def attend_back(*operands):
    def shape(dims, kind=f32):
        return jax.ShapeDtypeStruct(dims, kind)

    return pl.pallas_call(
        attend_back_kernel,
        out_shape=[
            shape((128, WIDTH), bf16),
            shape((128, WIDTH)),
            shape((24, WIDTH)),
            shape((8, WIDTH)),
        ],
        in_specs=[VMEM] * 14,
        out_specs=[VMEM] * 4,
        scratch_shapes=[
            pltpu.VMEM((SEQ, WIDTH), bf16),
            pltpu.VMEM((2, 16, 32, WIDTH), bf16),
            pltpu.VMEM((16, 32, WIDTH), bf16),
            pltpu.VMEM((16, 32, WIDTH), bf16),
            pltpu.VMEM((8, WIDTH), f32),
            pltpu.VMEM((3, 8, WIDTH), f32),
            pltpu.SemaphoreType.DMA,
            pltpu.SemaphoreType.DMA,
            pltpu.SemaphoreType.DMA,
            pltpu.SemaphoreType.DMA,
            pltpu.SemaphoreType.DMA((3,)),
            pltpu.SemaphoreType.DMA((3,)),
        ]
        + GATHER_SCRATCH
        + SUM_SCRATCH
        + RETURN_SCRATCH,
        compiler_params=kernel_params(2),
        name="attend_back",
    )(*operands)


def body(
    tokens,
    gain_attn,
    gain_moe,
    qkv_weight,
    proj_weight,
    bias_table,
    expert_in,
    expert_out,
    expert_ids,
    gate_values,
    bucket_table,
    cotangent,
):
    share = qkv_weight.shape[0]
    weights = jnp.concatenate([qkv_weight.reshape(share, 3 * HEAD_WIDTH), proj_weight.T], axis=1)
    weights = jnp.pad(weights, ((0, 8), (0, 0)))
    gain_first, gain_second = gain_attn[None], gain_moe[None]
    bucket_rev = jnp.concatenate([bucket_table[:1], bucket_table[:0:-1]])[None]
    resid, units, whole, qkv, probs, attended, picked, send_rows, grad_rows = attend(
        tokens, gain_first, gain_second, weights, cotangent, expert_ids, gate_values,
        bias_table, bucket_rev,
    )
    received, hidden, grad_pre, y_part, grad_resid, gain_part = run_experts(
        send_rows, grad_rows, expert_in, expert_out, picked, resid, cotangent, gain_second
    )
    out, grad_input, weight_grad, small = attend_back(
        grad_resid, y_part, units, whole, qkv, probs, attended, tokens, resid, gate_values,
        picked, gain_first, gain_part, bucket_rev,
    )
    expert_out_grad = jnp.einsum("jrf,jrd->jfd", hidden, grad_rows, preferred_element_type=f32)
    expert_in_grad = jnp.einsum("jrd,jrf->jdf", received, grad_pre, preferred_element_type=f32)
    e, z = lax.axis_index("expert"), lax.axis_index("mp")
    piece = (e * RING + z) * 6
    gains = lax.dynamic_slice_in_dim(small[:2], piece, 6, axis=1)
    table_grad = lax.dynamic_slice_in_dim(small[2 : 2 + LOCAL_HEADS], e, 1, axis=1).T
    return (
        out,
        grad_input,
        gains[0],
        gains[1],
        weight_grad[:, : 3 * HEAD_WIDTH].reshape(share, 3, HEAD_WIDTH),
        weight_grad[:, 3 * HEAD_WIDTH :].T,
        table_grad,
        expert_in_grad,
        expert_out_grad,
    )


def solution(mesh):
    placed = (
        P(("expert", "mp"), None),
        P(),
        P(),
        P("expert", None, "mp"),
        P("mp", "expert"),
        P(None, "mp"),
        P("expert", None, "mp"),
        P("expert", "mp", None),
        P(("expert", "mp"), None),
        P(("expert", "mp"), None),
        P(),
        P(("expert", "mp"), None),
    )
    return jax.shard_map(
        body,
        mesh=mesh,
        in_specs=placed,
        out_specs=(
            P(("expert", "mp"), None),
            P(("expert", "mp"), None),
            P(("expert", "mp")),
            P(("expert", "mp")),
            P("expert", None, "mp"),
            P("mp", "expert"),
            P("expert", "mp"),
            P("expert", None, "mp"),
            P("expert", "mp", None),
        ),
        check_vma=False,
    )
```

```python
import jax
import jax.numpy as jnp
from jax import lax
from jax.experimental import pallas as pl
from jax.experimental.pallas import tpu as pltpu
from jax.sharding import PartitionSpec as P

HEAD_DIM = 64
TOPK = 2


epsilon = 1e-06
masked_value = -1e30
inv_root_two = 0.7071067811865476
inv_root_tau = 0.3989422804014327
highest = lax.Precision.HIGHEST


MESH = pl.DeviceIdType.MESH
BLOCK = 16
HALF = 80
PLANE = 32
RING = 4
PAD = PLANE * BLOCK
ROWS = 320
EXPERT_ROWS = 640
f32 = jnp.float32
bf16 = jnp.bfloat16


def place():
    e, z = lax.axis_index("expert"), lax.axis_index("mp")
    return e, z, lax.rem(z + 1, RING), lax.rem(z + RING - 1, RING)


def plane_target(e, d):
    step = d // 8
    dy, dx, dc = lax.rem(step * 2, 4) + step // 2, lax.rem(d // 2, 4), lax.rem(d, 2)
    y, x, c = e // 8, lax.rem(e // 2, 4), lax.rem(e, 2)
    return lax.rem(y + dy, 4) * 8 + lax.rem(x + dx, 4) * 2 + lax.rem(c + dc, 2)


def plane_source(e, d):
    step = d // 8
    dy, dx, dc = lax.rem(step * 2, 4) + step // 2, lax.rem(d // 2, 4), lax.rem(d, 2)
    y, x, c = e // 8, lax.rem(e // 2, 4), lax.rem(e, 2)
    return lax.rem(y + 4 - dy, 4) * 8 + lax.rem(x + 4 - dx, 4) * 2 + lax.rem(c + dc, 2)


def block_at(index):
    return pl.ds(pl.multiple_of(index * BLOCK, BLOCK), BLOCK)


def greet(plane, ring, across=0):
    e, z, right, left = place()
    barrier = pltpu.get_barrier_semaphore()
    if plane:

        def signal(d, carry):
            pl.semaphore_signal(
                barrier, inc=1, device_id=(plane_target(e, d), z), device_id_type=MESH
            )
            return carry

        lax.fori_loop(1, PLANE, signal, 0)
    if ring:
        for other in (right, left):
            pl.semaphore_signal(barrier, inc=1, device_id=(e, other), device_id_type=MESH)
    if across:
        other = lax.rem(z + 2, RING)
        pl.semaphore_signal(barrier, inc=1, device_id=(e, other), device_id_type=MESH)
    pl.semaphore_wait(barrier, (PLANE - 1) * plane + 2 * ring + across)


def drain(ref, sem):
    pltpu.make_async_copy(ref, ref, sem).wait()


def dot(left, right):
    return jnp.dot(left, right, preferred_element_type=f32)


def dot_rows(left, right):
    return lax.dot_general(left, right, (((0,), (0,)), ((), ())), preferred_element_type=f32)


def dot_cols(left, right):
    return lax.dot_general(left, right, (((1,), (1,)), ((), ())), preferred_element_type=f32)


def packer():
    row = lax.broadcasted_iota(jnp.int32, (2 * HALF, 256), 0)
    col = lax.broadcasted_iota(jnp.int32, (2 * HALF, 256), 1)
    expert = (row >= HALF).astype(jnp.int32)
    inner = row - expert * HALF
    source = (inner * 205) // 1024
    slot = inner - source * 5
    return (col == source * BLOCK + expert * 5 + slot).astype(bf16)


class Dispatch:
    def __init__(self, send, landed, rows, sems):
        self.send, self.landed, self.rows = send, landed, rows
        self.plane_out, self.plane_in, self.ring_out, self.ring_in = sems

    def part(self, slot, half):
        return self.rows.at[:, pl.ds(slot * 160 + half * HALF, HALF)]

    def cross(self, half):
        e, z, right, left = place()

        def send(d, carry):
            other = plane_target(e, d)
            pltpu.make_async_remote_copy(
                self.send.at[block_at(other)],
                self.landed.at[block_at(d)],
                self.plane_out.at[half],
                self.plane_in.at[half],
                device_id=(other, z),
                device_id_type=MESH,
            ).start()
            return carry

        lax.fori_loop(max(1, 16 * half), 16 * half + 16, send, 0)
        if half == 0:
            self.landed[0:BLOCK] = self.send[block_at(e)]

    def crossed(self, half):
        drain(self.send.at[pl.ds(0, (15 + half) * BLOCK)], self.plane_out.at[half])

    def copy(self, index, source, target, other):
        e = lax.axis_index("expert")
        return pltpu.make_async_remote_copy(
            source,
            target,
            self.ring_out.at[index],
            self.ring_in.at[index],
            device_id=(e, other),
            device_id_type=MESH,
        )

    def copies(self):
        e, z, right, left = place()
        part = self.part
        return [
            self.copy(0, part(0, 0), part(2, 0), right),
            self.copy(1, part(0, 1), part(2, 1), right),
            self.copy(2, part(0, 0), part(1, 0), left),
            self.copy(3, part(0, 1), part(1, 1), left),
            self.copy(4, part(2, 0), part(3, 0), right),
            self.copy(5, part(1, 1), part(3, 1), left),
        ]

    def turn(self, half, pack):
        lo = 256 * half
        span = self.landed.at[pl.ds(lo + (BLOCK if half == 0 else 0), 256 - (BLOCK if half == 0 else 0))]
        drain(span, self.plane_in.at[half])
        packed = dot(pack, self.landed[lo : lo + 256]).astype(bf16)
        for j in range(2):
            self.rows[j, half * HALF : half * HALF + HALF] = packed[j * HALF : j * HALF + HALF]
        ring = self.copies()
        ring[half].start()
        ring[2 + half].start()

    def relay(self):
        ring = self.copies()
        ring[0].wait_recv()
        ring[4].start()
        ring[3].wait_recv()
        ring[5].start()
        ring[1].wait_recv()
        ring[2].wait_recv()

    def last(self):
        ring = self.copies()
        ring[4].wait_recv()
        ring[5].wait_recv()

    def close(self):
        for copy in self.copies():
            copy.wait_send()


DISPATCH_SCRATCH = [
    pltpu.SemaphoreType.DMA((2,)),
    pltpu.SemaphoreType.DMA((2,)),
    pltpu.SemaphoreType.DMA((6,)),
    pltpu.SemaphoreType.DMA((6,)),
]


class Return:
    def __init__(self, partial, relayed, landed, spread, home, sems):
        self.partial, self.relayed, self.landed = partial, relayed, landed
        self.spread, self.home = spread, home
        self.ring_out, self.ring_in, self.plane_out, self.plane_in = sems

    def part(self, slot, half):
        return self.partial.at[:, pl.ds(slot * 160 + half * HALF, HALF)]

    def copies(self):
        e, z, right, left = place()

        def copy(index, source, other):
            return pltpu.make_async_remote_copy(
                source,
                self.landed.at[index],
                self.ring_out.at[index],
                self.ring_in.at[index],
                device_id=(e, other),
                device_id_type=MESH,
            )

        part = self.part
        return [
            copy(0, part(3, 0), right),
            copy(1, part(3, 1), left),
            copy(2, part(1, 1), right),
            copy(3, part(2, 0), left),
            copy(4, self.relayed.at[0], right),
            copy(5, self.relayed.at[1], left),
        ]

    def near(self):
        ring = self.copies()
        ring[2].start()
        ring[3].start()

    def far(self):
        ring = self.copies()
        ring[0].start()
        ring[1].start()

    def add_far(self):
        ring = self.copies()
        for index, slot, half in ((0, 1, 0), (1, 2, 1)):
            ring[index].wait_recv()
            self.relayed[index] = (
                self.part(slot, half)[...].astype(f32) + self.landed[index].astype(f32)
            ).astype(bf16)
            ring[4 + index].start()

    def finish(self, half, pack):
        e, z, right, left = place()
        ring = self.copies()
        direct, summed = (3, 4) if half == 0 else (2, 5)
        ring[direct].wait_recv()
        ring[summed].wait_recv()
        total = (
            self.part(0, half)[...].astype(f32)
            + self.landed[direct].astype(f32)
            + self.landed[summed].astype(f32)
        ).astype(bf16)
        flat = jnp.concatenate([total[0], total[1]], axis=0)
        self.spread[256 * half : 256 * half + 256] = dot_rows(pack, flat).astype(bf16)

        def send(d, carry):
            pltpu.make_async_remote_copy(
                self.spread.at[block_at(d)],
                self.home.at[block_at(e)],
                self.plane_out,
                self.plane_in,
                device_id=(plane_source(e, d), z),
                device_id_type=MESH,
            ).start()
            return carry

        lax.fori_loop(max(1, 16 * half), 16 * half + 16, send, 0)
        if half == 0:
            self.home[block_at(e)] = self.spread[0:BLOCK]

    def arrive(self):
        drain(self.home.at[pl.ds(0, (PLANE - 1) * BLOCK)], self.plane_in)

    def close(self):
        for copy in self.copies():
            copy.wait_send()
        drain(self.spread.at[pl.ds(0, (PLANE - 1) * BLOCK)], self.plane_out)


RETURN_SCRATCH = [
    pltpu.VMEM((2, 2, HALF, 768), bf16),
    pltpu.VMEM((6, 2, HALF, 768), bf16),
    pltpu.VMEM((PAD, 768), bf16),
    pltpu.VMEM((PAD, 768), bf16),
    pltpu.SemaphoreType.DMA((6,)),
    pltpu.SemaphoreType.DMA((6,)),
    pltpu.SemaphoreType.DMA,
    pltpu.SemaphoreType.DMA,
]


def kernel_params(collective_id):
    return pltpu.CompilerParams(
        collective_id=collective_id, has_side_effects=True, vmem_limit_bytes=60 * 1024 * 1024
    )


VMEM = pl.BlockSpec(memory_space=pltpu.VMEM)


SEQ = 512
SIDE = 64
WIDTH = 768
HEAD_WIDTH = 192
LOCAL_HEADS = 3
score_scale = HEAD_DIM ** (-0.5)


class RingGather:
    def __init__(self, rows, sems):
        self.rows = rows
        self.out, self.arrived = sems

    def copies(self):
        e, z, right, left = place()

        def copy(index, owner, half, other):
            block = self.rows.at[pl.ds(pl.multiple_of(owner * 128 + half * SIDE, SIDE), SIDE)]
            return pltpu.make_async_remote_copy(
                block,
                block,
                self.out.at[index],
                self.arrived.at[index],
                device_id=(e, other),
                device_id_type=MESH,
            )

        def landing(index, owner, half):
            block = self.rows.at[pl.ds(pl.multiple_of(owner * 128 + half * SIDE, SIDE), SIDE)]
            return pltpu.make_async_copy(block, block, self.arrived.at[index])

        far = lax.rem(z + 2, RING)
        sends = [
            copy(0, z, 0, right),
            copy(1, z, 1, right),
            copy(2, z, 0, left),
            copy(3, z, 1, left),
            copy(4, left, 0, right),
            copy(5, right, 1, left),
        ]
        lands = [
            landing(0, left, 0),
            landing(1, left, 1),
            landing(2, right, 0),
            landing(3, right, 1),
            landing(4, far, 0),
            landing(5, far, 1),
        ]
        return sends, lands

    def start(self):
        sends, lands = self.copies()
        for index in (0, 3, 1, 2):
            sends[index].start()

    def finish(self):
        sends, lands = self.copies()
        lands[0].wait()
        sends[4].start()
        lands[3].wait()
        sends[5].start()
        for index in (1, 2, 4, 5):
            lands[index].wait()

    def close(self):
        sends, lands = self.copies()
        for send in sends:
            send.wait_send()


GATHER_SCRATCH = [pltpu.SemaphoreType.DMA((6,)), pltpu.SemaphoreType.DMA((6,))]


class RingSum:
    def __init__(self, partial, relayed, landed, sems):
        self.partial, self.relayed, self.landed = partial, relayed, landed
        self.out, self.arrived = sems

    def part(self, slot, half):
        e, z, right, left = place()
        owner = (z, right, left, lax.rem(z + 2, RING))[slot]
        return self.partial.at[pl.ds(pl.multiple_of(owner * 128 + half * SIDE, SIDE), SIDE)]

    def copies(self):
        e, z, right, left = place()

        def copy(index, source, other):
            return pltpu.make_async_remote_copy(
                source,
                self.landed.at[index],
                self.out.at[index],
                self.arrived.at[index],
                device_id=(e, other),
                device_id_type=MESH,
            )

        part = self.part
        return [
            copy(0, part(3, 0), right),
            copy(1, part(3, 1), left),
            copy(2, part(1, 1), right),
            copy(3, part(2, 0), left),
            copy(4, self.relayed.at[0], right),
            copy(5, self.relayed.at[1], left),
        ]

    def start(self):
        ring = self.copies()
        for index in range(4):
            ring[index].start()

    def add_far(self):
        ring = self.copies()
        for index, slot, half in ((0, 1, 0), (1, 2, 1)):
            ring[index].wait_recv()
            self.relayed[index] = (
                self.part(slot, half)[...].astype(f32) + self.landed[index].astype(f32)
            ).astype(bf16)
            ring[4 + index].start()

    def total(self):
        ring = self.copies()
        halves = []
        for half, direct, summed in ((0, 3, 4), (1, 2, 5)):
            ring[direct].wait_recv()
            ring[summed].wait_recv()
            halves.append(
                self.part(0, half)[...].astype(f32)
                + self.landed[direct].astype(f32)
                + self.landed[summed].astype(f32)
            )
        return jnp.concatenate(halves, axis=0)

    def close(self):
        for copy in self.copies():
            copy.wait_send()


SUM_SCRATCH = [
    pltpu.VMEM((SEQ, WIDTH), bf16),
    pltpu.VMEM((2, SIDE, WIDTH), bf16),
    pltpu.VMEM((6, SIDE, WIDTH), bf16),
    pltpu.SemaphoreType.DMA((6,)),
    pltpu.SemaphoreType.DMA((6,)),
]


def head_mask(h):
    lane = lax.broadcasted_iota(jnp.int32, (SEQ, HEAD_WIDTH), 1)
    return (lane >= h * HEAD_DIM) & (lane < (h + 1) * HEAD_DIM)


def sum_diagonals(square):
    rows = square
    for step in (32, 8, 1):
        count = rows.shape[0] // step
        rows = sum(
            pltpu.roll(rows[a * step : a * step + step], (SEQ - a * step) % SEQ, 1)
            if a
            else rows[:step]
            for a in range(count)
        )
    return rows


def bucket_hot_rows(bucket_rev):
    return (bucket_rev == lax.broadcasted_iota(jnp.int32, (32, SEQ), 0)).astype(f32)


def plane_sends(source_at, target_at, send_sem, recv_sem_at):
    e, z, right, left = place()

    def send(chip, carry):
        other = plane_target(e, chip * 2)
        pltpu.make_async_remote_copy(
            source_at(other // 2),
            target_at(e // 2),
            send_sem,
            recv_sem_at(e // 2),
            device_id=(other, z),
            device_id_type=MESH,
        ).start()
        return carry

    lax.fori_loop(1, 16, send, 0)


def rms_scale(values):
    return lax.rsqrt(jnp.mean(values * values, axis=1, keepdims=True) + epsilon)


def select_rows(ids):
    expert = lax.broadcasted_iota(jnp.int32, (128, 64), 1)
    hot = [(ids[:, c : c + 1] == expert).astype(f32) for c in range(TOPK)]
    row = lax.broadcasted_iota(jnp.int32, (128, 128), 0)
    col = lax.broadcasted_iota(jnp.int32, (128, 128), 1)
    before = dot((col < row).astype(bf16), (hot[0] + hot[1]).astype(bf16))
    pos = lax.broadcasted_iota(jnp.int32, (128, PAD), 1)
    picks = []
    for c in range(TOPK):
        slot = jnp.sum(before * hot[c], axis=1, keepdims=True).astype(jnp.int32)
        own = ids[:, c : c + 1]
        first = own // 2
        picks.append((pos == first * BLOCK + (own - first * 2) * 5 + slot).astype(bf16))
    return picks


def as_column(row):
    n = row.shape[1]
    same = lax.broadcasted_iota(jnp.int32, (n, n), 0) == lax.broadcasted_iota(jnp.int32, (n, n), 1)
    return jnp.sum(jnp.where(same, row, 0.0), axis=1, keepdims=True)


def as_row(rows):
    return jnp.concatenate([rows[i : i + 1] for i in range(rows.shape[0])], axis=1)


def layer_kernel(
    tokens, gain_attn, gain_moe, qkv_weight, proj_weight, bias, weight_in, weight_out,
    ids, gates, buckets, cotangent,
    out, grad_input, qkv_grad, proj_grad, gain_first, gain_second, table_out,
    rows_hbm, hidden_hbm, grad_pre_hbm, grad_rows_hbm,
    units, whole, probs, picked, resid, mine, wall, whole32,
    x_send, x_landed, x_rows, g_send, g_landed, g_rows,
    held_in, held_out, hidden, grad_pre, grad_part, y_part,
    seq_grad, blocks, near_blocks, plane_landed, small_own, small_landed,
    load_sems, save_sems, w_send, w_recv, s_send, s_recv, v_send, v_recv,
    p_send, p_recv, t_send, t_recv, *rest,
):
    x_sems, g_sems, rest = rest[:4], rest[4:8], rest[8:]
    unit_sems, grad_sems, rest = rest[:2], rest[2:4], rest[4:]
    sum_a, sum_b, rest = rest[:5], rest[5:10], rest[10:]
    back_x, back_y = rest[:8], rest[8:]
    e, z, right, left = place()
    core, chip = lax.rem(e, 2), e // 2
    twin = chip * 2 + 1 - core
    opposite = lax.rem(z + 2, RING)
    loads = [
        pltpu.make_async_copy(weight_in, held_in, load_sems.at[0]),
        pltpu.make_async_copy(weight_out, held_out, load_sems.at[1]),
    ]
    for load in loads:
        load.start()
    greet(1, 1, 1)

    mine[...] = jnp.concatenate(
        [qkv_weight[i].astype(f32) for i in range(3)] + [proj_weight[...].astype(f32)], axis=1
    ).astype(bf16)
    plane_sends(lambda other: mine, lambda own: wall.at[core, own], w_send, w_recv.at.__getitem__)
    inputs = tokens[...].astype(f32)
    own_rows = pl.ds(pl.multiple_of(z * 128, 128), 128)
    units[own_rows] = (inputs * rms_scale(inputs)).astype(bf16)
    unit_ring = RingGather(units, unit_sems)
    unit_ring.start()
    wall[core, chip] = mine[...]

    gain_a, gain_m = as_row(gain_attn[...]), as_row(gain_moe[...])
    id_columns = jnp.concatenate(
        [as_column(ids[c : c + 1].astype(f32)) for c in range(TOPK)], axis=1
    ).astype(jnp.int32)
    gate_columns = [as_column(gates[c : c + 1]) for c in range(TOPK)]
    picks = select_rows(id_columns)
    for c in range(TOPK):
        picked[c] = picks[c]
    grad_out = cotangent[...].astype(f32)
    g_send[...] = (
        dot_rows(picks[0], (gate_columns[0] * grad_out).astype(bf16))
        + dot_rows(picks[1], (gate_columns[1] * grad_out).astype(bf16))
    ).astype(bf16)
    grads = Dispatch(g_send, g_landed, g_rows, g_sems)
    far_row = lax.broadcasted_iota(jnp.int32, (SEQ, SEQ), 0)
    far_col = lax.broadcasted_iota(jnp.int32, (SEQ, SEQ), 1)
    mirror = (far_row + far_col == jnp.where(far_col == 0, 0, SEQ)).astype(bf16)
    hot = dot(bucket_hot_rows(as_row(buckets[...])).astype(bf16), mirror)
    pack = packer()
    unit_ring.finish()
    unit_rows = units[...].astype(f32)
    normed = (unit_rows * gain_a).astype(bf16)

    def pass_on(source):
        return pltpu.make_async_remote_copy(
            wall.at[core, source],
            wall.at[core, source],
            s_send,
            s_recv,
            device_id=(twin, z),
            device_id_type=MESH,
        )

    pass_on(chip).start()

    def forward(step, carry):
        source = plane_source(e, step * 2) // 2
        pltpu.make_async_copy(wall.at[core, source], wall.at[core, source], w_recv.at[source]).wait()
        pass_on(source).start()
        return carry

    lax.fori_loop(1, 16, forward, 0)
    drain(wall.at[0, pl.ds(0, 15)], w_send)
    grads.cross(0)
    grads.cross(1)
    drain(wall.at[1 - core], s_recv)
    for block in range(PLANE):
        whole32[24 * block : 24 * block + 24] = wall[block % 2, block // 2].astype(f32)
    whole[...] = whole32[...].astype(bf16)

    projected = dot(normed, whole[:, :640]).astype(bf16)
    queries = projected[:, :HEAD_WIDTH]
    keys = projected[:, HEAD_WIDTH : 2 * HEAD_WIDTH]
    values = projected[:, 2 * HEAD_WIDTH : 3 * HEAD_WIDTH]
    mixed = jnp.zeros((SEQ, HEAD_WIDTH), f32)
    for h in range(LOCAL_HEADS):
        mask = head_mask(h)
        rel = jnp.sum(as_column(bias[h : h + 1]) * hot, axis=0, keepdims=True)
        shifted = pltpu.roll(jnp.broadcast_to(rel, (SEQ, SEQ)), 0, 1, stride=1, stride_axis=0)
        scores = dot_cols(jnp.where(mask, queries, jnp.zeros_like(queries)), keys) * score_scale
        scores = jnp.where(far_col <= far_row, scores + shifted, masked_value)
        raised = jnp.exp(scores - jnp.max(scores, axis=1, keepdims=True))
        weights_p = (raised / jnp.sum(raised, axis=1, keepdims=True)).astype(bf16)
        probs[h] = weights_p
        mixed = jnp.where(mask, dot(weights_p, values), mixed)
    attended = mixed.astype(bf16)
    proj = whole[:, 3 * HEAD_WIDTH :]
    sum_a[0][...] = dot_cols(attended, proj).astype(bf16)
    attn_sum = RingSum(sum_a[0], sum_a[1], sum_a[2], sum_a[3:])
    attn_sum.start()
    attn_sum.add_far()
    residual = inputs + attn_sum.total()
    resid[...] = residual
    scale_m = rms_scale(residual)
    normal_m = residual * scale_m
    x_send[...] = dot_rows(picks[0] + picks[1], (normal_m * gain_m).astype(bf16)).astype(bf16)

    out_way = Dispatch(x_send, x_landed, x_rows, x_sems)
    home_way = Return(grad_part, back_x[0], back_x[1], back_x[2], back_x[3], back_x[4:])
    out_way.cross(0)
    grads.turn(0, pack)
    grads.turn(1, pack)
    out_way.crossed(0)
    out_way.cross(1)
    out_way.turn(0, pack)
    out_way.turn(1, pack)
    for load in loads:
        load.wait()

    def run(first, count):
        for j in range(2):
            span = pl.ds(first * 160, count * 160)
            pre_act = dot(x_rows[j, span], held_in[j])
            cdf = 0.5 * (1.0 + lax.erf(pre_act * inv_root_two))
            hidden[j, span] = (pre_act * cdf).astype(bf16)
            slope = cdf + pre_act * jnp.exp(-0.5 * pre_act * pre_act) * inv_root_tau
            grad_hidden = dot_cols(g_rows[j, span], held_out[j])
            grad_pre[j, span] = (grad_hidden * slope).astype(bf16)
            grad_part[j, span] = dot_cols(grad_pre[j, span], held_in[j]).astype(bf16)

    run(0, 1)
    grads.relay()
    out_way.relay()
    run(1, 2)
    home_way.near()
    grads.last()
    out_way.last()
    run(3, 1)
    home_way.far()
    saves = [
        pltpu.make_async_copy(source, target, save_sems.at[index])
        for index, (source, target) in enumerate(
            (
                (x_rows, rows_hbm),
                (hidden, hidden_hbm),
                (grad_pre, grad_pre_hbm),
                (g_rows, grad_rows_hbm),
            )
        )
    ]
    for save in saves:
        save.start()
    for j in range(2):
        y_part[j, 0:320] = dot(hidden[j, 0:320], held_out[j]).astype(bf16)
    home_way.add_far()
    for j in range(2):
        y_part[j, 320:640] = dot(hidden[j, 320:640], held_out[j]).astype(bf16)
    home_way.finish(0, pack)
    home_way.finish(1, pack)
    y_way = Return(y_part, back_y[0], back_y[1], back_y[2], back_y[3], back_y[4:])
    y_way.far()
    y_way.near()
    y_way.add_far()
    home_way.arrive()
    grad_normed = dot(picked[0] + picked[1], home_way.home[...])
    gain_m_part = jnp.sum(grad_normed * normal_m, axis=0, keepdims=True)
    grad_unit_m = grad_normed * gain_m
    grad_resid = grad_out + scale_m * (
        grad_unit_m - normal_m * jnp.mean(grad_unit_m * normal_m, axis=1, keepdims=True)
    )

    seq_grad[own_rows] = grad_resid.astype(bf16)
    grad_ring = RingGather(seq_grad, grad_sems)
    grad_ring.start()
    grad_ring.finish()
    grad_att = dot(seq_grad[...], proj).astype(bf16)
    proj_part = dot_rows(seq_grad[...], attended)
    y_way.finish(0, pack)
    y_way.finish(1, pack)
    zeros = jnp.zeros((SEQ, HEAD_WIDTH), f32)
    grad_q, grad_k, grad_v = zeros, zeros, zeros
    diagonals = []
    for h in range(LOCAL_HEADS):
        mask = head_mask(h)
        weights_p = probs[h]
        soft = weights_p.astype(f32)
        grad_w = dot_cols(jnp.where(mask, grad_att, jnp.zeros_like(grad_att)), values)
        row_dot = jnp.sum(soft * grad_w, axis=1, keepdims=True)
        grad_scores = (soft * (grad_w - row_dot)).astype(bf16)
        diagonals.append(sum_diagonals(grad_scores.astype(f32)))
        grad_q = jnp.where(mask, dot(grad_scores, keys), grad_q)
        grad_k = jnp.where(mask, dot_rows(grad_scores, queries), grad_k)
        grad_v = jnp.where(mask, dot_rows(weights_p, grad_att), grad_v)
    grad_qkv = jnp.concatenate(
        [grad_q * score_scale, grad_k * score_scale, grad_v], axis=1
    ).astype(bf16)
    grad_normed_a = dot_cols(grad_qkv, whole[:, : 3 * HEAD_WIDTH])
    sum_b[0][...] = grad_normed_a.astype(bf16)
    input_sum = RingSum(sum_b[0], sum_b[1], sum_b[2], sum_b[3:])
    input_sum.start()
    gain_part = jnp.sum(grad_normed_a * unit_rows, axis=0, keepdims=True)
    full = jnp.concatenate([dot_rows(normed, grad_qkv), proj_part], axis=1)
    diagonal = jnp.concatenate(diagonals + [jnp.zeros((5, SEQ), f32)], axis=0)
    table_rows = lax.dot_general(
        diagonal, hot, (((1,), (1,)), ((), ())), precision=highest, preferred_element_type=f32
    )
    table_wide = jnp.concatenate([table_rows[:LOCAL_HEADS], jnp.zeros((3, 32), f32)], axis=0)
    table_wide = jnp.concatenate([table_wide, jnp.zeros((6, WIDTH - 32), f32)], axis=1)
    extra = jnp.concatenate([gain_part, gain_m_part, table_wide], axis=0)
    for block in range(PLANE):
        blocks[block % 2, block // 2] = jnp.concatenate(
            [full[24 * block : 24 * block + 24], extra], axis=0
        ).astype(bf16)
    sibling = pltpu.make_async_remote_copy(
        blocks.at[1 - core],
        near_blocks,
        v_send,
        v_recv,
        device_id=(twin, z),
        device_id_type=MESH,
    )
    sibling.start()
    input_sum.add_far()
    sibling.wait_recv()
    near_blocks[...] = (blocks[core].astype(f32) + near_blocks[...].astype(f32)).astype(bf16)
    plane_sends(
        lambda other: near_blocks.at[other],
        lambda own: plane_landed.at[own],
        p_send,
        lambda own: p_recv,
    )
    plane_landed[chip] = near_blocks[chip]
    y_way.arrive()
    home = y_way.home[...]
    out[...] = (
        resid[...] + gate_columns[0] * dot(picked[0], home) + gate_columns[1] * dot(picked[1], home)
    ).astype(bf16)
    scale_first = rms_scale(inputs)
    normal_first = inputs * scale_first
    grad_unit = input_sum.total() * gain_a
    grad_input[...] = grad_resid + scale_first * (
        grad_unit - normal_first * jnp.mean(grad_unit * normal_first, axis=1, keepdims=True)
    )
    drain(plane_landed.at[pl.ds(0, 15)], p_recv)
    total = plane_landed[0].astype(f32)
    for block in range(1, 16):
        total = total + plane_landed[block].astype(f32)
    small_own[...] = total[24:]
    shares = [
        pltpu.make_async_remote_copy(
            small_own,
            small_landed.at[index],
            t_send.at[index],
            t_recv.at[index],
            device_id=(e, other),
            device_id_type=MESH,
        )
        for index, other in enumerate((right, left, opposite))
    ]
    for share in shares:
        share.start()
    for i in range(3):
        qkv_grad[i] = total[:24, i * HEAD_WIDTH : (i + 1) * HEAD_WIDTH]
    proj_grad[...] = total[:24, 3 * HEAD_WIDTH :]
    column = lax.broadcasted_iota(jnp.int32, (8, WIDTH), 1)
    table_own = jnp.sum(jnp.where(column == e, total[24:], 0.0), axis=1, keepdims=True)
    table_out[...] = table_own[2 : 2 + LOCAL_HEADS]
    for share in shares:
        share.wait_recv()
    summed = small_own[...] + small_landed[0] + small_landed[1] + small_landed[2]
    feature = lax.broadcasted_iota(jnp.int32, (WIDTH, 128), 0)
    lane = lax.broadcasted_iota(jnp.int32, (WIDTH, 128), 1)
    taken = (feature == (e * RING + z) * 6 + lane).astype(f32)
    gains = jnp.dot(summed, taken, precision=highest, preferred_element_type=f32)
    gain_first[...] = gains[0:1, :6]
    gain_second[...] = gains[1:2, :6]

    for share in shares:
        share.wait_send()
    for save in saves:
        save.wait()
    for way in (grads, out_way):
        way.close()
        way.crossed(1)
    grads.crossed(0)
    home_way.close()
    y_way.close()
    unit_ring.close()
    grad_ring.close()
    attn_sum.close()
    input_sum.close()
    sibling.wait_send()
    drain(wall.at[0], s_send)
    drain(plane_landed.at[pl.ds(0, 15)], p_send)


def run_layer(*operands):
    def shape(dims, kind=f32):
        return jax.ShapeDtypeStruct(dims, kind)

    anywhere = pl.BlockSpec(memory_space=pl.ANY)
    rows = (2, EXPERT_ROWS, WIDTH)
    dma = pltpu.SemaphoreType.DMA
    return pl.pallas_call(
        layer_kernel,
        out_shape=[
            shape((128, WIDTH), bf16),
            shape((128, WIDTH)),
            shape((3, 24, HEAD_WIDTH)),
            shape((24, HEAD_WIDTH)),
            shape((1, 6)),
            shape((1, 6)),
            shape((LOCAL_HEADS, 1)),
        ]
        + [shape(rows, bf16)] * 4,
        in_specs=[VMEM] * 6 + [anywhere] * 2 + [VMEM] * 4,
        out_specs=[VMEM] * 7 + [anywhere] * 4,
        scratch_shapes=[
            pltpu.VMEM((SEQ, WIDTH), bf16),
            pltpu.VMEM((WIDTH, WIDTH), bf16),
            pltpu.VMEM((LOCAL_HEADS, SEQ, SEQ), bf16),
            pltpu.VMEM((TOPK, 128, PAD), bf16),
            pltpu.VMEM((128, WIDTH), f32),
            pltpu.VMEM((24, WIDTH), bf16),
            pltpu.VMEM((2, 16, 24, WIDTH), bf16),
            pltpu.VMEM((WIDTH, WIDTH), f32),
        ]
        + [pltpu.VMEM((PAD, WIDTH), bf16), pltpu.VMEM((PAD, WIDTH), bf16), pltpu.VMEM(rows, bf16)] * 2
        + [pltpu.VMEM((2, WIDTH, WIDTH), bf16)] * 2
        + [pltpu.VMEM(rows, bf16)] * 4
        + [
            pltpu.VMEM((SEQ, WIDTH), bf16),
            pltpu.VMEM((2, 16, 32, WIDTH), bf16),
            pltpu.VMEM((16, 32, WIDTH), bf16),
            pltpu.VMEM((16, 32, WIDTH), bf16),
            pltpu.VMEM((8, WIDTH), f32),
            pltpu.VMEM((3, 8, WIDTH), f32),
            dma((2,)),
            dma((4,)),
            dma,
            dma((16,)),
            dma,
            dma,
            dma,
            dma,
            dma,
            dma,
            dma((3,)),
            dma((3,)),
        ]
        + DISPATCH_SCRATCH * 2
        + GATHER_SCRATCH * 2
        + SUM_SCRATCH * 2
        + RETURN_SCRATCH * 2,
        compiler_params=kernel_params(1),
        name="layer",
    )(*operands)


def expert_grad_kernel(rows, grad_pre, hidden, grad_rows, *refs):
    grad_in, grad_out = refs[-2:]
    passed = refs[:-2]
    grad_in[0] = dot_rows(rows[0], grad_pre[0])
    grad_out[0] = dot_rows(hidden[0], grad_rows[0])

    @pl.when((pl.program_id(0) == 0) & (pl.program_id(1) == 0))
    def _():
        for source, target in zip(passed[: len(passed) // 2], passed[len(passed) // 2 :]):
            target[...] = source[...]


def expert_grads(rows, grad_pre, hidden, grad_rows, *small):
    half = WIDTH // 2
    whole_rows = pl.BlockSpec((1, EXPERT_ROWS, WIDTH), lambda j, n: (j, 0, 0))
    half_rows = pl.BlockSpec((1, EXPERT_ROWS, half), lambda j, n: (j, 0, n))

    def still(array):
        return pl.BlockSpec(array.shape, lambda j, n, rank=array.ndim: (0,) * rank)

    grads = jax.ShapeDtypeStruct((2, WIDTH, WIDTH), f32)
    return pl.pallas_call(
        expert_grad_kernel,
        grid=(2, 2),
        out_shape=[jax.ShapeDtypeStruct(a.shape, a.dtype) for a in small] + [grads, grads],
        in_specs=[whole_rows, half_rows, half_rows, whole_rows] + [still(a) for a in small],
        out_specs=[still(a) for a in small]
        + [
            pl.BlockSpec((1, WIDTH, half), lambda j, n: (j, 0, n)),
            pl.BlockSpec((1, half, WIDTH), lambda j, n: (j, n, 0)),
        ],
        compiler_params=pltpu.CompilerParams(vmem_limit_bytes=48 * 1024 * 1024),
        name="expert_grads",
    )(rows, grad_pre, hidden, grad_rows, *small)


def body(
    tokens,
    gain_attn,
    gain_moe,
    qkv_weight,
    proj_weight,
    bias_table,
    expert_in,
    expert_out,
    expert_ids,
    gate_values,
    bucket_table,
    cotangent,
):
    results = run_layer(
        tokens,
        gain_attn.reshape(6, 128),
        gain_moe.reshape(6, 128),
        qkv_weight.transpose(1, 0, 2),
        proj_weight.T,
        bias_table.T,
        expert_in,
        expert_out,
        expert_ids.T,
        gate_values.T,
        bucket_table.reshape(4, 128),
        cotangent,
    )
    rows, hidden, grad_pre, grad_rows = results[7:]
    out, grad_input, qkv_grad, proj_grad, gain_first, gain_second, table, grad_in, grad_out = (
        expert_grads(rows, grad_pre, hidden, grad_rows, *results[:7])
    )
    return (
        out,
        grad_input,
        gain_first[0],
        gain_second[0],
        qkv_grad.transpose(1, 0, 2),
        proj_grad.T,
        table.T,
        grad_in,
        grad_out,
    )


def solution(mesh):
    placed = (
        P(("expert", "mp"), None),
        P(),
        P(),
        P("expert", None, "mp"),
        P("mp", "expert"),
        P(None, "mp"),
        P("expert", None, "mp"),
        P("expert", "mp", None),
        P(("expert", "mp"), None),
        P(("expert", "mp"), None),
        P(),
        P(("expert", "mp"), None),
    )
    return jax.shard_map(
        body,
        mesh=mesh,
        in_specs=placed,
        out_specs=(
            P(("expert", "mp"), None),
            P(("expert", "mp"), None),
            P(("expert", "mp")),
            P(("expert", "mp")),
            P("expert", None, "mp"),
            P("mp", "expert"),
            P("expert", "mp"),
            P("expert", None, "mp"),
            P("expert", "mp", None),
        ),
        check_vma=False,
    )
```

```python
import jax
import jax.numpy as jnp
from jax import lax
from jax.experimental import pallas as pl
from jax.experimental.pallas import tpu as pltpu
from jax.sharding import PartitionSpec as P

HEAD_DIM = 64
TOPK = 2


epsilon = 1e-06
masked_value = -1e30
inv_root_two = 0.7071067811865476
inv_root_tau = 0.3989422804014327
highest = lax.Precision.HIGHEST


MESH = pl.DeviceIdType.MESH
BLOCK = 16
HALF = 80
PLANE = 32
RING = 4
PAD = PLANE * BLOCK
ROWS = 320
EXPERT_ROWS = 640
f32 = jnp.float32
bf16 = jnp.bfloat16


def place():
    e, z = lax.axis_index("expert"), lax.axis_index("mp")
    return e, z, lax.rem(z + 1, RING), lax.rem(z + RING - 1, RING)


def plane_target(e, d):
    step = d // 8
    dy, dx, dc = lax.rem(step * 2, 4) + step // 2, lax.rem(d // 2, 4), lax.rem(d, 2)
    y, x, c = e // 8, lax.rem(e // 2, 4), lax.rem(e, 2)
    return lax.rem(y + dy, 4) * 8 + lax.rem(x + dx, 4) * 2 + lax.rem(c + dc, 2)


def plane_source(e, d):
    step = d // 8
    dy, dx, dc = lax.rem(step * 2, 4) + step // 2, lax.rem(d // 2, 4), lax.rem(d, 2)
    y, x, c = e // 8, lax.rem(e // 2, 4), lax.rem(e, 2)
    return lax.rem(y + 4 - dy, 4) * 8 + lax.rem(x + 4 - dx, 4) * 2 + lax.rem(c + dc, 2)


def block_at(index):
    return pl.ds(pl.multiple_of(index * BLOCK, BLOCK), BLOCK)


def greet(plane, ring, across=0):
    e, z, right, left = place()
    barrier = pltpu.get_barrier_semaphore()
    if plane:

        def signal(d, carry):
            pl.semaphore_signal(
                barrier, inc=1, device_id=(plane_target(e, d), z), device_id_type=MESH
            )
            return carry

        lax.fori_loop(1, PLANE, signal, 0)
    if ring:
        for other in (right, left):
            pl.semaphore_signal(barrier, inc=1, device_id=(e, other), device_id_type=MESH)
    if across:
        other = lax.rem(z + 2, RING)
        pl.semaphore_signal(barrier, inc=1, device_id=(e, other), device_id_type=MESH)
    return (PLANE - 1) * plane + 2 * ring + across


def drain(ref, sem):
    pltpu.make_async_copy(ref, ref, sem).wait()


def dot(left, right):
    return jnp.dot(left, right, preferred_element_type=f32)


def dot_rows(left, right):
    return lax.dot_general(left, right, (((0,), (0,)), ((), ())), preferred_element_type=f32)


def dot_cols(left, right):
    return lax.dot_general(left, right, (((1,), (1,)), ((), ())), preferred_element_type=f32)


def packer():
    row = lax.broadcasted_iota(jnp.int32, (2 * HALF, 256), 0)
    col = lax.broadcasted_iota(jnp.int32, (2 * HALF, 256), 1)
    expert = (row >= HALF).astype(jnp.int32)
    inner = row - expert * HALF
    source = (inner * 205) // 1024
    slot = inner - source * 5
    return (col == source * BLOCK + expert * 5 + slot).astype(bf16)


class Dispatch:
    def __init__(self, send, landed, rows, sems):
        self.send, self.landed, self.rows = send, landed, rows
        self.plane_out, self.plane_in, self.ring_out, self.ring_in = sems

    def part(self, slot, half):
        return self.rows.at[:, pl.ds(slot * 160 + half * HALF, HALF)]

    def one(self, expert, slot, half):
        return self.rows.at[expert, pl.ds(slot * 160 + half * HALF, HALF)]

    def cross(self, half):
        e, z, right, left = place()

        def send(d, carry):
            other = plane_target(e, d)
            pltpu.make_async_remote_copy(
                self.send.at[block_at(other)],
                self.landed.at[block_at(d)],
                self.plane_out.at[half],
                self.plane_in.at[half],
                device_id=(other, z),
                device_id_type=MESH,
            ).start()
            return carry

        lax.fori_loop(max(1, 16 * half), 16 * half + 16, send, 0)
        if half == 0:
            self.landed[0:BLOCK] = self.send[block_at(e)]

    def crossed(self, half):
        drain(self.send.at[pl.ds(0, (15 + half) * BLOCK)], self.plane_out.at[half])

    def copy(self, index, source, target, other):
        e = lax.axis_index("expert")
        return pltpu.make_async_remote_copy(
            source,
            target,
            self.ring_out.at[index],
            self.ring_in.at[index],
            device_id=(e, other),
            device_id_type=MESH,
        )

    def copies(self):
        e, z, right, left = place()
        part = self.part
        return [
            self.copy(0, part(0, 0), part(2, 0), right),
            self.copy(1, part(0, 1), part(2, 1), right),
            self.copy(2, part(0, 0), part(1, 0), left),
            self.copy(3, part(0, 1), part(1, 1), left),
            self.copy(4, self.one(0, 2, 0), self.one(0, 3, 0), right),
            self.copy(5, self.one(1, 1, 0), self.one(1, 3, 0), left),
            self.copy(6, self.one(0, 2, 1), self.one(0, 3, 1), right),
            self.copy(7, self.one(1, 1, 1), self.one(1, 3, 1), left),
        ]

    def turn(self, half, pack):
        lo = 256 * half
        span = self.landed.at[pl.ds(lo + (BLOCK if half == 0 else 0), 256 - (BLOCK if half == 0 else 0))]
        drain(span, self.plane_in.at[half])
        packed = dot(pack, self.landed[lo : lo + 256]).astype(bf16)
        for j in range(2):
            self.rows[j, half * HALF : half * HALF + HALF] = packed[j * HALF : j * HALF + HALF]
        ring = self.copies()
        ring[half].start()
        ring[2 + half].start()

    def relay(self):
        ring = self.copies()
        for near, far in ((0, 4), (2, 5), (1, 6), (3, 7)):
            ring[near].wait_recv()
            ring[far].start()

    def last(self):
        ring = self.copies()
        for far in range(4, 8):
            ring[far].wait_recv()

    def close(self):
        for copy in self.copies():
            copy.wait_send()


DISPATCH_SCRATCH = [
    pltpu.SemaphoreType.DMA((2,)),
    pltpu.SemaphoreType.DMA((2,)),
    pltpu.SemaphoreType.DMA((8,)),
    pltpu.SemaphoreType.DMA((8,)),
]


class Return:
    def __init__(self, partial, relayed, landed, spread, home, sems):
        self.partial, self.relayed, self.landed = partial, relayed, landed
        self.spread, self.home = spread, home
        self.ring_out, self.ring_in, self.plane_out, self.plane_in = sems

    def one(self, expert, slot, half):
        return self.partial.at[expert, pl.ds(slot * 160 + half * HALF, HALF)]

    def copies(self, half):
        e, z, right, left = place()

        def copy(index, source, other):
            index = half * 6 + index
            return pltpu.make_async_remote_copy(
                source,
                self.landed.at[index],
                self.ring_out.at[index],
                self.ring_in.at[index],
                device_id=(e, other),
                device_id_type=MESH,
            )

        one = self.one
        return [
            copy(0, one(0, 3, half), right),
            copy(1, one(1, 3, half), left),
            copy(2, one(1, 1, half), right),
            copy(3, one(0, 2, half), left),
            copy(4, self.relayed.at[half, 0], right),
            copy(5, self.relayed.at[half, 1], left),
        ]

    def near(self, half):
        ring = self.copies(half)
        ring[2].start()
        ring[3].start()

    def far(self, half, index):
        self.copies(half)[index].start()

    def add_far(self, half):
        ring = self.copies(half)
        for index, expert, slot in ((0, 0, 1), (1, 1, 2)):
            ring[index].wait_recv()
            self.relayed[half, index] = (
                self.one(expert, slot, half)[...].astype(f32)
                + self.landed[half * 6 + index].astype(f32)
            ).astype(bf16)
            ring[4 + index].start()

    def finish(self, half, pack):
        e, z, right, left = place()
        ring = self.copies(half)
        total = []
        for expert, direct, summed in ((0, 3, 4), (1, 2, 5)):
            ring[direct].wait_recv()
            ring[summed].wait_recv()
            total.append(
                (
                    self.one(expert, 0, half)[...].astype(f32)
                    + self.landed[half * 6 + direct].astype(f32)
                    + self.landed[half * 6 + summed].astype(f32)
                ).astype(bf16)
            )
        flat = jnp.concatenate([total[0], total[1]], axis=0)
        self.spread[256 * half : 256 * half + 256] = dot_rows(pack, flat).astype(bf16)

        def send(d, carry):
            pltpu.make_async_remote_copy(
                self.spread.at[block_at(d)],
                self.home.at[block_at(e)],
                self.plane_out,
                self.plane_in,
                device_id=(plane_source(e, d), z),
                device_id_type=MESH,
            ).start()
            return carry

        lax.fori_loop(max(1, 16 * half), 16 * half + 16, send, 0)
        if half == 0:
            self.home[block_at(e)] = self.spread[0:BLOCK]

    def arrive(self):
        drain(self.home.at[pl.ds(0, (PLANE - 1) * BLOCK)], self.plane_in)

    def close(self):
        for copy in self.copies(0) + self.copies(1):
            copy.wait_send()
        drain(self.spread.at[pl.ds(0, (PLANE - 1) * BLOCK)], self.plane_out)


RETURN_SCRATCH = [
    pltpu.VMEM((2, 2, HALF, 768), bf16),
    pltpu.VMEM((12, HALF, 768), bf16),
    pltpu.VMEM((PAD, 768), bf16),
    pltpu.VMEM((PAD, 768), bf16),
    pltpu.SemaphoreType.DMA((12,)),
    pltpu.SemaphoreType.DMA((12,)),
    pltpu.SemaphoreType.DMA,
    pltpu.SemaphoreType.DMA,
]


def kernel_params(collective_id):
    return pltpu.CompilerParams(
        collective_id=collective_id, has_side_effects=True, vmem_limit_bytes=60 * 1024 * 1024
    )


VMEM = pl.BlockSpec(memory_space=pltpu.VMEM)


SEQ = 512
SIDE = 64
WIDTH = 768
HEAD_WIDTH = 192
LOCAL_HEADS = 3
score_scale = HEAD_DIM ** (-0.5)


class RingGather:
    def __init__(self, rows, sems):
        self.rows = rows
        self.out, self.arrived = sems

    def copies(self):
        e, z, right, left = place()

        def copy(index, owner, half, other):
            block = self.rows.at[pl.ds(pl.multiple_of(owner * 128 + half * SIDE, SIDE), SIDE)]
            return pltpu.make_async_remote_copy(
                block,
                block,
                self.out.at[index],
                self.arrived.at[index],
                device_id=(e, other),
                device_id_type=MESH,
            )

        def landing(index, owner, half):
            block = self.rows.at[pl.ds(pl.multiple_of(owner * 128 + half * SIDE, SIDE), SIDE)]
            return pltpu.make_async_copy(block, block, self.arrived.at[index])

        far = lax.rem(z + 2, RING)
        sends = [
            copy(0, z, 0, right),
            copy(1, z, 1, right),
            copy(2, z, 0, left),
            copy(3, z, 1, left),
            copy(4, left, 0, right),
            copy(5, right, 1, left),
        ]
        lands = [
            landing(0, left, 0),
            landing(1, left, 1),
            landing(2, right, 0),
            landing(3, right, 1),
            landing(4, far, 0),
            landing(5, far, 1),
        ]
        return sends, lands

    def start(self):
        sends, lands = self.copies()
        for index in (0, 3, 1, 2):
            sends[index].start()

    def relay(self):
        sends, lands = self.copies()
        lands[0].wait()
        sends[4].start()
        lands[3].wait()
        sends[5].start()

    def land(self, index):
        sends, lands = self.copies()
        lands[index].wait()

    def finish(self):
        self.relay()
        for index in (1, 2, 4, 5):
            self.land(index)

    def close(self):
        sends, lands = self.copies()
        for send in sends:
            send.wait_send()


GATHER_SCRATCH = [pltpu.SemaphoreType.DMA((6,)), pltpu.SemaphoreType.DMA((6,))]


class RingSum:
    def __init__(self, partial, relayed, landed, sems):
        self.partial, self.relayed, self.landed = partial, relayed, landed
        self.out, self.arrived = sems

    def part(self, slot, half):
        e, z, right, left = place()
        owner = (z, right, left, lax.rem(z + 2, RING))[slot]
        return self.partial.at[pl.ds(pl.multiple_of(owner * 128 + half * SIDE, SIDE), SIDE)]

    def copies(self):
        e, z, right, left = place()

        def copy(index, source, other):
            return pltpu.make_async_remote_copy(
                source,
                self.landed.at[index],
                self.out.at[index],
                self.arrived.at[index],
                device_id=(e, other),
                device_id_type=MESH,
            )

        part = self.part
        return [
            copy(0, part(3, 0), right),
            copy(1, part(3, 1), left),
            copy(2, part(1, 1), right),
            copy(3, part(2, 0), left),
            copy(4, self.relayed.at[0], right),
            copy(5, self.relayed.at[1], left),
        ]

    def send(self, index):
        self.copies()[index].start()

    def add_far(self):
        ring = self.copies()
        for index, slot, half in ((0, 1, 0), (1, 2, 1)):
            ring[index].wait_recv()
            self.relayed[index] = (
                self.part(slot, half)[...].astype(f32) + self.landed[index].astype(f32)
            ).astype(bf16)
            ring[4 + index].start()

    def total(self):
        ring = self.copies()
        halves = []
        for half, direct, summed in ((0, 3, 4), (1, 2, 5)):
            ring[direct].wait_recv()
            ring[summed].wait_recv()
            halves.append(
                self.part(0, half)[...].astype(f32)
                + self.landed[direct].astype(f32)
                + self.landed[summed].astype(f32)
            )
        return jnp.concatenate(halves, axis=0)

    def close(self):
        for copy in self.copies():
            copy.wait_send()


SUM_SCRATCH = [
    pltpu.VMEM((SEQ, WIDTH), bf16),
    pltpu.VMEM((2, SIDE, WIDTH), bf16),
    pltpu.VMEM((6, SIDE, WIDTH), bf16),
    pltpu.SemaphoreType.DMA((6,)),
    pltpu.SemaphoreType.DMA((6,)),
]


def head_mask(h):
    lane = lax.broadcasted_iota(jnp.int32, (1, HEAD_WIDTH), 1)
    return (lane >= h * HEAD_DIM) & (lane < (h + 1) * HEAD_DIM)


def sum_diagonals(square):
    rows = square
    for step in (32, 8, 1):
        count = rows.shape[0] // step
        rows = sum(
            pltpu.roll(rows[a * step : a * step + step], (SEQ - a * step) % SEQ, 1)
            if a
            else rows[:step]
            for a in range(count)
        )
    return rows


def bucket_hot_rows(bucket_rev):
    return (bucket_rev == lax.broadcasted_iota(jnp.int32, (32, SEQ), 0)).astype(f32)


def plane_sends(source_at, target_at, send_sem, recv_sem_at):
    e, z, right, left = place()

    def send(chip, carry):
        other = plane_target(e, chip * 2)
        pltpu.make_async_remote_copy(
            source_at(other // 2),
            target_at(e // 2),
            send_sem,
            recv_sem_at(e // 2),
            device_id=(other, z),
            device_id_type=MESH,
        ).start()
        return carry

    lax.fori_loop(1, 16, send, 0)


def rms_scale(values):
    return lax.rsqrt(jnp.mean(values * values, axis=1, keepdims=True) + epsilon)


def select_rows(ids):
    expert = lax.broadcasted_iota(jnp.int32, (128, 64), 1)
    hot = [(ids[:, c : c + 1] == expert).astype(f32) for c in range(TOPK)]
    row = lax.broadcasted_iota(jnp.int32, (128, 128), 0)
    col = lax.broadcasted_iota(jnp.int32, (128, 128), 1)
    before = dot((col < row).astype(bf16), (hot[0] + hot[1]).astype(bf16))
    pos = lax.broadcasted_iota(jnp.int32, (128, PAD), 1)
    picks = []
    for c in range(TOPK):
        slot = jnp.sum(before * hot[c], axis=1, keepdims=True).astype(jnp.int32)
        own = ids[:, c : c + 1]
        first = own // 2
        picks.append((pos == first * BLOCK + (own - first * 2) * 5 + slot).astype(bf16))
    return picks


def as_column(row):
    n = row.shape[1]
    same = lax.broadcasted_iota(jnp.int32, (n, n), 0) == lax.broadcasted_iota(jnp.int32, (n, n), 1)
    return jnp.sum(jnp.where(same, row, 0.0), axis=1, keepdims=True)


def as_row(rows):
    return jnp.concatenate([rows[i : i + 1] for i in range(rows.shape[0])], axis=1)


def layer_kernel(
    tokens, gain_attn, gain_moe, qkv_weight, proj_weight, bias, weight_in, weight_out,
    ids, gates, buckets, cotangent,
    out, grad_input, qkv_grad, proj_grad, gain_first, gain_second, table_out,
    grads_hbm,
    units, whole, qkv, attended, probs, picked, resid, mine, wall, whole32,
    x_send, x_landed, x_rows, g_send, g_landed, g_rows,
    held_in, held_out, hidden, grad_pre, grad_part, y_part, expert_grads,
    seq_grad, grad_qkv, blocks, near_blocks, plane_landed, small_own, small_landed, small_sum, small_plane,
    load_sems, save_sems, w_send, w_recv, s_send, s_recv, v_send, v_recv,
    p_send, p_recv, t_send, t_recv, q_send, q_recv, *rest,
):
    x_sems, g_sems, rest = rest[:4], rest[4:8], rest[8:]
    unit_sems, grad_sems, rest = rest[:2], rest[2:4], rest[4:]
    sum_a, sum_b, rest = rest[:5], rest[5:10], rest[10:]
    back_x, back_y = rest[:8], rest[8:]
    e, z, right, left = place()
    core, chip = lax.rem(e, 2), e // 2
    twin = chip * 2 + 1 - core
    opposite = lax.rem(z + 2, RING)
    loads = [
        pltpu.make_async_copy(weight_in, held_in, load_sems.at[0]),
        pltpu.make_async_copy(weight_out, held_out, load_sems.at[1]),
    ]
    for load in loads:
        load.start()
    arrivals = greet(1, 1, 1)

    mine[...] = jnp.concatenate(
        [qkv_weight[i].astype(f32) for i in range(3)] + [proj_weight[...].astype(f32)], axis=1
    ).astype(bf16)
    inputs = tokens[...].astype(f32)
    own_rows = pl.ds(pl.multiple_of(z * 128, 128), 128)
    units[own_rows] = (inputs * rms_scale(inputs)).astype(bf16)
    pl.semaphore_wait(pltpu.get_barrier_semaphore(), arrivals)
    plane_sends(lambda other: mine, lambda own: wall.at[core, own], w_send, w_recv.at.__getitem__)
    unit_ring = RingGather(units, unit_sems)
    unit_ring.start()
    wall[core, chip] = mine[...]

    def pass_on(source):
        return pltpu.make_async_remote_copy(
            wall.at[core, source],
            wall.at[core, source],
            s_send,
            s_recv,
            device_id=(twin, z),
            device_id_type=MESH,
        )

    pass_on(chip).start()
    gain_a, gain_m = as_row(gain_attn[...]), as_row(gain_moe[...])
    id_columns = jnp.concatenate(
        [as_column(ids[c : c + 1].astype(f32)) for c in range(TOPK)], axis=1
    ).astype(jnp.int32)
    gate_columns = [as_column(gates[c : c + 1]) for c in range(TOPK)]
    picks = select_rows(id_columns)
    for c in range(TOPK):
        picked[c] = picks[c]
    grad_out = cotangent[...].astype(f32)
    g_send[...] = (
        dot_rows(picks[0], (gate_columns[0] * grad_out).astype(bf16))
        + dot_rows(picks[1], (gate_columns[1] * grad_out).astype(bf16))
    ).astype(bf16)
    grads = Dispatch(g_send, g_landed, g_rows, g_sems)
    unit_ring.relay()
    far_row = lax.broadcasted_iota(jnp.int32, (SEQ, SEQ), 0)
    far_col = lax.broadcasted_iota(jnp.int32, (SEQ, SEQ), 1)
    mirror = (far_row + far_col == jnp.where(far_col == 0, 0, SEQ)).astype(bf16)
    hot = dot(bucket_hot_rows(as_row(buckets[...])).astype(bf16), mirror)
    rels = [
        jnp.sum(as_column(bias[h : h + 1]) * hot, axis=0, keepdims=True)
        for h in range(LOCAL_HEADS)
    ]
    pack = packer()

    def forward(step, carry):
        source = plane_source(e, step * 2) // 2
        pltpu.make_async_copy(wall.at[core, source], wall.at[core, source], w_recv.at[source]).wait()
        pass_on(source).start()
        return carry

    lax.fori_loop(1, 16, forward, 0)
    for index in (1, 2, 4, 5):
        unit_ring.land(index)
    drain(wall.at[0, pl.ds(0, 15)], w_send)
    grads.cross(0)
    grads.cross(1)
    unit_rows = units[...].astype(f32)
    normed = (unit_rows * gain_a).astype(bf16)
    drain(wall.at[1 - core], s_recv)
    for block in range(PLANE):
        whole32[24 * block : 24 * block + 24] = wall[block % 2, block // 2].astype(f32)
    whole[...] = whole32[...].astype(bf16)

    qkv[...] = dot(normed, whole[:, :640]).astype(bf16)[:, : 3 * HEAD_WIDTH]
    keys = qkv[:, HEAD_WIDTH : 2 * HEAD_WIDTH]
    values = qkv[:, 2 * HEAD_WIDTH :]
    proj = whole[:, 3 * HEAD_WIDTH :]
    attn_sum = RingSum(sum_a[0], sum_a[1], sum_a[2], sum_a[3:])
    owners = (z, right, left, opposite)
    query_row = lax.broadcasted_iota(jnp.int32, (128, SEQ), 0)
    key_col = lax.broadcasted_iota(jnp.int32, (128, SEQ), 1)

    def rows_of(slot):
        return pl.ds(pl.multiple_of(owners[slot] * 128, 128), 128)

    def attend(slot):
        rows = rows_of(slot)
        first = owners[slot] * 128
        queries = qkv[rows, :HEAD_WIDTH]
        mixed = jnp.zeros((128, HEAD_WIDTH), f32)
        for h in range(LOCAL_HEADS):
            mask = head_mask(h)
            turned = pltpu.roll(rels[h], first, 1)
            shifted = pltpu.roll(
                jnp.broadcast_to(turned, (128, SEQ)), 0, 1, stride=1, stride_axis=0
            )
            scores = dot_cols(jnp.where(mask, queries, jnp.zeros_like(queries)), keys) * score_scale
            scores = jnp.where(key_col <= query_row + first, scores + shifted, masked_value)
            raised = jnp.exp(scores - jnp.max(scores, axis=1, keepdims=True))
            weights_p = (raised / jnp.sum(raised, axis=1, keepdims=True)).astype(bf16)
            probs[h, rows] = weights_p
            mixed = jnp.where(mask, dot(weights_p, values), mixed)
        mixed = mixed.astype(bf16)
        attended[rows] = mixed
        sum_a[0][rows] = dot_cols(mixed, proj).astype(bf16)

    attend(3)
    attn_sum.send(0)
    attn_sum.send(1)
    attend(1)
    attn_sum.send(2)
    attend(2)
    attn_sum.send(3)
    attend(0)
    attn_sum.add_far()
    grads.turn(0, pack)
    grads.turn(1, pack)
    residual = inputs + attn_sum.total()
    resid[...] = residual
    scale_m = rms_scale(residual)
    normal_m = residual * scale_m
    x_send[...] = dot_rows(picks[0] + picks[1], (normal_m * gain_m).astype(bf16)).astype(bf16)

    out_way = Dispatch(x_send, x_landed, x_rows, x_sems)
    home_way = Return(grad_part, back_x[0], back_x[1], back_x[2], back_x[3], back_x[4:])
    out_way.cross(0)
    out_way.crossed(0)
    out_way.cross(1)
    out_way.turn(0, pack)
    out_way.turn(1, pack)
    for load in loads:
        load.wait()

    def run(first, count, experts=(0, 1)):
        for j in experts:
            span = pl.ds(first * 160, count * 160)
            pre_act = dot(x_rows[j, span], held_in[j])
            cdf = 0.5 * (1.0 + lax.erf(pre_act * inv_root_two))
            hidden[j, span] = (pre_act * cdf).astype(bf16)
            slope = cdf + pre_act * jnp.exp(-0.5 * pre_act * pre_act) * inv_root_tau
            grad_hidden = dot_cols(g_rows[j, span], held_out[j])
            grad_pre[j, span] = (grad_hidden * slope).astype(bf16)
            grad_part[j, span] = dot_cols(grad_pre[j, span], held_in[j]).astype(bf16)

    run(0, 1)
    grads.relay()
    out_way.relay()
    run(1, 2)
    home_way.near(0)
    home_way.near(1)
    grads.last()
    out_way.last()
    for j in range(2):
        run(3, 1, (j,))
        home_way.far(0, j)
        home_way.far(1, j)
    y_way = Return(y_part, back_y[0], back_y[1], back_y[2], back_y[3], back_y[4:])
    for j in range(2):
        y_part[j] = dot(hidden[j], held_out[j]).astype(bf16)
    home_way.add_far(0)
    home_way.add_far(1)
    for half in range(2):
        y_way.far(half, 0)
        y_way.far(half, 1)
        y_way.near(half)
    home_way.finish(0, pack)
    home_way.finish(1, pack)
    saves = []
    for j in range(2):
        expert_grads[j] = dot_rows(x_rows[j], grad_pre[j]).astype(bf16)
        expert_grads[2 + j] = dot_rows(hidden[j], g_rows[j]).astype(bf16)
        y_way.add_far(j)
    for index in range(4):
        saves.append(
            pltpu.make_async_copy(expert_grads.at[index], grads_hbm.at[index], save_sems.at[index])
        )
        saves[index].start()
    home_way.arrive()
    grad_normed = dot(picked[0] + picked[1], home_way.home[...])
    gain_m_part = jnp.sum(grad_normed * normal_m, axis=0, keepdims=True)
    grad_unit_m = grad_normed * gain_m
    grad_resid = grad_out + scale_m * (
        grad_unit_m - normal_m * jnp.mean(grad_unit_m * normal_m, axis=1, keepdims=True)
    )

    seq_grad[own_rows] = grad_resid.astype(bf16)
    grad_ring = RingGather(seq_grad, grad_sems)
    grad_ring.start()
    zeros = jnp.zeros((SEQ, HEAD_WIDTH), f32)
    carried = [zeros, zeros, jnp.zeros((WIDTH, HEAD_WIDTH), f32)]
    diagonals = [jnp.zeros((1, SEQ), f32)] * LOCAL_HEADS

    def attend_back(slot):
        rows = rows_of(slot)
        queries = qkv[rows, :HEAD_WIDTH]
        grad_rows = seq_grad[rows]
        grad_att = dot(grad_rows, proj).astype(bf16)
        carried[2] = carried[2] + dot_rows(grad_rows, attended[rows])
        grad_q = jnp.zeros((128, HEAD_WIDTH), f32)
        for h in range(LOCAL_HEADS):
            mask = head_mask(h)
            weights_p = probs[h, rows]
            soft = weights_p.astype(f32)
            own_att = jnp.where(mask, grad_att, jnp.zeros_like(grad_att))
            own_queries = jnp.where(mask, queries, jnp.zeros_like(queries))
            grad_w = dot_cols(own_att, values)
            row_dot = jnp.sum(soft * grad_w, axis=1, keepdims=True)
            grad_scores = (soft * (grad_w - row_dot)).astype(bf16)
            turn = lax.rem(SEQ - owners[slot] * 128, SEQ)
            diagonals[h] = diagonals[h] + pltpu.roll(
                sum_diagonals(grad_scores.astype(f32)), turn, 1
            )
            grad_q = jnp.where(mask, dot(grad_scores, keys), grad_q)
            carried[0] = carried[0] + dot_rows(grad_scores, own_queries)
            carried[1] = carried[1] + dot_rows(weights_p, own_att)
        grad_qkv[rows, :HEAD_WIDTH] = (grad_q * score_scale).astype(bf16)

    attend_back(0)
    grad_ring.relay()
    grad_ring.land(2)
    attend_back(1)
    y_way.finish(0, pack)
    grad_ring.land(1)
    attend_back(2)
    y_way.finish(1, pack)
    grad_ring.land(4)
    grad_ring.land(5)
    attend_back(3)
    grad_qkv[:, HEAD_WIDTH:] = jnp.concatenate(
        [carried[0] * score_scale, carried[1]], axis=1
    ).astype(bf16)
    proj_part = carried[2]
    full = jnp.concatenate([dot_rows(normed, grad_qkv[...]), proj_part], axis=1)
    for block in range(PLANE):
        blocks[block % 2, block // 2] = full[24 * block : 24 * block + 24].astype(bf16)
    sibling = pltpu.make_async_remote_copy(
        blocks.at[1 - core],
        near_blocks,
        v_send,
        v_recv,
        device_id=(twin, z),
        device_id_type=MESH,
    )
    sibling.start()
    grad_normed_a = dot_cols(grad_qkv[...], whole[:, : 3 * HEAD_WIDTH])
    sum_b[0][...] = grad_normed_a.astype(bf16)
    input_sum = RingSum(sum_b[0], sum_b[1], sum_b[2], sum_b[3:])
    for index in range(4):
        input_sum.send(index)
    gain_part = jnp.sum(grad_normed_a * unit_rows, axis=0, keepdims=True)
    diagonal = jnp.concatenate(diagonals + [jnp.zeros((5, SEQ), f32)], axis=0)
    table_rows = lax.dot_general(
        diagonal, hot, (((1,), (1,)), ((), ())), precision=highest, preferred_element_type=f32
    )
    pieces = [
        part[:, 128 * i : 128 * i + 128] for part in (gain_part, gain_m_part) for i in range(6)
    ]
    small_own[...] = jnp.concatenate(
        pieces + [jnp.zeros((4, 128), f32)], axis=0
    )
    small_own[12 : 12 + LOCAL_HEADS, :32] = table_rows[:LOCAL_HEADS]
    shares = [
        pltpu.make_async_remote_copy(
            small_own,
            small_landed.at[index],
            t_send.at[index],
            t_recv.at[index],
            device_id=(e, other),
            device_id_type=MESH,
        )
        for index, other in enumerate((right, left, opposite))
    ]
    for share in shares:
        share.start()
    input_sum.add_far()
    sibling.wait_recv()
    near_blocks[...] = (blocks[core].astype(f32) + near_blocks[...].astype(f32)).astype(bf16)
    plane_sends(
        lambda other: near_blocks.at[other],
        lambda own: plane_landed.at[own],
        p_send,
        lambda own: p_recv,
    )
    plane_landed[chip] = near_blocks[chip]
    for share in shares:
        share.wait_recv()
    own_small = small_own[...]
    line = lax.broadcasted_iota(jnp.int32, (16, 128), 0)
    small_sum[...] = jnp.where(
        line < 12, own_small + small_landed[0] + small_landed[1] + small_landed[2], own_small
    )

    def spread_small(d, carry):
        pltpu.make_async_remote_copy(
            small_sum,
            small_plane.at[d],
            q_send,
            q_recv,
            device_id=(plane_target(e, d), z),
            device_id_type=MESH,
        ).start()
        return carry

    lax.fori_loop(1, PLANE, spread_small, 0)
    small_plane[0] = small_sum[...]
    y_way.arrive()
    home = y_way.home[...]
    out[...] = (
        resid[...] + gate_columns[0] * dot(picked[0], home) + gate_columns[1] * dot(picked[1], home)
    ).astype(bf16)
    scale_first = rms_scale(inputs)
    normal_first = inputs * scale_first
    grad_unit = input_sum.total() * gain_a
    grad_input[...] = grad_resid + scale_first * (
        grad_unit - normal_first * jnp.mean(grad_unit * normal_first, axis=1, keepdims=True)
    )
    drain(plane_landed.at[pl.ds(0, 15)], p_recv)
    total = plane_landed[0].astype(f32)
    for block in range(1, 16):
        total = total + plane_landed[block].astype(f32)
    for i in range(3):
        qkv_grad[i] = total[:, i * HEAD_WIDTH : (i + 1) * HEAD_WIDTH]
    proj_grad[...] = total[:, 3 * HEAD_WIDTH :]
    drain(small_plane.at[pl.ds(1, PLANE - 1)], q_recv)
    summed = jnp.sum(small_plane[...], axis=0)
    column = lax.broadcasted_iota(jnp.int32, (16, 128), 1)
    table_own = jnp.sum(jnp.where(column == e, summed, 0.0), axis=1, keepdims=True)
    table_out[...] = jnp.concatenate(
        [table_own[12 + h : 13 + h] for h in range(LOCAL_HEADS)], axis=1
    )
    wide = jnp.concatenate([as_row(summed[0:6]), as_row(summed[6:12])], axis=0)
    wide = jnp.concatenate([wide, jnp.zeros((6, WIDTH), f32)], axis=0)
    feature = lax.broadcasted_iota(jnp.int32, (WIDTH, 128), 0)
    lane = lax.broadcasted_iota(jnp.int32, (WIDTH, 128), 1)
    taken = (feature == (e * RING + z) * 6 + lane).astype(f32)
    gains = jnp.dot(wide, taken, precision=highest, preferred_element_type=f32)
    gain_first[...] = gains[0:1, :6]
    gain_second[...] = gains[1:2, :6]

    drain(small_plane.at[pl.ds(1, PLANE - 1)], q_send)
    for share in shares:
        share.wait_send()
    for save in saves:
        save.wait()
    for way in (grads, out_way):
        way.close()
        way.crossed(1)
    grads.crossed(0)
    home_way.close()
    y_way.close()
    unit_ring.close()
    grad_ring.close()
    attn_sum.close()
    input_sum.close()
    sibling.wait_send()
    drain(wall.at[0], s_send)
    drain(plane_landed.at[pl.ds(0, 15)], p_send)


def run_layer(*operands):
    def shape(dims, kind=f32):
        return jax.ShapeDtypeStruct(dims, kind)

    anywhere = pl.BlockSpec(memory_space=pl.ANY)
    rows = (2, EXPERT_ROWS, WIDTH)
    dma = pltpu.SemaphoreType.DMA
    return pl.pallas_call(
        layer_kernel,
        out_shape=[
            shape((128, WIDTH), bf16),
            shape((128, WIDTH)),
            shape((3, 24, HEAD_WIDTH)),
            shape((24, HEAD_WIDTH)),
            shape((1, 6)),
            shape((1, 6)),
            shape((1, LOCAL_HEADS)),
        ]
        + [shape((4, WIDTH, WIDTH), bf16)],
        in_specs=[VMEM] * 6 + [anywhere] * 2 + [VMEM] * 4,
        out_specs=[VMEM] * 7 + [anywhere],
        scratch_shapes=[
            pltpu.VMEM((SEQ, WIDTH), bf16),
            pltpu.VMEM((WIDTH, WIDTH), bf16),
            pltpu.VMEM((SEQ, 3 * HEAD_WIDTH), bf16),
            pltpu.VMEM((SEQ, HEAD_WIDTH), bf16),
            pltpu.VMEM((LOCAL_HEADS, SEQ, SEQ), bf16),
            pltpu.VMEM((TOPK, 128, PAD), bf16),
            pltpu.VMEM((128, WIDTH), f32),
            pltpu.VMEM((24, WIDTH), bf16),
            pltpu.VMEM((2, 16, 24, WIDTH), bf16),
            pltpu.VMEM((WIDTH, WIDTH), f32),
        ]
        + [pltpu.VMEM((PAD, WIDTH), bf16), pltpu.VMEM((PAD, WIDTH), bf16), pltpu.VMEM(rows, bf16)] * 2
        + [pltpu.VMEM((2, WIDTH, WIDTH), bf16)] * 2
        + [pltpu.VMEM(rows, bf16)] * 4
        + [
            pltpu.VMEM((4, WIDTH, WIDTH), bf16),
            pltpu.VMEM((SEQ, WIDTH), bf16),
            pltpu.VMEM((SEQ, 3 * HEAD_WIDTH), bf16),
            pltpu.VMEM((2, 16, 24, WIDTH), bf16),
            pltpu.VMEM((16, 24, WIDTH), bf16),
            pltpu.VMEM((16, 24, WIDTH), bf16),
            pltpu.VMEM((16, 128), f32),
            pltpu.VMEM((3, 16, 128), f32),
            pltpu.VMEM((16, 128), f32),
            pltpu.VMEM((PLANE, 16, 128), f32),
            dma((2,)),
            dma((4,)),
            dma,
            dma((16,)),
            dma,
            dma,
            dma,
            dma,
            dma,
            dma,
            dma((3,)),
            dma((3,)),
            dma,
            dma,
        ]
        + DISPATCH_SCRATCH * 2
        + GATHER_SCRATCH * 2
        + SUM_SCRATCH * 2
        + RETURN_SCRATCH * 2,
        compiler_params=kernel_params(1),
        name="layer",
    )(*operands)


def widen_kernel(narrow, *refs):
    small = (len(refs) - 6) // 2
    passed, results = refs[:small], refs[small : 2 * small]
    wide_in, wide_out, held, wide, loads, saves = refs[2 * small :]
    reads = [
        pltpu.make_async_copy(narrow.at[i], held.at[i], loads.at[i]) for i in range(4)
    ]
    for read in reads:
        read.start()
    for source, target in zip(passed, results):
        target[...] = source[...]
    writes = []
    for i in range(4):
        reads[i].wait()
        wide[i] = held[i].astype(f32)
        target = (wide_in, wide_out)[i // 2].at[i % 2]
        writes.append(pltpu.make_async_copy(wide.at[i], target, saves.at[i]))
        writes[i].start()
    for write in writes:
        write.wait()


def widen(narrow, *small):
    anywhere = pl.BlockSpec(memory_space=pl.ANY)
    grads = jax.ShapeDtypeStruct((2, WIDTH, WIDTH), f32)
    return pl.pallas_call(
        widen_kernel,
        out_shape=[jax.ShapeDtypeStruct(a.shape, a.dtype) for a in small] + [grads, grads],
        in_specs=[anywhere] + [VMEM] * len(small),
        out_specs=[VMEM] * len(small) + [anywhere] * 2,
        scratch_shapes=[
            pltpu.VMEM((4, WIDTH, WIDTH), bf16),
            pltpu.VMEM((4, WIDTH, WIDTH), f32),
            pltpu.SemaphoreType.DMA((4,)),
            pltpu.SemaphoreType.DMA((4,)),
        ],
        compiler_params=pltpu.CompilerParams(vmem_limit_bytes=60 * 1024 * 1024),
        name="widen",
    )(narrow, *small)


def body(
    tokens,
    gain_attn,
    gain_moe,
    qkv_weight,
    proj_weight,
    bias_table,
    expert_in,
    expert_out,
    expert_ids,
    gate_values,
    bucket_table,
    cotangent,
):
    results = run_layer(
        tokens,
        gain_attn.reshape(6, 128),
        gain_moe.reshape(6, 128),
        qkv_weight.transpose(1, 0, 2),
        proj_weight.T,
        bias_table.T,
        expert_in,
        expert_out,
        expert_ids.T,
        gate_values.T,
        bucket_table.reshape(4, 128),
        cotangent,
    )
    out, grad_input, qkv_grad, proj_grad, gain_first, gain_second, table, grad_in, grad_out = widen(
        results[7], *results[:7]
    )
    return (
        out,
        grad_input,
        gain_first[0],
        gain_second[0],
        qkv_grad.transpose(1, 0, 2),
        proj_grad.T,
        table,
        grad_in,
        grad_out,
    )


def solution(mesh):
    placed = (
        P(("expert", "mp"), None),
        P(),
        P(),
        P("expert", None, "mp"),
        P("mp", "expert"),
        P(None, "mp"),
        P("expert", None, "mp"),
        P("expert", "mp", None),
        P(("expert", "mp"), None),
        P(("expert", "mp"), None),
        P(),
        P(("expert", "mp"), None),
    )
    return jax.shard_map(
        body,
        mesh=mesh,
        in_specs=placed,
        out_specs=(
            P(("expert", "mp"), None),
            P(("expert", "mp"), None),
            P(("expert", "mp")),
            P(("expert", "mp")),
            P("expert", None, "mp"),
            P("mp", "expert"),
            P("expert", "mp"),
            P("expert", None, "mp"),
            P("expert", "mp", None),
        ),
        check_vma=False,
    )
```

```python
import jax
import jax.numpy as jnp
from jax import lax
from jax.experimental import pallas as pl
from jax.experimental.pallas import tpu as pltpu
from jax.sharding import PartitionSpec as P

HEAD_DIM = 64
TOPK = 2


epsilon = 1e-06
masked_value = -1e30
inv_root_two = 0.7071067811865476
inv_root_tau = 0.3989422804014327
highest = lax.Precision.HIGHEST


MESH = pl.DeviceIdType.MESH
BLOCK = 24
NARROW = 384
HALF = 80
PLANE = 32
RING = 4
PAD = PLANE * BLOCK
BLOCKS = (PLANE, BLOCK, NARROW)
ROWS = 320
EXPERT_ROWS = 640
f32 = jnp.float32
bf16 = jnp.bfloat16


def place():
    e, z = lax.axis_index("expert"), lax.axis_index("mp")
    return e, z, lax.rem(z + 1, RING), lax.rem(z + RING - 1, RING)


def plane_target(e, d):
    step = d // 8
    dy, dx, dc = lax.rem(step * 2, 4) + step // 2, lax.rem(d // 2, 4), lax.rem(d, 2)
    y, x, c = e // 8, lax.rem(e // 2, 4), lax.rem(e, 2)
    return lax.rem(y + dy, 4) * 8 + lax.rem(x + dx, 4) * 2 + lax.rem(c + dc, 2)


def plane_source(e, d):
    step = d // 8
    dy, dx, dc = lax.rem(step * 2, 4) + step // 2, lax.rem(d // 2, 4), lax.rem(d, 2)
    y, x, c = e // 8, lax.rem(e // 2, 4), lax.rem(e, 2)
    return lax.rem(y + 4 - dy, 4) * 8 + lax.rem(x + 4 - dx, 4) * 2 + lax.rem(c + dc, 2)


def fold(rows):
    return jnp.concatenate([rows[:, :NARROW], rows[:, NARROW:]], axis=0)


def unfold(rows):
    half = rows.shape[0] // 2
    return jnp.concatenate([rows[:half], rows[half:]], axis=1)


def as_blocks(rows):
    return rows.reshape(rows.shape[0] // BLOCK, BLOCK, NARROW).astype(bf16)


def from_blocks(blocks):
    return blocks.astype(f32).reshape(blocks.shape[0] * BLOCK, NARROW).astype(bf16)


def greet(plane, ring, across=0):
    e, z, right, left = place()
    barrier = pltpu.get_barrier_semaphore()
    if plane:

        def signal(d, carry):
            pl.semaphore_signal(
                barrier, inc=1, device_id=(plane_target(e, d), z), device_id_type=MESH
            )
            return carry

        lax.fori_loop(1, PLANE, signal, 0)
    if ring:
        for other in (right, left):
            pl.semaphore_signal(barrier, inc=1, device_id=(e, other), device_id_type=MESH)
    if across:
        other = lax.rem(z + 2, RING)
        pl.semaphore_signal(barrier, inc=1, device_id=(e, other), device_id_type=MESH)
    return (PLANE - 1) * plane + 2 * ring + across


def drain(ref, sem):
    pltpu.make_async_copy(ref, ref, sem).wait()


def dot(left, right):
    return jnp.dot(left, right, preferred_element_type=f32)


def dot_rows(left, right):
    return lax.dot_general(left, right, (((0,), (0,)), ((), ())), preferred_element_type=f32)


def dot_cols(left, right):
    return lax.dot_general(left, right, (((1,), (1,)), ((), ())), preferred_element_type=f32)


def packer():
    row = lax.broadcasted_iota(jnp.int32, (4 * HALF, 16 * BLOCK), 0)
    col = lax.broadcasted_iota(jnp.int32, (4 * HALF, 16 * BLOCK), 1)
    side = (row >= 2 * HALF).astype(jnp.int32)
    rest = row - side * 2 * HALF
    expert = (rest >= HALF).astype(jnp.int32)
    inner = rest - expert * HALF
    source = (inner * 205) // 1024
    slot = inner - source * 5
    return (col == source * BLOCK + side * 10 + expert * 5 + slot).astype(bf16)


class Dispatch:
    def __init__(self, send, landed, rows, sems):
        self.send, self.landed, self.rows = send, landed, rows
        self.plane_out, self.plane_in, self.ring_out, self.ring_in = sems

    def part(self, slot, half):
        return self.rows.at[:, pl.ds(slot * 160 + half * HALF, HALF)]

    def one(self, expert, slot, half):
        return self.rows.at[expert, pl.ds(slot * 160 + half * HALF, HALF)]

    def cross(self, half):
        e, z, right, left = place()

        def send(d, carry):
            other = plane_target(e, d)
            pltpu.make_async_remote_copy(
                self.send.at[other],
                self.landed.at[d],
                self.plane_out.at[half],
                self.plane_in.at[half],
                device_id=(other, z),
                device_id_type=MESH,
            ).start()
            return carry

        lax.fori_loop(max(1, 16 * half), 16 * half + 16, send, 0)
        if half == 0:
            self.landed[0] = self.send[e]

    def crossed(self, half):
        drain(self.send.at[pl.ds(0, 15 + half)], self.plane_out.at[half])

    def copy(self, index, source, target, other):
        e = lax.axis_index("expert")
        return pltpu.make_async_remote_copy(
            source,
            target,
            self.ring_out.at[index],
            self.ring_in.at[index],
            device_id=(e, other),
            device_id_type=MESH,
        )

    def copies(self):
        e, z, right, left = place()
        part = self.part
        return [
            self.copy(0, part(0, 0), part(2, 0), right),
            self.copy(1, part(0, 1), part(2, 1), right),
            self.copy(2, part(0, 0), part(1, 0), left),
            self.copy(3, part(0, 1), part(1, 1), left),
            self.copy(4, self.one(0, 2, 0), self.one(0, 3, 0), right),
            self.copy(5, self.one(1, 1, 0), self.one(1, 3, 0), left),
            self.copy(6, self.one(0, 2, 1), self.one(0, 3, 1), right),
            self.copy(7, self.one(1, 1, 1), self.one(1, 3, 1), left),
        ]

    def turn(self, half, pack):
        drain(self.landed.at[pl.ds(15 * half + 1, 15 + half)], self.plane_in.at[half])
        packed = unfold(dot(pack, from_blocks(self.landed[16 * half : 16 * half + 16]))).astype(bf16)
        for j in range(2):
            self.rows[j, half * HALF : half * HALF + HALF] = packed[j * HALF : j * HALF + HALF]
        ring = self.copies()
        ring[half].start()
        ring[2 + half].start()

    def relay(self):
        ring = self.copies()
        for near, far in ((0, 4), (2, 5), (1, 6), (3, 7)):
            ring[near].wait_recv()
            ring[far].start()

    def last(self):
        ring = self.copies()
        for far in range(4, 8):
            ring[far].wait_recv()

    def close(self):
        for copy in self.copies():
            copy.wait_send()


DISPATCH_SCRATCH = [
    pltpu.SemaphoreType.DMA((2,)),
    pltpu.SemaphoreType.DMA((2,)),
    pltpu.SemaphoreType.DMA((8,)),
    pltpu.SemaphoreType.DMA((8,)),
]


class Return:
    def __init__(self, partial, relayed, landed, spread, home, sems):
        self.partial, self.relayed, self.landed = partial, relayed, landed
        self.spread, self.home = spread, home
        self.ring_out, self.ring_in, self.plane_out, self.plane_in = sems

    def one(self, expert, slot, half):
        return self.partial.at[expert, pl.ds(slot * 160 + half * HALF, HALF)]

    def copies(self, half):
        e, z, right, left = place()

        def copy(index, source, other):
            index = half * 6 + index
            return pltpu.make_async_remote_copy(
                source,
                self.landed.at[index],
                self.ring_out.at[index],
                self.ring_in.at[index],
                device_id=(e, other),
                device_id_type=MESH,
            )

        one = self.one
        return [
            copy(0, one(0, 3, half), right),
            copy(1, one(1, 3, half), left),
            copy(2, one(1, 1, half), right),
            copy(3, one(0, 2, half), left),
            copy(4, self.relayed.at[half, 0], right),
            copy(5, self.relayed.at[half, 1], left),
        ]

    def near(self, half):
        ring = self.copies(half)
        ring[2].start()
        ring[3].start()

    def far(self, half, index):
        self.copies(half)[index].start()

    def add_far(self, half):
        ring = self.copies(half)
        for index, expert, slot in ((0, 0, 1), (1, 1, 2)):
            ring[index].wait_recv()
            self.relayed[half, index] = (
                self.one(expert, slot, half)[...].astype(f32)
                + self.landed[half * 6 + index].astype(f32)
            ).astype(bf16)
            ring[4 + index].start()

    def finish(self, half, pack):
        e, z, right, left = place()
        ring = self.copies(half)
        total = []
        for expert, direct, summed in ((0, 3, 4), (1, 2, 5)):
            ring[direct].wait_recv()
            ring[summed].wait_recv()
            total.append(
                (
                    self.one(expert, 0, half)[...].astype(f32)
                    + self.landed[half * 6 + direct].astype(f32)
                    + self.landed[half * 6 + summed].astype(f32)
                ).astype(bf16)
            )
        flat = jnp.concatenate([total[0], total[1]], axis=0)
        self.spread[16 * half : 16 * half + 16] = as_blocks(dot_rows(pack, fold(flat)))

        def send(d, carry):
            pltpu.make_async_remote_copy(
                self.spread.at[d],
                self.home.at[e],
                self.plane_out,
                self.plane_in,
                device_id=(plane_source(e, d), z),
                device_id_type=MESH,
            ).start()
            return carry

        lax.fori_loop(max(1, 16 * half), 16 * half + 16, send, 0)
        if half == 0:
            self.home[e] = self.spread[0]

    def arrive(self):
        drain(self.home.at[pl.ds(0, PLANE - 1)], self.plane_in)

    def close(self):
        for copy in self.copies(0) + self.copies(1):
            copy.wait_send()
        drain(self.spread.at[pl.ds(0, PLANE - 1)], self.plane_out)


RETURN_SCRATCH = [
    pltpu.VMEM((2, 2, HALF, 768), bf16),
    pltpu.VMEM((12, HALF, 768), bf16),
    pltpu.VMEM(BLOCKS, bf16),
    pltpu.VMEM(BLOCKS, bf16),
    pltpu.SemaphoreType.DMA((12,)),
    pltpu.SemaphoreType.DMA((12,)),
    pltpu.SemaphoreType.DMA,
    pltpu.SemaphoreType.DMA,
]


def kernel_params(collective_id):
    return pltpu.CompilerParams(
        collective_id=collective_id, has_side_effects=True, vmem_limit_bytes=60 * 1024 * 1024
    )


VMEM = pl.BlockSpec(memory_space=pltpu.VMEM)


SEQ = 512
SIDE = 64
WIDTH = 768
HEAD_WIDTH = 192
LOCAL_HEADS = 3
score_scale = HEAD_DIM ** (-0.5)


class RingGather:
    def __init__(self, rows, sems):
        self.rows = rows
        self.out, self.arrived = sems

    def copies(self):
        e, z, right, left = place()

        def copy(index, owner, half, other):
            block = self.rows.at[pl.ds(pl.multiple_of(owner * 128 + half * SIDE, SIDE), SIDE)]
            return pltpu.make_async_remote_copy(
                block,
                block,
                self.out.at[index],
                self.arrived.at[index],
                device_id=(e, other),
                device_id_type=MESH,
            )

        def landing(index, owner, half):
            block = self.rows.at[pl.ds(pl.multiple_of(owner * 128 + half * SIDE, SIDE), SIDE)]
            return pltpu.make_async_copy(block, block, self.arrived.at[index])

        far = lax.rem(z + 2, RING)
        sends = [
            copy(0, z, 0, right),
            copy(1, z, 1, right),
            copy(2, z, 0, left),
            copy(3, z, 1, left),
            copy(4, left, 0, right),
            copy(5, right, 1, left),
        ]
        lands = [
            landing(0, left, 0),
            landing(1, left, 1),
            landing(2, right, 0),
            landing(3, right, 1),
            landing(4, far, 0),
            landing(5, far, 1),
        ]
        return sends, lands

    def start(self):
        sends, lands = self.copies()
        for index in (0, 3, 1, 2):
            sends[index].start()

    def relay(self):
        sends, lands = self.copies()
        lands[0].wait()
        sends[4].start()
        lands[3].wait()
        sends[5].start()

    def land(self, index):
        sends, lands = self.copies()
        lands[index].wait()

    def finish(self):
        self.relay()
        for index in (1, 2, 4, 5):
            self.land(index)

    def close(self):
        sends, lands = self.copies()
        for send in sends:
            send.wait_send()


GATHER_SCRATCH = [pltpu.SemaphoreType.DMA((6,)), pltpu.SemaphoreType.DMA((6,))]


class RingSum:
    def __init__(self, partial, relayed, landed, sems):
        self.partial, self.relayed, self.landed = partial, relayed, landed
        self.out, self.arrived = sems

    def part(self, slot, half):
        e, z, right, left = place()
        owner = (z, right, left, lax.rem(z + 2, RING))[slot]
        return self.partial.at[pl.ds(pl.multiple_of(owner * 128 + half * SIDE, SIDE), SIDE)]

    def copies(self):
        e, z, right, left = place()

        def copy(index, source, other):
            return pltpu.make_async_remote_copy(
                source,
                self.landed.at[index],
                self.out.at[index],
                self.arrived.at[index],
                device_id=(e, other),
                device_id_type=MESH,
            )

        part = self.part
        return [
            copy(0, part(3, 0), right),
            copy(1, part(3, 1), left),
            copy(2, part(1, 1), right),
            copy(3, part(2, 0), left),
            copy(4, self.relayed.at[0], right),
            copy(5, self.relayed.at[1], left),
        ]

    def send(self, index):
        self.copies()[index].start()

    def add_far(self):
        ring = self.copies()
        for index, slot, half in ((0, 1, 0), (1, 2, 1)):
            ring[index].wait_recv()
            self.relayed[index] = (
                self.part(slot, half)[...].astype(f32) + self.landed[index].astype(f32)
            ).astype(bf16)
            ring[4 + index].start()

    def total(self):
        ring = self.copies()
        halves = []
        for half, direct, summed in ((0, 3, 4), (1, 2, 5)):
            ring[direct].wait_recv()
            ring[summed].wait_recv()
            halves.append(
                self.part(0, half)[...].astype(f32)
                + self.landed[direct].astype(f32)
                + self.landed[summed].astype(f32)
            )
        return jnp.concatenate(halves, axis=0)

    def close(self):
        for copy in self.copies():
            copy.wait_send()


SUM_SCRATCH = [
    pltpu.VMEM((SEQ, WIDTH), bf16),
    pltpu.VMEM((2, SIDE, WIDTH), bf16),
    pltpu.VMEM((6, SIDE, WIDTH), bf16),
    pltpu.SemaphoreType.DMA((6,)),
    pltpu.SemaphoreType.DMA((6,)),
]


def head_mask(h):
    lane = lax.broadcasted_iota(jnp.int32, (1, HEAD_WIDTH), 1)
    return (lane >= h * HEAD_DIM) & (lane < (h + 1) * HEAD_DIM)


def sum_diagonals(square):
    rows = square
    for step in (32, 8, 1):
        count = rows.shape[0] // step
        rows = sum(
            pltpu.roll(rows[a * step : a * step + step], (SEQ - a * step) % SEQ, 1)
            if a
            else rows[:step]
            for a in range(count)
        )
    return rows


def bucket_hot_rows(bucket_rev):
    return (bucket_rev == lax.broadcasted_iota(jnp.int32, (32, SEQ), 0)).astype(f32)


def plane_sends(source_at, target_at, send_sem, recv_sem_at):
    e, z, right, left = place()

    def send(chip, carry):
        other = plane_target(e, chip * 2)
        pltpu.make_async_remote_copy(
            source_at(other // 2),
            target_at(e // 2),
            send_sem,
            recv_sem_at(e // 2),
            device_id=(other, z),
            device_id_type=MESH,
        ).start()
        return carry

    lax.fori_loop(1, 16, send, 0)


def rms_scale(values):
    return lax.rsqrt(jnp.mean(values * values, axis=1, keepdims=True) + epsilon)


def select_rows(ids):
    expert = lax.broadcasted_iota(jnp.int32, (128, 64), 1)
    hot = [(ids[:, c : c + 1] == expert).astype(f32) for c in range(TOPK)]
    row = lax.broadcasted_iota(jnp.int32, (128, 128), 0)
    col = lax.broadcasted_iota(jnp.int32, (128, 128), 1)
    before = dot((col < row).astype(bf16), (hot[0] + hot[1]).astype(bf16))
    pos = lax.broadcasted_iota(jnp.int32, (128, PAD), 1)
    picks = []
    for c in range(TOPK):
        slot = jnp.sum(before * hot[c], axis=1, keepdims=True).astype(jnp.int32)
        own = ids[:, c : c + 1]
        first = own // 2
        base = first * BLOCK + (own - first * 2) * 5 + slot
        picks.append(
            jnp.concatenate([(pos == base).astype(bf16), (pos == base + 10).astype(bf16)], axis=0)
        )
    return picks


def as_column(row):
    n = row.shape[1]
    same = lax.broadcasted_iota(jnp.int32, (n, n), 0) == lax.broadcasted_iota(jnp.int32, (n, n), 1)
    return jnp.sum(jnp.where(same, row, 0.0), axis=1, keepdims=True)


def as_row(rows):
    return jnp.concatenate([rows[i : i + 1] for i in range(rows.shape[0])], axis=1)


def layer_kernel(
    tokens, gain_attn, gain_moe, qkv_weight, proj_weight, bias, weight_in, weight_out,
    ids, gates, buckets, cotangent,
    out, grad_input, qkv_grad, proj_grad, gain_first, gain_second, table_out,
    grads_hbm,
    units, whole, qkv, attended, probs, picked, resid, mine, wall, whole32,
    x_send, x_landed, x_rows, g_send, g_landed, g_rows,
    held_in, held_out, hidden, grad_pre, grad_part, y_part, expert_grads,
    seq_grad, grad_qkv, blocks, near_blocks, plane_landed, small_own, small_landed, small_sum, small_plane,
    load_sems, save_sems, w_send, w_recv, s_send, s_recv, v_send, v_recv,
    p_send, p_recv, t_send, t_recv, q_send, q_recv, *rest,
):
    x_sems, g_sems, rest = rest[:4], rest[4:8], rest[8:]
    unit_sems, grad_sems, rest = rest[:2], rest[2:4], rest[4:]
    sum_a, sum_b, rest = rest[:5], rest[5:10], rest[10:]
    back_x, back_y = rest[:8], rest[8:]
    e, z, right, left = place()
    core, chip = lax.rem(e, 2), e // 2
    twin = chip * 2 + 1 - core
    opposite = lax.rem(z + 2, RING)
    loads = [
        pltpu.make_async_copy(weight_in, held_in, load_sems.at[0]),
        pltpu.make_async_copy(weight_out, held_out, load_sems.at[1]),
    ]
    for load in loads:
        load.start()
    arrivals = greet(1, 1, 1)

    mine[...] = jnp.concatenate(
        [qkv_weight[i].astype(f32) for i in range(3)] + [proj_weight[...].astype(f32)], axis=1
    ).astype(bf16)
    inputs = tokens[...].astype(f32)
    own_rows = pl.ds(pl.multiple_of(z * 128, 128), 128)
    units[own_rows] = (inputs * rms_scale(inputs)).astype(bf16)
    pl.semaphore_wait(pltpu.get_barrier_semaphore(), arrivals)
    plane_sends(lambda other: mine, lambda own: wall.at[core, own], w_send, w_recv.at.__getitem__)
    unit_ring = RingGather(units, unit_sems)
    unit_ring.start()
    wall[core, chip] = mine[...]

    def pass_on(source):
        return pltpu.make_async_remote_copy(
            wall.at[core, source],
            wall.at[core, source],
            s_send,
            s_recv,
            device_id=(twin, z),
            device_id_type=MESH,
        )

    pass_on(chip).start()
    gain_a, gain_m = as_row(gain_attn[...]), as_row(gain_moe[...])
    id_columns = jnp.concatenate(
        [as_column(ids[c : c + 1].astype(f32)) for c in range(TOPK)], axis=1
    ).astype(jnp.int32)
    gate_columns = [as_column(gates[c : c + 1]) for c in range(TOPK)]
    picks = select_rows(id_columns)
    for c in range(TOPK):
        picked[c] = picks[c]
    grad_out = cotangent[...].astype(f32)
    g_send[...] = as_blocks(
        dot_rows(picks[0], fold((gate_columns[0] * grad_out).astype(bf16)))
        + dot_rows(picks[1], fold((gate_columns[1] * grad_out).astype(bf16)))
    )
    grads = Dispatch(g_send, g_landed, g_rows, g_sems)
    unit_ring.relay()
    far_row = lax.broadcasted_iota(jnp.int32, (SEQ, SEQ), 0)
    far_col = lax.broadcasted_iota(jnp.int32, (SEQ, SEQ), 1)
    mirror = (far_row + far_col == jnp.where(far_col == 0, 0, SEQ)).astype(bf16)
    hot = dot(bucket_hot_rows(as_row(buckets[...])).astype(bf16), mirror)
    rels = [
        jnp.sum(as_column(bias[h : h + 1]) * hot, axis=0, keepdims=True)
        for h in range(LOCAL_HEADS)
    ]
    pack = packer()

    def forward(step, carry):
        source = plane_source(e, step * 2) // 2
        pltpu.make_async_copy(wall.at[core, source], wall.at[core, source], w_recv.at[source]).wait()
        pass_on(source).start()
        return carry

    lax.fori_loop(1, 16, forward, 0)
    for index in (1, 2, 4, 5):
        unit_ring.land(index)
    drain(wall.at[0, pl.ds(0, 15)], w_send)
    grads.cross(0)
    grads.cross(1)
    unit_rows = units[...].astype(f32)
    normed = (unit_rows * gain_a).astype(bf16)
    drain(wall.at[1 - core], s_recv)
    for block in range(PLANE):
        whole32[24 * block : 24 * block + 24] = wall[block % 2, block // 2].astype(f32)
    whole[...] = whole32[...].astype(bf16)

    qkv[...] = dot(normed, whole[:, :640]).astype(bf16)[:, : 3 * HEAD_WIDTH]
    keys = qkv[:, HEAD_WIDTH : 2 * HEAD_WIDTH]
    values = qkv[:, 2 * HEAD_WIDTH :]
    proj = whole[:, 3 * HEAD_WIDTH :]
    attn_sum = RingSum(sum_a[0], sum_a[1], sum_a[2], sum_a[3:])
    owners = (z, right, left, opposite)
    query_row = lax.broadcasted_iota(jnp.int32, (128, SEQ), 0)
    key_col = lax.broadcasted_iota(jnp.int32, (128, SEQ), 1)

    def rows_of(slot):
        return pl.ds(pl.multiple_of(owners[slot] * 128, 128), 128)

    def attend(slot):
        rows = rows_of(slot)
        first = owners[slot] * 128
        queries = qkv[rows, :HEAD_WIDTH]
        mixed = jnp.zeros((128, HEAD_WIDTH), f32)
        for h in range(LOCAL_HEADS):
            mask = head_mask(h)
            turned = pltpu.roll(rels[h], first, 1)
            shifted = pltpu.roll(
                jnp.broadcast_to(turned, (128, SEQ)), 0, 1, stride=1, stride_axis=0
            )
            scores = dot_cols(jnp.where(mask, queries, jnp.zeros_like(queries)), keys) * score_scale
            scores = jnp.where(key_col <= query_row + first, scores + shifted, masked_value)
            raised = jnp.exp(scores - jnp.max(scores, axis=1, keepdims=True))
            weights_p = (raised / jnp.sum(raised, axis=1, keepdims=True)).astype(bf16)
            probs[h, rows] = weights_p
            mixed = jnp.where(mask, dot(weights_p, values), mixed)
        mixed = mixed.astype(bf16)
        attended[rows] = mixed
        sum_a[0][rows] = dot_cols(mixed, proj).astype(bf16)

    attend(3)
    attn_sum.send(0)
    attn_sum.send(1)
    attend(1)
    attn_sum.send(2)
    attend(2)
    attn_sum.send(3)
    attend(0)
    attn_sum.add_far()
    grads.turn(0, pack)
    grads.turn(1, pack)
    residual = inputs + attn_sum.total()
    resid[...] = residual
    scale_m = rms_scale(residual)
    normal_m = residual * scale_m
    x_send[...] = as_blocks(
        dot_rows(picks[0] + picks[1], fold((normal_m * gain_m).astype(bf16)))
    )

    out_way = Dispatch(x_send, x_landed, x_rows, x_sems)
    home_way = Return(grad_part, back_x[0], back_x[1], back_x[2], back_x[3], back_x[4:])
    out_way.cross(0)
    out_way.crossed(0)
    out_way.cross(1)
    out_way.turn(0, pack)
    out_way.turn(1, pack)
    for load in loads:
        load.wait()

    def run(first, count, experts=(0, 1)):
        for j in experts:
            span = pl.ds(first * 160, count * 160)
            pre_act = dot(x_rows[j, span], held_in[j])
            cdf = 0.5 * (1.0 + lax.erf(pre_act * inv_root_two))
            hidden[j, span] = (pre_act * cdf).astype(bf16)
            slope = cdf + pre_act * jnp.exp(-0.5 * pre_act * pre_act) * inv_root_tau
            grad_hidden = dot_cols(g_rows[j, span], held_out[j])
            grad_pre[j, span] = (grad_hidden * slope).astype(bf16)
            grad_part[j, span] = dot_cols(grad_pre[j, span], held_in[j]).astype(bf16)

    run(0, 1)
    grads.relay()
    out_way.relay()
    run(1, 2)
    home_way.near(0)
    home_way.near(1)
    grads.last()
    out_way.last()
    for j in range(2):
        run(3, 1, (j,))
        home_way.far(0, j)
        home_way.far(1, j)
    y_way = Return(y_part, back_y[0], back_y[1], back_y[2], back_y[3], back_y[4:])
    for j in range(2):
        y_part[j] = dot(hidden[j], held_out[j]).astype(bf16)
    home_way.add_far(0)
    home_way.add_far(1)
    for half in range(2):
        y_way.far(half, 0)
        y_way.far(half, 1)
        y_way.near(half)
    home_way.finish(0, pack)
    home_way.finish(1, pack)
    saves = []
    for j in range(2):
        expert_grads[j] = dot_rows(x_rows[j], grad_pre[j]).astype(bf16)
        expert_grads[2 + j] = dot_rows(hidden[j], g_rows[j]).astype(bf16)
        y_way.add_far(j)
    for index in range(4):
        saves.append(
            pltpu.make_async_copy(expert_grads.at[index], grads_hbm.at[index], save_sems.at[index])
        )
        saves[index].start()
    home_way.arrive()
    grad_normed = unfold(dot(picked[0] + picked[1], from_blocks(home_way.home[...])))
    gain_m_part = jnp.sum(grad_normed * normal_m, axis=0, keepdims=True)
    grad_unit_m = grad_normed * gain_m
    grad_resid = grad_out + scale_m * (
        grad_unit_m - normal_m * jnp.mean(grad_unit_m * normal_m, axis=1, keepdims=True)
    )

    seq_grad[own_rows] = grad_resid.astype(bf16)
    grad_ring = RingGather(seq_grad, grad_sems)
    grad_ring.start()
    zeros = jnp.zeros((SEQ, HEAD_WIDTH), f32)
    carried = [zeros, zeros, jnp.zeros((WIDTH, HEAD_WIDTH), f32)]
    diagonals = [jnp.zeros((1, SEQ), f32)] * LOCAL_HEADS

    def attend_back(slot):
        rows = rows_of(slot)
        queries = qkv[rows, :HEAD_WIDTH]
        grad_rows = seq_grad[rows]
        grad_att = dot(grad_rows, proj).astype(bf16)
        carried[2] = carried[2] + dot_rows(grad_rows, attended[rows])
        grad_q = jnp.zeros((128, HEAD_WIDTH), f32)
        for h in range(LOCAL_HEADS):
            mask = head_mask(h)
            weights_p = probs[h, rows]
            soft = weights_p.astype(f32)
            own_att = jnp.where(mask, grad_att, jnp.zeros_like(grad_att))
            own_queries = jnp.where(mask, queries, jnp.zeros_like(queries))
            grad_w = dot_cols(own_att, values)
            row_dot = jnp.sum(soft * grad_w, axis=1, keepdims=True)
            grad_scores = (soft * (grad_w - row_dot)).astype(bf16)
            turn = lax.rem(SEQ - owners[slot] * 128, SEQ)
            diagonals[h] = diagonals[h] + pltpu.roll(
                sum_diagonals(grad_scores.astype(f32)), turn, 1
            )
            grad_q = jnp.where(mask, dot(grad_scores, keys), grad_q)
            carried[0] = carried[0] + dot_rows(grad_scores, own_queries)
            carried[1] = carried[1] + dot_rows(weights_p, own_att)
        grad_qkv[rows, :HEAD_WIDTH] = (grad_q * score_scale).astype(bf16)

    attend_back(0)
    grad_ring.relay()
    grad_ring.land(2)
    attend_back(1)
    y_way.finish(0, pack)
    grad_ring.land(1)
    attend_back(2)
    y_way.finish(1, pack)
    grad_ring.land(4)
    grad_ring.land(5)
    attend_back(3)
    grad_qkv[:, HEAD_WIDTH:] = jnp.concatenate(
        [carried[0] * score_scale, carried[1]], axis=1
    ).astype(bf16)
    proj_part = carried[2]
    full = jnp.concatenate([dot_rows(normed, grad_qkv[...]), proj_part], axis=1)
    for block in range(PLANE):
        blocks[block % 2, block // 2] = full[24 * block : 24 * block + 24].astype(bf16)
    sibling = pltpu.make_async_remote_copy(
        blocks.at[1 - core],
        near_blocks,
        v_send,
        v_recv,
        device_id=(twin, z),
        device_id_type=MESH,
    )
    sibling.start()
    grad_normed_a = dot_cols(grad_qkv[...], whole[:, : 3 * HEAD_WIDTH])
    sum_b[0][...] = grad_normed_a.astype(bf16)
    input_sum = RingSum(sum_b[0], sum_b[1], sum_b[2], sum_b[3:])
    for index in range(4):
        input_sum.send(index)
    gain_part = jnp.sum(grad_normed_a * unit_rows, axis=0, keepdims=True)
    diagonal = jnp.concatenate(diagonals + [jnp.zeros((5, SEQ), f32)], axis=0)
    table_rows = lax.dot_general(
        diagonal, hot, (((1,), (1,)), ((), ())), precision=highest, preferred_element_type=f32
    )
    pieces = [
        part[:, 128 * i : 128 * i + 128] for part in (gain_part, gain_m_part) for i in range(6)
    ]
    small_own[...] = jnp.concatenate(
        pieces + [jnp.zeros((4, 128), f32)], axis=0
    )
    small_own[12 : 12 + LOCAL_HEADS, :32] = table_rows[:LOCAL_HEADS]
    shares = [
        pltpu.make_async_remote_copy(
            small_own,
            small_landed.at[index],
            t_send.at[index],
            t_recv.at[index],
            device_id=(e, other),
            device_id_type=MESH,
        )
        for index, other in enumerate((right, left, opposite))
    ]
    for share in shares:
        share.start()
    sibling.wait_recv()
    near_blocks[...] = (blocks[core].astype(f32) + near_blocks[...].astype(f32)).astype(bf16)
    plane_sends(
        lambda other: near_blocks.at[other],
        lambda own: plane_landed.at[own],
        p_send,
        lambda own: p_recv,
    )
    plane_landed[chip] = near_blocks[chip]
    input_sum.add_far()
    for share in shares:
        share.wait_recv()
    own_small = small_own[...]
    line = lax.broadcasted_iota(jnp.int32, (16, 128), 0)
    small_sum[...] = jnp.where(
        line < 12, own_small + small_landed[0] + small_landed[1] + small_landed[2], own_small
    )

    def spread_small(d, carry):
        pltpu.make_async_remote_copy(
            small_sum,
            small_plane.at[d],
            q_send,
            q_recv,
            device_id=(plane_target(e, d), z),
            device_id_type=MESH,
        ).start()
        return carry

    lax.fori_loop(1, PLANE, spread_small, 0)
    small_plane[0] = small_sum[...]
    y_way.arrive()
    home = from_blocks(y_way.home[...])
    out[...] = (
        resid[...]
        + gate_columns[0] * unfold(dot(picked[0], home))
        + gate_columns[1] * unfold(dot(picked[1], home))
    ).astype(bf16)
    scale_first = rms_scale(inputs)
    normal_first = inputs * scale_first
    grad_unit = input_sum.total() * gain_a
    grad_input[...] = grad_resid + scale_first * (
        grad_unit - normal_first * jnp.mean(grad_unit * normal_first, axis=1, keepdims=True)
    )
    drain(plane_landed.at[pl.ds(0, 15)], p_recv)
    total = plane_landed[0].astype(f32)
    for block in range(1, 16):
        total = total + plane_landed[block].astype(f32)
    for i in range(3):
        qkv_grad[i] = total[:, i * HEAD_WIDTH : (i + 1) * HEAD_WIDTH]
    proj_grad[...] = total[:, 3 * HEAD_WIDTH :]
    drain(small_plane.at[pl.ds(1, PLANE - 1)], q_recv)
    summed = jnp.sum(small_plane[...], axis=0)
    column = lax.broadcasted_iota(jnp.int32, (16, 128), 1)
    table_own = jnp.sum(jnp.where(column == e, summed, 0.0), axis=1, keepdims=True)
    table_out[...] = jnp.concatenate(
        [table_own[12 + h : 13 + h] for h in range(LOCAL_HEADS)], axis=1
    )
    wide = jnp.concatenate([as_row(summed[0:6]), as_row(summed[6:12])], axis=0)
    wide = jnp.concatenate([wide, jnp.zeros((6, WIDTH), f32)], axis=0)
    feature = lax.broadcasted_iota(jnp.int32, (WIDTH, 128), 0)
    lane = lax.broadcasted_iota(jnp.int32, (WIDTH, 128), 1)
    taken = (feature == (e * RING + z) * 6 + lane).astype(f32)
    gains = jnp.dot(wide, taken, precision=highest, preferred_element_type=f32)
    gain_first[...] = gains[0:1, :6]
    gain_second[...] = gains[1:2, :6]

    drain(small_plane.at[pl.ds(1, PLANE - 1)], q_send)
    for share in shares:
        share.wait_send()
    for save in saves:
        save.wait()
    for way in (grads, out_way):
        way.close()
        way.crossed(1)
    grads.crossed(0)
    home_way.close()
    y_way.close()
    unit_ring.close()
    grad_ring.close()
    attn_sum.close()
    input_sum.close()
    sibling.wait_send()
    drain(wall.at[0], s_send)
    drain(plane_landed.at[pl.ds(0, 15)], p_send)


def run_layer(*operands):
    def shape(dims, kind=f32):
        return jax.ShapeDtypeStruct(dims, kind)

    anywhere = pl.BlockSpec(memory_space=pl.ANY)
    rows = (2, EXPERT_ROWS, WIDTH)
    dma = pltpu.SemaphoreType.DMA
    return pl.pallas_call(
        layer_kernel,
        out_shape=[
            shape((128, WIDTH), bf16),
            shape((128, WIDTH)),
            shape((3, 24, HEAD_WIDTH)),
            shape((24, HEAD_WIDTH)),
            shape((1, 6)),
            shape((1, 6)),
            shape((1, LOCAL_HEADS)),
        ]
        + [shape((4, WIDTH, WIDTH), bf16)],
        in_specs=[VMEM] * 6 + [anywhere] * 2 + [VMEM] * 4,
        out_specs=[VMEM] * 7 + [anywhere],
        scratch_shapes=[
            pltpu.VMEM((SEQ, WIDTH), bf16),
            pltpu.VMEM((WIDTH, WIDTH), bf16),
            pltpu.VMEM((SEQ, 3 * HEAD_WIDTH), bf16),
            pltpu.VMEM((SEQ, HEAD_WIDTH), bf16),
            pltpu.VMEM((LOCAL_HEADS, SEQ, SEQ), bf16),
            pltpu.VMEM((TOPK, 256, PAD), bf16),
            pltpu.VMEM((128, WIDTH), f32),
            pltpu.VMEM((24, WIDTH), bf16),
            pltpu.VMEM((2, 16, 24, WIDTH), bf16),
            pltpu.VMEM((WIDTH, WIDTH), f32),
        ]
        + [pltpu.VMEM(BLOCKS, bf16), pltpu.VMEM(BLOCKS, bf16), pltpu.VMEM(rows, bf16)] * 2
        + [pltpu.VMEM((2, WIDTH, WIDTH), bf16)] * 2
        + [pltpu.VMEM(rows, bf16)] * 4
        + [
            pltpu.VMEM((4, WIDTH, WIDTH), bf16),
            pltpu.VMEM((SEQ, WIDTH), bf16),
            pltpu.VMEM((SEQ, 3 * HEAD_WIDTH), bf16),
            pltpu.VMEM((2, 16, 24, WIDTH), bf16),
            pltpu.VMEM((16, 24, WIDTH), bf16),
            pltpu.VMEM((16, 24, WIDTH), bf16),
            pltpu.VMEM((16, 128), f32),
            pltpu.VMEM((3, 16, 128), f32),
            pltpu.VMEM((16, 128), f32),
            pltpu.VMEM((PLANE, 16, 128), f32),
            dma((2,)),
            dma((4,)),
            dma,
            dma((16,)),
            dma,
            dma,
            dma,
            dma,
            dma,
            dma,
            dma((3,)),
            dma((3,)),
            dma,
            dma,
        ]
        + DISPATCH_SCRATCH * 2
        + GATHER_SCRATCH * 2
        + SUM_SCRATCH * 2
        + RETURN_SCRATCH * 2,
        compiler_params=kernel_params(1),
        name="layer",
    )(*operands)


def widen_kernel(narrow, *refs):
    count = (len(refs) - 8) // 3
    passed, results = refs[:count], refs[count : 2 * count]
    wide_in, wide_out, held, wide, loads, saves, ins, outs = refs[2 * count : 2 * count + 8]
    bounced = refs[2 * count + 8 :]
    reads = [pltpu.make_async_copy(narrow.at[i], held.at[i], loads.at[i]) for i in range(4)]
    for read in reads:
        read.start()
    arrive = [
        pltpu.make_async_copy(passed[i], bounced[i], ins.at[i]) for i in range(count)
    ]
    leave = [
        pltpu.make_async_copy(bounced[i], results[i], outs.at[i]) for i in range(count)
    ]
    for copy in arrive:
        copy.start()
    writes = []
    for i in range(4):
        reads[i].wait()
        wide[i] = held[i].astype(f32)
        target = (wide_in, wide_out)[i // 2].at[i % 2]
        writes.append(pltpu.make_async_copy(wide.at[i], target, saves.at[i]))
        writes[i].start()
        if i == 0:
            for one, other in zip(arrive, leave):
                one.wait()
                other.start()
    for write in writes + leave:
        write.wait()


def widen(narrow, *small):
    anywhere = pl.BlockSpec(memory_space=pl.ANY)
    grads = jax.ShapeDtypeStruct((2, WIDTH, WIDTH), f32)
    return pl.pallas_call(
        widen_kernel,
        out_shape=[jax.ShapeDtypeStruct(a.shape, a.dtype) for a in small] + [grads, grads],
        in_specs=[anywhere] * (1 + len(small)),
        out_specs=[anywhere] * (len(small) + 2),
        scratch_shapes=[
            pltpu.VMEM((4, WIDTH, WIDTH), bf16),
            pltpu.VMEM((4, WIDTH, WIDTH), f32),
            pltpu.SemaphoreType.DMA((4,)),
            pltpu.SemaphoreType.DMA((4,)),
            pltpu.SemaphoreType.DMA((len(small),)),
            pltpu.SemaphoreType.DMA((len(small),)),
        ]
        + [pltpu.VMEM(a.shape, a.dtype) for a in small],
        compiler_params=pltpu.CompilerParams(vmem_limit_bytes=60 * 1024 * 1024),
        name="widen",
    )(narrow, *small)


def body(
    tokens,
    gain_attn,
    gain_moe,
    qkv_weight,
    proj_weight,
    bias_table,
    expert_in,
    expert_out,
    expert_ids,
    gate_values,
    bucket_table,
    cotangent,
):
    results = run_layer(
        tokens,
        gain_attn.reshape(6, 128),
        gain_moe.reshape(6, 128),
        qkv_weight.transpose(1, 0, 2),
        proj_weight.T,
        bias_table.T,
        expert_in,
        expert_out,
        expert_ids.T,
        gate_values.T,
        bucket_table.reshape(4, 128),
        cotangent,
    )
    out, grad_input, qkv_grad, proj_grad, gain_first, gain_second, table, grad_in, grad_out = widen(
        results[7], *results[:7]
    )
    return (
        out,
        grad_input,
        gain_first[0],
        gain_second[0],
        qkv_grad.transpose(1, 0, 2),
        proj_grad.T,
        table,
        grad_in,
        grad_out,
    )


def solution(mesh):
    placed = (
        P(("expert", "mp"), None),
        P(),
        P(),
        P("expert", None, "mp"),
        P("mp", "expert"),
        P(None, "mp"),
        P("expert", None, "mp"),
        P("expert", "mp", None),
        P(("expert", "mp"), None),
        P(("expert", "mp"), None),
        P(),
        P(("expert", "mp"), None),
    )
    return jax.shard_map(
        body,
        mesh=mesh,
        in_specs=placed,
        out_specs=(
            P(("expert", "mp"), None),
            P(("expert", "mp"), None),
            P(("expert", "mp")),
            P(("expert", "mp")),
            P("expert", None, "mp"),
            P("mp", "expert"),
            P("expert", "mp"),
            P("expert", None, "mp"),
            P("expert", "mp", None),
        ),
        check_vma=False,
    )
```

```python
import jax
import jax.numpy as jnp
from jax import lax
from jax.experimental import pallas as pl
from jax.experimental.pallas import tpu as pltpu
from jax.sharding import PartitionSpec as P

HEAD_DIM = 64
TOPK = 2


epsilon = 1e-06
masked_value = -1e30
inv_root_two = 0.7071067811865476
inv_root_tau = 0.3989422804014327
highest = lax.Precision.HIGHEST


MESH = pl.DeviceIdType.MESH
BLOCK = 24
NARROW = 384
HALF = 80
PLANE = 32
RING = 4
PAD = PLANE * BLOCK
BLOCKS = (PLANE, BLOCK, NARROW)
ROWS = 320
EXPERT_ROWS = 640
f32 = jnp.float32
bf16 = jnp.bfloat16


def place():
    e, z = lax.axis_index("expert"), lax.axis_index("mp")
    return e, z, lax.rem(z + 1, RING), lax.rem(z + RING - 1, RING)


def plane_target(e, d):
    step = d // 8
    dy, dx, dc = lax.rem(step * 2, 4) + step // 2, lax.rem(d // 2, 4), lax.rem(d, 2)
    y, x, c = e // 8, lax.rem(e // 2, 4), lax.rem(e, 2)
    return lax.rem(y + dy, 4) * 8 + lax.rem(x + dx, 4) * 2 + lax.rem(c + dc, 2)


def plane_source(e, d):
    step = d // 8
    dy, dx, dc = lax.rem(step * 2, 4) + step // 2, lax.rem(d // 2, 4), lax.rem(d, 2)
    y, x, c = e // 8, lax.rem(e // 2, 4), lax.rem(e, 2)
    return lax.rem(y + 4 - dy, 4) * 8 + lax.rem(x + 4 - dx, 4) * 2 + lax.rem(c + dc, 2)


def fold(rows):
    return jnp.concatenate([rows[:, :NARROW], rows[:, NARROW:]], axis=0)


def unfold(rows):
    half = rows.shape[0] // 2
    return jnp.concatenate([rows[:half], rows[half:]], axis=1)


def as_blocks(rows):
    return rows.reshape(rows.shape[0] // BLOCK, BLOCK, NARROW).astype(bf16)


def from_blocks(blocks):
    return blocks.astype(f32).reshape(blocks.shape[0] * BLOCK, NARROW).astype(bf16)


def greet(plane, ring, across=0):
    e, z, right, left = place()
    barrier = pltpu.get_barrier_semaphore()
    if plane:

        def signal(d, carry):
            pl.semaphore_signal(
                barrier, inc=1, device_id=(plane_target(e, d), z), device_id_type=MESH
            )
            return carry

        lax.fori_loop(1, PLANE, signal, 0)
    if ring:
        for other in (right, left):
            pl.semaphore_signal(barrier, inc=1, device_id=(e, other), device_id_type=MESH)
    if across:
        other = lax.rem(z + 2, RING)
        pl.semaphore_signal(barrier, inc=1, device_id=(e, other), device_id_type=MESH)
    return (PLANE - 1) * plane + 2 * ring + across


def drain(ref, sem):
    pltpu.make_async_copy(ref, ref, sem).wait()


def dot(left, right):
    return jnp.dot(left, right, preferred_element_type=f32)


def dot_rows(left, right):
    return lax.dot_general(left, right, (((0,), (0,)), ((), ())), preferred_element_type=f32)


def dot_cols(left, right):
    return lax.dot_general(left, right, (((1,), (1,)), ((), ())), preferred_element_type=f32)


def packer():
    row = lax.broadcasted_iota(jnp.int32, (4 * HALF, 16 * BLOCK), 0)
    col = lax.broadcasted_iota(jnp.int32, (4 * HALF, 16 * BLOCK), 1)
    side = (row >= 2 * HALF).astype(jnp.int32)
    rest = row - side * 2 * HALF
    expert = (rest >= HALF).astype(jnp.int32)
    inner = rest - expert * HALF
    source = (inner * 205) // 1024
    slot = inner - source * 5
    return (col == source * BLOCK + side * 10 + expert * 5 + slot).astype(bf16)


class Dispatch:
    def __init__(self, send, landed, rows, sems):
        self.send, self.landed, self.rows = send, landed, rows
        self.plane_out, self.plane_in, self.ring_out, self.ring_in = sems

    def part(self, slot, half):
        return self.rows.at[:, pl.ds(slot * 160 + half * HALF, HALF)]

    def one(self, expert, slot, half):
        return self.rows.at[expert, pl.ds(slot * 160 + half * HALF, HALF)]

    def cross(self, half):
        e, z, right, left = place()

        def send(d, carry):
            other = plane_target(e, d)
            pltpu.make_async_remote_copy(
                self.send.at[other],
                self.landed.at[d],
                self.plane_out.at[half],
                self.plane_in.at[half],
                device_id=(other, z),
                device_id_type=MESH,
            ).start()
            return carry

        lax.fori_loop(max(1, 16 * half), 16 * half + 16, send, 0)
        if half == 0:
            self.landed[0] = self.send[e]

    def crossed(self, half):
        drain(self.send.at[pl.ds(0, 15 + half)], self.plane_out.at[half])

    def copy(self, index, source, target, other):
        e = lax.axis_index("expert")
        return pltpu.make_async_remote_copy(
            source,
            target,
            self.ring_out.at[index],
            self.ring_in.at[index],
            device_id=(e, other),
            device_id_type=MESH,
        )

    def copies(self):
        e, z, right, left = place()
        part = self.part
        return [
            self.copy(0, part(0, 0), part(2, 0), right),
            self.copy(1, part(0, 1), part(2, 1), right),
            self.copy(2, part(0, 0), part(1, 0), left),
            self.copy(3, part(0, 1), part(1, 1), left),
            self.copy(4, self.one(0, 2, 0), self.one(0, 3, 0), right),
            self.copy(5, self.one(1, 1, 0), self.one(1, 3, 0), left),
            self.copy(6, self.one(0, 2, 1), self.one(0, 3, 1), right),
            self.copy(7, self.one(1, 1, 1), self.one(1, 3, 1), left),
        ]

    def turn(self, half, pack):
        drain(self.landed.at[pl.ds(15 * half + 1, 15 + half)], self.plane_in.at[half])
        packed = unfold(dot(pack, from_blocks(self.landed[16 * half : 16 * half + 16]))).astype(bf16)
        for j in range(2):
            self.rows[j, half * HALF : half * HALF + HALF] = packed[j * HALF : j * HALF + HALF]
        ring = self.copies()
        ring[half].start()
        ring[2 + half].start()

    def relay(self):
        ring = self.copies()
        for near, far in ((0, 4), (2, 5), (1, 6), (3, 7)):
            ring[near].wait_recv()
            ring[far].start()

    def last(self):
        ring = self.copies()
        for far in range(4, 8):
            ring[far].wait_recv()

    def close(self):
        for copy in self.copies():
            copy.wait_send()


DISPATCH_SCRATCH = [
    pltpu.SemaphoreType.DMA((2,)),
    pltpu.SemaphoreType.DMA((2,)),
    pltpu.SemaphoreType.DMA((8,)),
    pltpu.SemaphoreType.DMA((8,)),
]


class Return:
    def __init__(self, partial, relayed, landed, spread, home, sems):
        self.partial, self.relayed, self.landed = partial, relayed, landed
        self.spread, self.home = spread, home
        self.ring_out, self.ring_in, self.plane_out, self.plane_in = sems

    def one(self, expert, slot, half):
        return self.partial.at[expert, pl.ds(slot * 160 + half * HALF, HALF)]

    def copies(self, half):
        e, z, right, left = place()

        def copy(index, source, other):
            index = half * 6 + index
            return pltpu.make_async_remote_copy(
                source,
                self.landed.at[index],
                self.ring_out.at[index],
                self.ring_in.at[index],
                device_id=(e, other),
                device_id_type=MESH,
            )

        one = self.one
        return [
            copy(0, one(0, 3, half), right),
            copy(1, one(1, 3, half), left),
            copy(2, one(1, 1, half), right),
            copy(3, one(0, 2, half), left),
            copy(4, self.relayed.at[half, 0], right),
            copy(5, self.relayed.at[half, 1], left),
        ]

    def near(self, half):
        ring = self.copies(half)
        ring[2].start()
        ring[3].start()

    def far(self, half, index):
        self.copies(half)[index].start()

    def add_far(self, half):
        ring = self.copies(half)
        for index, expert, slot in ((0, 0, 1), (1, 1, 2)):
            ring[index].wait_recv()
            self.relayed[half, index] = (
                self.one(expert, slot, half)[...].astype(f32)
                + self.landed[half * 6 + index].astype(f32)
            ).astype(bf16)
            ring[4 + index].start()

    def finish(self, half, pack):
        e, z, right, left = place()
        ring = self.copies(half)
        total = []
        for expert, direct, summed in ((0, 3, 4), (1, 2, 5)):
            ring[direct].wait_recv()
            ring[summed].wait_recv()
            total.append(
                (
                    self.one(expert, 0, half)[...].astype(f32)
                    + self.landed[half * 6 + direct].astype(f32)
                    + self.landed[half * 6 + summed].astype(f32)
                ).astype(bf16)
            )
        flat = jnp.concatenate([total[0], total[1]], axis=0)
        self.spread[16 * half : 16 * half + 16] = as_blocks(dot_rows(pack, fold(flat)))

        def send(d, carry):
            pltpu.make_async_remote_copy(
                self.spread.at[d],
                self.home.at[e],
                self.plane_out,
                self.plane_in,
                device_id=(plane_source(e, d), z),
                device_id_type=MESH,
            ).start()
            return carry

        lax.fori_loop(max(1, 16 * half), 16 * half + 16, send, 0)
        if half == 0:
            self.home[e] = self.spread[0]

    def arrive(self):
        drain(self.home.at[pl.ds(0, PLANE - 1)], self.plane_in)

    def close(self):
        for copy in self.copies(0) + self.copies(1):
            copy.wait_send()
        drain(self.spread.at[pl.ds(0, PLANE - 1)], self.plane_out)


RETURN_SCRATCH = [
    pltpu.VMEM((2, 2, HALF, 768), bf16),
    pltpu.VMEM((12, HALF, 768), bf16),
    pltpu.VMEM(BLOCKS, bf16),
    pltpu.VMEM(BLOCKS, bf16),
    pltpu.SemaphoreType.DMA((12,)),
    pltpu.SemaphoreType.DMA((12,)),
    pltpu.SemaphoreType.DMA,
    pltpu.SemaphoreType.DMA,
]


def kernel_params(collective_id):
    return pltpu.CompilerParams(
        collective_id=collective_id, has_side_effects=True, vmem_limit_bytes=60 * 1024 * 1024
    )


VMEM = pl.BlockSpec(memory_space=pltpu.VMEM)


SEQ = 512
SIDE = 64
WIDTH = 768
HEAD_WIDTH = 192
LOCAL_HEADS = 3
score_scale = HEAD_DIM ** (-0.5)


class RingGather:
    def __init__(self, rows, sems):
        self.rows = rows
        self.out, self.arrived = sems

    def copies(self):
        e, z, right, left = place()

        def copy(index, owner, half, other):
            block = self.rows.at[pl.ds(pl.multiple_of(owner * 128 + half * SIDE, SIDE), SIDE)]
            return pltpu.make_async_remote_copy(
                block,
                block,
                self.out.at[index],
                self.arrived.at[index],
                device_id=(e, other),
                device_id_type=MESH,
            )

        def landing(index, owner, half):
            block = self.rows.at[pl.ds(pl.multiple_of(owner * 128 + half * SIDE, SIDE), SIDE)]
            return pltpu.make_async_copy(block, block, self.arrived.at[index])

        far = lax.rem(z + 2, RING)
        sends = [
            copy(0, z, 0, right),
            copy(1, z, 1, right),
            copy(2, z, 0, left),
            copy(3, z, 1, left),
            copy(4, left, 0, right),
            copy(5, right, 1, left),
        ]
        lands = [
            landing(0, left, 0),
            landing(1, left, 1),
            landing(2, right, 0),
            landing(3, right, 1),
            landing(4, far, 0),
            landing(5, far, 1),
        ]
        return sends, lands

    def start(self):
        sends, lands = self.copies()
        for index in (0, 3, 1, 2):
            sends[index].start()

    def relay(self):
        sends, lands = self.copies()
        lands[0].wait()
        sends[4].start()
        lands[3].wait()
        sends[5].start()

    def land(self, index):
        sends, lands = self.copies()
        lands[index].wait()

    def finish(self):
        self.relay()
        for index in (1, 2, 4, 5):
            self.land(index)

    def close(self):
        sends, lands = self.copies()
        for send in sends:
            send.wait_send()


GATHER_SCRATCH = [pltpu.SemaphoreType.DMA((6,)), pltpu.SemaphoreType.DMA((6,))]


class RingSum:
    def __init__(self, partial, relayed, landed, sems):
        self.partial, self.relayed, self.landed = partial, relayed, landed
        self.out, self.arrived = sems

    def part(self, slot, half):
        e, z, right, left = place()
        owner = (z, right, left, lax.rem(z + 2, RING))[slot]
        return self.partial.at[pl.ds(pl.multiple_of(owner * 128 + half * SIDE, SIDE), SIDE)]

    def copies(self):
        e, z, right, left = place()

        def copy(index, source, other):
            return pltpu.make_async_remote_copy(
                source,
                self.landed.at[index],
                self.out.at[index],
                self.arrived.at[index],
                device_id=(e, other),
                device_id_type=MESH,
            )

        part = self.part
        return [
            copy(0, part(3, 0), right),
            copy(1, part(3, 1), left),
            copy(2, part(1, 1), right),
            copy(3, part(2, 0), left),
            copy(4, self.relayed.at[0], right),
            copy(5, self.relayed.at[1], left),
        ]

    def send(self, index):
        self.copies()[index].start()

    def add_far(self):
        ring = self.copies()
        for index, slot, half in ((0, 1, 0), (1, 2, 1)):
            ring[index].wait_recv()
            self.relayed[index] = (
                self.part(slot, half)[...].astype(f32) + self.landed[index].astype(f32)
            ).astype(bf16)
            ring[4 + index].start()

    def total(self):
        ring = self.copies()
        halves = []
        for half, direct, summed in ((0, 3, 4), (1, 2, 5)):
            ring[direct].wait_recv()
            ring[summed].wait_recv()
            halves.append(
                self.part(0, half)[...].astype(f32)
                + self.landed[direct].astype(f32)
                + self.landed[summed].astype(f32)
            )
        return jnp.concatenate(halves, axis=0)

    def close(self):
        for copy in self.copies():
            copy.wait_send()


SUM_SCRATCH = [
    pltpu.VMEM((SEQ, WIDTH), bf16),
    pltpu.VMEM((2, SIDE, WIDTH), bf16),
    pltpu.VMEM((6, SIDE, WIDTH), bf16),
    pltpu.SemaphoreType.DMA((6,)),
    pltpu.SemaphoreType.DMA((6,)),
]


def head_mask(h):
    lane = lax.broadcasted_iota(jnp.int32, (1, HEAD_WIDTH), 1)
    return (lane >= h * HEAD_DIM) & (lane < (h + 1) * HEAD_DIM)


def sum_diagonals(square):
    rows = square
    for step in (32, 8, 1):
        count = rows.shape[0] // step
        rows = sum(
            pltpu.roll(rows[a * step : a * step + step], (SEQ - a * step) % SEQ, 1)
            if a
            else rows[:step]
            for a in range(count)
        )
    return rows


def bucket_hot_rows(bucket_rev):
    return (bucket_rev == lax.broadcasted_iota(jnp.int32, (32, SEQ), 0)).astype(f32)


def plane_sends(source_at, target_at, send_sem, recv_sem_at):
    e, z, right, left = place()

    def send(chip, carry):
        other = plane_target(e, chip * 2)
        pltpu.make_async_remote_copy(
            source_at(other // 2),
            target_at(e // 2),
            send_sem,
            recv_sem_at(e // 2),
            device_id=(other, z),
            device_id_type=MESH,
        ).start()
        return carry

    lax.fori_loop(1, 16, send, 0)


def rms_scale(values):
    return lax.rsqrt(jnp.mean(values * values, axis=1, keepdims=True) + epsilon)


def select_rows(ids):
    expert = lax.broadcasted_iota(jnp.int32, (128, 64), 1)
    hot = [(ids[:, c : c + 1] == expert).astype(f32) for c in range(TOPK)]
    row = lax.broadcasted_iota(jnp.int32, (128, 128), 0)
    col = lax.broadcasted_iota(jnp.int32, (128, 128), 1)
    before = dot((col < row).astype(bf16), (hot[0] + hot[1]).astype(bf16))
    pos = lax.broadcasted_iota(jnp.int32, (128, PAD), 1)
    picks = []
    for c in range(TOPK):
        slot = jnp.sum(before * hot[c], axis=1, keepdims=True).astype(jnp.int32)
        own = ids[:, c : c + 1]
        first = own // 2
        base = first * BLOCK + (own - first * 2) * 5 + slot
        picks.append(
            jnp.concatenate([(pos == base).astype(bf16), (pos == base + 10).astype(bf16)], axis=0)
        )
    return picks


def as_column(row):
    n = row.shape[1]
    same = lax.broadcasted_iota(jnp.int32, (n, n), 0) == lax.broadcasted_iota(jnp.int32, (n, n), 1)
    return jnp.sum(jnp.where(same, row, 0.0), axis=1, keepdims=True)


def as_row(rows):
    return jnp.concatenate([rows[i : i + 1] for i in range(rows.shape[0])], axis=1)


def layer_kernel(
    tokens_hbm, qkv_hbm, proj_hbm, gain_attn_hbm, gain_moe_hbm, bias_hbm,
    ids_hbm, gates_hbm, buckets_hbm, cotangent_hbm, weight_in, weight_out,
    out, grad_input, qkv_grad, proj_grad, gain_first, gain_second, table_out,
    grads_hbm,
    tokens, qkv_weight, proj_weight, gain_attn, gain_moe, bias,
    ids, gates, buckets, cotangent, input_sems,
    units, whole, qkv, attended, probs, picked, resid, mine, wall, whole32,
    x_send, x_landed, x_rows, g_send, g_landed, g_rows,
    held_in, held_out, hidden, grad_pre, grad_part, y_part, expert_grads,
    seq_grad, grad_qkv, blocks, near_blocks, plane_landed, small_own, small_landed, small_sum, small_plane,
    load_sems, save_sems, w_send, w_recv, s_send, s_recv, v_send, v_recv,
    p_send, p_recv, t_send, t_recv, q_send, q_recv, *rest,
):
    x_sems, g_sems, rest = rest[:4], rest[4:8], rest[8:]
    unit_sems, grad_sems, rest = rest[:2], rest[2:4], rest[4:]
    sum_a, sum_b, rest = rest[:5], rest[5:10], rest[10:]
    back_x, back_y = rest[:8], rest[8:]
    e, z, right, left = place()
    core, chip = lax.rem(e, 2), e // 2
    twin = chip * 2 + 1 - core
    opposite = lax.rem(z + 2, RING)
    inputs_in = [
        pltpu.make_async_copy(source, target, input_sems.at[index])
        for index, (source, target) in enumerate(
            (
                (tokens_hbm, tokens),
                (qkv_hbm, qkv_weight),
                (proj_hbm, proj_weight),
                (gain_attn_hbm, gain_attn),
                (gain_moe_hbm, gain_moe),
                (bias_hbm, bias),
                (ids_hbm, ids),
                (gates_hbm, gates),
                (buckets_hbm, buckets),
                (cotangent_hbm, cotangent),
            )
        )
    ]
    loads = [
        pltpu.make_async_copy(weight_in, held_in, load_sems.at[0]),
        pltpu.make_async_copy(weight_out, held_out, load_sems.at[1]),
    ]
    arrivals = greet(1, 1, 1)
    for load in inputs_in + loads:
        load.start()
    for load in inputs_in[:3]:
        load.wait()

    mine[...] = jnp.concatenate(
        [qkv_weight[i].astype(f32) for i in range(3)] + [proj_weight[...].astype(f32)], axis=1
    ).astype(bf16)
    inputs = tokens[...].astype(f32)
    own_rows = pl.ds(pl.multiple_of(z * 128, 128), 128)
    units[own_rows] = (inputs * rms_scale(inputs)).astype(bf16)
    pl.semaphore_wait(pltpu.get_barrier_semaphore(), arrivals)
    plane_sends(lambda other: mine, lambda own: wall.at[core, own], w_send, w_recv.at.__getitem__)
    unit_ring = RingGather(units, unit_sems)
    unit_ring.start()
    wall[core, chip] = mine[...]

    def pass_on(source):
        return pltpu.make_async_remote_copy(
            wall.at[core, source],
            wall.at[core, source],
            s_send,
            s_recv,
            device_id=(twin, z),
            device_id_type=MESH,
        )

    pass_on(chip).start()
    for load in inputs_in[3:]:
        load.wait()
    gain_a, gain_m = as_row(gain_attn[...]), as_row(gain_moe[...])
    id_columns = jnp.concatenate(
        [as_column(ids[c : c + 1].astype(f32)) for c in range(TOPK)], axis=1
    ).astype(jnp.int32)
    gate_columns = [as_column(gates[c : c + 1]) for c in range(TOPK)]
    picks = select_rows(id_columns)
    for c in range(TOPK):
        picked[c] = picks[c]
    grad_out = cotangent[...].astype(f32)
    g_send[...] = as_blocks(
        dot_rows(picks[0], fold((gate_columns[0] * grad_out).astype(bf16)))
        + dot_rows(picks[1], fold((gate_columns[1] * grad_out).astype(bf16)))
    )
    grads = Dispatch(g_send, g_landed, g_rows, g_sems)
    unit_ring.relay()
    far_row = lax.broadcasted_iota(jnp.int32, (SEQ, SEQ), 0)
    far_col = lax.broadcasted_iota(jnp.int32, (SEQ, SEQ), 1)
    mirror = (far_row + far_col == jnp.where(far_col == 0, 0, SEQ)).astype(bf16)
    hot = dot(bucket_hot_rows(as_row(buckets[...])).astype(bf16), mirror)
    rels = [
        jnp.sum(as_column(bias[h : h + 1]) * hot, axis=0, keepdims=True)
        for h in range(LOCAL_HEADS)
    ]
    pack = packer()

    def forward(step, carry):
        source = plane_source(e, step * 2) // 2
        pltpu.make_async_copy(wall.at[core, source], wall.at[core, source], w_recv.at[source]).wait()
        pass_on(source).start()
        return carry

    lax.fori_loop(1, 16, forward, 0)
    for index in (1, 2, 4, 5):
        unit_ring.land(index)
    drain(wall.at[0, pl.ds(0, 15)], w_send)
    grads.cross(0)
    grads.cross(1)
    unit_rows = units[...].astype(f32)
    normed = (unit_rows * gain_a).astype(bf16)
    drain(wall.at[1 - core], s_recv)
    for block in range(PLANE):
        whole32[24 * block : 24 * block + 24] = wall[block % 2, block // 2].astype(f32)
    whole[...] = whole32[...].astype(bf16)

    qkv[...] = dot(normed, whole[:, :640]).astype(bf16)[:, : 3 * HEAD_WIDTH]
    keys = qkv[:, HEAD_WIDTH : 2 * HEAD_WIDTH]
    values = qkv[:, 2 * HEAD_WIDTH :]
    proj = whole[:, 3 * HEAD_WIDTH :]
    attn_sum = RingSum(sum_a[0], sum_a[1], sum_a[2], sum_a[3:])
    owners = (z, right, left, opposite)
    query_row = lax.broadcasted_iota(jnp.int32, (128, SEQ), 0)
    key_col = lax.broadcasted_iota(jnp.int32, (128, SEQ), 1)

    def rows_of(slot):
        return pl.ds(pl.multiple_of(owners[slot] * 128, 128), 128)

    def attend(slot):
        rows = rows_of(slot)
        first = owners[slot] * 128
        queries = qkv[rows, :HEAD_WIDTH]
        mixed = jnp.zeros((128, HEAD_WIDTH), f32)
        for h in range(LOCAL_HEADS):
            mask = head_mask(h)
            turned = pltpu.roll(rels[h], first, 1)
            shifted = pltpu.roll(
                jnp.broadcast_to(turned, (128, SEQ)), 0, 1, stride=1, stride_axis=0
            )
            scores = dot_cols(jnp.where(mask, queries, jnp.zeros_like(queries)), keys) * score_scale
            scores = jnp.where(key_col <= query_row + first, scores + shifted, masked_value)
            raised = jnp.exp(scores - jnp.max(scores, axis=1, keepdims=True))
            weights_p = (raised / jnp.sum(raised, axis=1, keepdims=True)).astype(bf16)
            probs[h, rows] = weights_p
            mixed = jnp.where(mask, dot(weights_p, values), mixed)
        mixed = mixed.astype(bf16)
        attended[rows] = mixed
        sum_a[0][rows] = dot_cols(mixed, proj).astype(bf16)

    attend(3)
    attn_sum.send(0)
    attn_sum.send(1)
    attend(1)
    attn_sum.send(2)
    attend(2)
    attn_sum.send(3)
    attend(0)
    attn_sum.add_far()
    grads.turn(0, pack)
    grads.turn(1, pack)
    residual = inputs + attn_sum.total()
    resid[...] = residual
    scale_m = rms_scale(residual)
    normal_m = residual * scale_m
    x_send[...] = as_blocks(
        dot_rows(picks[0] + picks[1], fold((normal_m * gain_m).astype(bf16)))
    )

    out_way = Dispatch(x_send, x_landed, x_rows, x_sems)
    home_way = Return(grad_part, back_x[0], back_x[1], back_x[2], back_x[3], back_x[4:])
    out_way.cross(0)
    out_way.crossed(0)
    out_way.cross(1)
    out_way.turn(0, pack)
    out_way.turn(1, pack)
    for load in loads:
        load.wait()

    def run(first, count, experts=(0, 1)):
        for j in experts:
            span = pl.ds(first * 160, count * 160)
            pre_act = dot(x_rows[j, span], held_in[j])
            cdf = 0.5 * (1.0 + lax.erf(pre_act * inv_root_two))
            hidden[j, span] = (pre_act * cdf).astype(bf16)
            slope = cdf + pre_act * jnp.exp(-0.5 * pre_act * pre_act) * inv_root_tau
            grad_hidden = dot_cols(g_rows[j, span], held_out[j])
            grad_pre[j, span] = (grad_hidden * slope).astype(bf16)
            grad_part[j, span] = dot_cols(grad_pre[j, span], held_in[j]).astype(bf16)

    run(0, 1)
    grads.relay()
    out_way.relay()
    run(1, 2)
    home_way.near(0)
    home_way.near(1)
    grads.last()
    out_way.last()
    for j in range(2):
        run(3, 1, (j,))
        home_way.far(0, j)
        home_way.far(1, j)
    y_way = Return(y_part, back_y[0], back_y[1], back_y[2], back_y[3], back_y[4:])
    for j in range(2):
        y_part[j] = dot(hidden[j], held_out[j]).astype(bf16)
    home_way.add_far(0)
    home_way.add_far(1)
    for half in range(2):
        y_way.far(half, 0)
        y_way.far(half, 1)
        y_way.near(half)
    home_way.finish(0, pack)
    home_way.finish(1, pack)
    saves = []
    for j in range(2):
        expert_grads[j] = dot_rows(x_rows[j], grad_pre[j]).astype(bf16)
        expert_grads[2 + j] = dot_rows(hidden[j], g_rows[j]).astype(bf16)
        y_way.add_far(j)
    for index in range(4):
        saves.append(
            pltpu.make_async_copy(expert_grads.at[index], grads_hbm.at[index], save_sems.at[index])
        )
        saves[index].start()
    home_way.arrive()
    grad_normed = unfold(dot(picked[0] + picked[1], from_blocks(home_way.home[...])))
    gain_m_part = jnp.sum(grad_normed * normal_m, axis=0, keepdims=True)
    grad_unit_m = grad_normed * gain_m
    grad_resid = grad_out + scale_m * (
        grad_unit_m - normal_m * jnp.mean(grad_unit_m * normal_m, axis=1, keepdims=True)
    )

    seq_grad[own_rows] = grad_resid.astype(bf16)
    grad_ring = RingGather(seq_grad, grad_sems)
    grad_ring.start()
    zeros = jnp.zeros((SEQ, HEAD_WIDTH), f32)
    carried = [zeros, zeros, jnp.zeros((WIDTH, HEAD_WIDTH), f32)]
    diagonals = [jnp.zeros((1, SEQ), f32)] * LOCAL_HEADS

    def attend_back(slot):
        rows = rows_of(slot)
        queries = qkv[rows, :HEAD_WIDTH]
        grad_rows = seq_grad[rows]
        grad_att = dot(grad_rows, proj).astype(bf16)
        carried[2] = carried[2] + dot_rows(grad_rows, attended[rows])
        grad_q = jnp.zeros((128, HEAD_WIDTH), f32)
        for h in range(LOCAL_HEADS):
            mask = head_mask(h)
            weights_p = probs[h, rows]
            soft = weights_p.astype(f32)
            own_att = jnp.where(mask, grad_att, jnp.zeros_like(grad_att))
            own_queries = jnp.where(mask, queries, jnp.zeros_like(queries))
            grad_w = dot_cols(own_att, values)
            row_dot = jnp.sum(soft * grad_w, axis=1, keepdims=True)
            grad_scores = (soft * (grad_w - row_dot)).astype(bf16)
            turn = lax.rem(SEQ - owners[slot] * 128, SEQ)
            diagonals[h] = diagonals[h] + pltpu.roll(
                sum_diagonals(grad_scores.astype(f32)), turn, 1
            )
            grad_q = jnp.where(mask, dot(grad_scores, keys), grad_q)
            carried[0] = carried[0] + dot_rows(grad_scores, own_queries)
            carried[1] = carried[1] + dot_rows(weights_p, own_att)
        grad_qkv[rows, :HEAD_WIDTH] = (grad_q * score_scale).astype(bf16)

    attend_back(0)
    grad_ring.relay()
    grad_ring.land(2)
    attend_back(1)
    y_way.finish(0, pack)
    grad_ring.land(1)
    attend_back(2)
    y_way.finish(1, pack)
    grad_ring.land(4)
    grad_ring.land(5)
    attend_back(3)
    def pair(side, full):
        for block in range(PLANE):
            blocks[side, block % 2, block // 2] = full[24 * block : 24 * block + 24].astype(bf16)
        exchange = pltpu.make_async_remote_copy(
            blocks.at[side, 1 - core],
            near_blocks.at[side],
            v_send.at[side],
            v_recv.at[side],
            device_id=(twin, z),
            device_id_type=MESH,
        )
        exchange.start()
        return exchange

    def spread_pair(side, exchange):
        exchange.wait_recv()
        near_blocks[side] = (
            blocks[side, core].astype(f32) + near_blocks[side].astype(f32)
        ).astype(bf16)
        plane_sends(
            lambda other: near_blocks.at[side, other],
            lambda own: plane_landed.at[side, own],
            p_send.at[side],
            lambda own: p_recv.at[side],
        )
        plane_landed[side, chip] = near_blocks[side, chip]

    query_part = dot_rows(normed, grad_qkv[:, :HEAD_WIDTH])
    pairs = [pair(0, jnp.concatenate([query_part, carried[2]], axis=1))]
    grad_qkv[:, HEAD_WIDTH:] = jnp.concatenate(
        [carried[0] * score_scale, carried[1]], axis=1
    ).astype(bf16)
    pairs.append(pair(1, dot_rows(normed, grad_qkv[:, HEAD_WIDTH:])))
    grad_normed_a = dot_cols(grad_qkv[...], whole[:, : 3 * HEAD_WIDTH])
    gain_part = jnp.sum(grad_normed_a * unit_rows, axis=0, keepdims=True)
    diagonal = jnp.concatenate(diagonals + [jnp.zeros((5, SEQ), f32)], axis=0)
    table_rows = lax.dot_general(
        diagonal, hot, (((1,), (1,)), ((), ())), precision=highest, preferred_element_type=f32
    )
    pieces = [
        part[:, 128 * i : 128 * i + 128] for part in (gain_part, gain_m_part) for i in range(6)
    ]
    small_own[...] = jnp.concatenate(
        pieces + [jnp.zeros((4, 128), f32)], axis=0
    )
    small_own[12 : 12 + LOCAL_HEADS, :32] = table_rows[:LOCAL_HEADS]
    shares = [
        pltpu.make_async_remote_copy(
            small_own,
            small_landed.at[index],
            t_send.at[index],
            t_recv.at[index],
            device_id=(e, other),
            device_id_type=MESH,
        )
        for index, other in enumerate((right, left, opposite))
    ]
    for share in shares:
        share.start()
    sum_b[0][...] = grad_normed_a.astype(bf16)
    input_sum = RingSum(sum_b[0], sum_b[1], sum_b[2], sum_b[3:])
    for index in range(4):
        input_sum.send(index)
    spread_pair(0, pairs[0])
    spread_pair(1, pairs[1])
    input_sum.add_far()
    for share in shares:
        share.wait_recv()
    own_small = small_own[...]
    line = lax.broadcasted_iota(jnp.int32, (16, 128), 0)
    small_sum[...] = jnp.where(
        line < 12, own_small + small_landed[0] + small_landed[1] + small_landed[2], own_small
    )

    def spread_small(d, carry):
        pltpu.make_async_remote_copy(
            small_sum,
            small_plane.at[d],
            q_send,
            q_recv,
            device_id=(plane_target(e, d), z),
            device_id_type=MESH,
        ).start()
        return carry

    lax.fori_loop(1, PLANE, spread_small, 0)
    small_plane[0] = small_sum[...]
    y_way.arrive()
    home = from_blocks(y_way.home[...])
    out[...] = (
        resid[...]
        + gate_columns[0] * unfold(dot(picked[0], home))
        + gate_columns[1] * unfold(dot(picked[1], home))
    ).astype(bf16)
    scale_first = rms_scale(inputs)
    normal_first = inputs * scale_first
    grad_unit = input_sum.total() * gain_a
    grad_input[...] = grad_resid + scale_first * (
        grad_unit - normal_first * jnp.mean(grad_unit * normal_first, axis=1, keepdims=True)
    )
    totals = []
    for side in range(2):
        drain(plane_landed.at[side, pl.ds(0, 15)], p_recv.at[side])
        total = plane_landed[side, 0].astype(f32)
        for block in range(1, 16):
            total = total + plane_landed[side, block].astype(f32)
        totals.append(total)
    qkv_grad[0] = totals[0][:, :HEAD_WIDTH]
    proj_grad[...] = totals[0][:, HEAD_WIDTH:]
    qkv_grad[1] = totals[1][:, :HEAD_WIDTH]
    qkv_grad[2] = totals[1][:, HEAD_WIDTH:]
    drain(small_plane.at[pl.ds(1, PLANE - 1)], q_recv)
    summed = jnp.sum(small_plane[...], axis=0)
    column = lax.broadcasted_iota(jnp.int32, (16, 128), 1)
    table_own = jnp.sum(jnp.where(column == e, summed, 0.0), axis=1, keepdims=True)
    table_out[...] = jnp.concatenate(
        [table_own[12 + h : 13 + h] for h in range(LOCAL_HEADS)], axis=1
    )
    wide = jnp.concatenate([as_row(summed[0:6]), as_row(summed[6:12])], axis=0)
    wide = jnp.concatenate([wide, jnp.zeros((6, WIDTH), f32)], axis=0)
    feature = lax.broadcasted_iota(jnp.int32, (WIDTH, 128), 0)
    lane = lax.broadcasted_iota(jnp.int32, (WIDTH, 128), 1)
    taken = (feature == (e * RING + z) * 6 + lane).astype(f32)
    gains = jnp.dot(wide, taken, precision=highest, preferred_element_type=f32)
    gain_first[...] = gains[0:1, :6]
    gain_second[...] = gains[1:2, :6]

    drain(small_plane.at[pl.ds(1, PLANE - 1)], q_send)
    for share in shares:
        share.wait_send()
    for save in saves:
        save.wait()
    for way in (grads, out_way):
        way.close()
        way.crossed(1)
    grads.crossed(0)
    home_way.close()
    y_way.close()
    unit_ring.close()
    grad_ring.close()
    attn_sum.close()
    input_sum.close()
    for exchange in pairs:
        exchange.wait_send()
    drain(wall.at[0], s_send)
    for side in range(2):
        drain(plane_landed.at[side, pl.ds(0, 15)], p_send.at[side])


def run_layer(*operands):
    def shape(dims, kind=f32):
        return jax.ShapeDtypeStruct(dims, kind)

    anywhere = pl.BlockSpec(memory_space=pl.ANY)
    rows = (2, EXPERT_ROWS, WIDTH)
    dma = pltpu.SemaphoreType.DMA
    return pl.pallas_call(
        layer_kernel,
        out_shape=[
            shape((128, WIDTH), bf16),
            shape((128, WIDTH)),
            shape((3, 24, HEAD_WIDTH)),
            shape((24, HEAD_WIDTH)),
            shape((1, 6)),
            shape((1, 6)),
            shape((1, LOCAL_HEADS)),
        ]
        + [shape((4, WIDTH, WIDTH), bf16)],
        in_specs=[anywhere] * 12,
        out_specs=[VMEM] * 7 + [anywhere],
        scratch_shapes=[pltpu.VMEM(a.shape, a.dtype) for a in operands[:10]]
        + [
            dma((10,)),
            pltpu.VMEM((SEQ, WIDTH), bf16),
            pltpu.VMEM((WIDTH, WIDTH), bf16),
            pltpu.VMEM((SEQ, 3 * HEAD_WIDTH), bf16),
            pltpu.VMEM((SEQ, HEAD_WIDTH), bf16),
            pltpu.VMEM((LOCAL_HEADS, SEQ, SEQ), bf16),
            pltpu.VMEM((TOPK, 256, PAD), bf16),
            pltpu.VMEM((128, WIDTH), f32),
            pltpu.VMEM((24, WIDTH), bf16),
            pltpu.VMEM((2, 16, 24, WIDTH), bf16),
            pltpu.VMEM((WIDTH, WIDTH), f32),
        ]
        + [pltpu.VMEM(BLOCKS, bf16), pltpu.VMEM(BLOCKS, bf16), pltpu.VMEM(rows, bf16)] * 2
        + [pltpu.VMEM((2, WIDTH, WIDTH), bf16)] * 2
        + [pltpu.VMEM(rows, bf16)] * 4
        + [
            pltpu.VMEM((4, WIDTH, WIDTH), bf16),
            pltpu.VMEM((SEQ, WIDTH), bf16),
            pltpu.VMEM((SEQ, 3 * HEAD_WIDTH), bf16),
            pltpu.VMEM((2, 2, 16, 24, NARROW), bf16),
            pltpu.VMEM((2, 16, 24, NARROW), bf16),
            pltpu.VMEM((2, 16, 24, NARROW), bf16),
            pltpu.VMEM((16, 128), f32),
            pltpu.VMEM((3, 16, 128), f32),
            pltpu.VMEM((16, 128), f32),
            pltpu.VMEM((PLANE, 16, 128), f32),
            dma((2,)),
            dma((4,)),
            dma,
            dma((16,)),
            dma,
            dma,
            dma((2,)),
            dma((2,)),
            dma((2,)),
            dma((2,)),
            dma((3,)),
            dma((3,)),
            dma,
            dma,
        ]
        + DISPATCH_SCRATCH * 2
        + GATHER_SCRATCH * 2
        + SUM_SCRATCH * 2
        + RETURN_SCRATCH * 2,
        compiler_params=kernel_params(1),
        name="layer",
    )(*operands)


def widen_kernel(narrow, *refs):
    count = (len(refs) - 8) // 3
    passed, results = refs[:count], refs[count : 2 * count]
    wide_in, wide_out, held, wide, loads, saves, ins, outs = refs[2 * count : 2 * count + 8]
    bounced = refs[2 * count + 8 :]
    reads = [pltpu.make_async_copy(narrow.at[i], held.at[i], loads.at[i]) for i in range(4)]
    for read in reads:
        read.start()
    arrive = [
        pltpu.make_async_copy(passed[i], bounced[i], ins.at[i]) for i in range(count)
    ]
    leave = [
        pltpu.make_async_copy(bounced[i], results[i], outs.at[i]) for i in range(count)
    ]
    for copy in arrive:
        copy.start()
    writes = []
    for i in range(4):
        reads[i].wait()
        wide[i] = held[i].astype(f32)
        target = (wide_in, wide_out)[i // 2].at[i % 2]
        writes.append(pltpu.make_async_copy(wide.at[i], target, saves.at[i]))
        writes[i].start()
        if i == 0:
            for one, other in zip(arrive, leave):
                one.wait()
                other.start()
    for write in writes + leave:
        write.wait()


def widen(narrow, *small):
    anywhere = pl.BlockSpec(memory_space=pl.ANY)
    grads = jax.ShapeDtypeStruct((2, WIDTH, WIDTH), f32)
    return pl.pallas_call(
        widen_kernel,
        out_shape=[jax.ShapeDtypeStruct(a.shape, a.dtype) for a in small] + [grads, grads],
        in_specs=[anywhere] * (1 + len(small)),
        out_specs=[anywhere] * (len(small) + 2),
        scratch_shapes=[
            pltpu.VMEM((4, WIDTH, WIDTH), bf16),
            pltpu.VMEM((4, WIDTH, WIDTH), f32),
            pltpu.SemaphoreType.DMA((4,)),
            pltpu.SemaphoreType.DMA((4,)),
            pltpu.SemaphoreType.DMA((len(small),)),
            pltpu.SemaphoreType.DMA((len(small),)),
        ]
        + [pltpu.VMEM(a.shape, a.dtype) for a in small],
        compiler_params=pltpu.CompilerParams(vmem_limit_bytes=60 * 1024 * 1024),
        name="widen",
    )(narrow, *small)


def body(
    tokens,
    gain_attn,
    gain_moe,
    qkv_weight,
    proj_weight,
    bias_table,
    expert_in,
    expert_out,
    expert_ids,
    gate_values,
    bucket_table,
    cotangent,
):
    results = run_layer(
        tokens,
        qkv_weight.transpose(1, 0, 2),
        proj_weight.T,
        gain_attn.reshape(6, 128),
        gain_moe.reshape(6, 128),
        bias_table.T,
        expert_ids.T,
        gate_values.T,
        bucket_table.reshape(4, 128),
        cotangent,
        expert_in,
        expert_out,
    )
    out, grad_input, qkv_grad, proj_grad, gain_first, gain_second, table, grad_in, grad_out = widen(
        results[7], *results[:7]
    )
    return (
        out,
        grad_input,
        gain_first[0],
        gain_second[0],
        qkv_grad.transpose(1, 0, 2),
        proj_grad.T,
        table,
        grad_in,
        grad_out,
    )


def solution(mesh):
    placed = (
        P(("expert", "mp"), None),
        P(),
        P(),
        P("expert", None, "mp"),
        P("mp", "expert"),
        P(None, "mp"),
        P("expert", None, "mp"),
        P("expert", "mp", None),
        P(("expert", "mp"), None),
        P(("expert", "mp"), None),
        P(),
        P(("expert", "mp"), None),
    )
    return jax.shard_map(
        body,
        mesh=mesh,
        in_specs=placed,
        out_specs=(
            P(("expert", "mp"), None),
            P(("expert", "mp"), None),
            P(("expert", "mp")),
            P(("expert", "mp")),
            P("expert", None, "mp"),
            P("mp", "expert"),
            P("expert", "mp"),
            P("expert", None, "mp"),
            P("expert", "mp", None),
        ),
        check_vma=False,
    )
```
